32 devices in a mesh: sec: 4 (over z), gx: 2 (over y), gy: 4 (over x, core).
Axes of the slice: x: 2, y: 2, z: 4, core: 2. Of those that a mesh axis runs over, the one named last changes fastest.
Arguments:
- fields: float32 [4, 3, 256, 8192], P('sec', None, 'gx', 'gy'), may hold values from -6 to 6
- x_ops: float32 [4, 3, 256, 256], P(None, None, 'gx'), may hold values from -4 to 4, as said below
- y_ops: float32 [4, 3, 256, 256], P(None, None, 'gy'), may hold values from -4 to 4, as said below
- x_line_class: int32 [256], P('gy'), may hold values from 0 to 3
- y_line_class: int32 [256], P('gx'), may hold values from 0 to 3
- box_offset: int32 [3, 2], replicated, may hold values from 0 to 127, as said below
- coupling: float32 [3, 3, 3], replicated, may hold values from -3 to 3
Outputs:
- fields_next: float32 [4, 3, 256, 8192], P('sec', None, 'gx', 'gy')
The draws below stay inside these ranges and needn't reach their ends.
Inputs may be any that keep to these rules, and one draw needn't show every extreme that they name: `box_offset`: column 0 is below 128 and column 1 below 64; each column reaches its largest value for some box. `x_ops`: A dense matrix for each class and characteristic. `y_ops`: A dense matrix for each class and characteristic.
All inputs are finite; a program needn't handle non-finite values.
Results may differ from the reference program's by a relative error of at most 0.00013.
Values sent between devices are 32-bit elements; how exact they have to be, the bound alone decides.
No kernel may reach another device: no remote copies, remote signals or barrier semaphores. Data moves between devices by JAX's collectives and lax.ppermute only.
A program may use at most 192 MiB of HBM per device.

```python
import jax
import jax.numpy as jnp
from jax import lax

NX = 256
NY = 256
CZ = 32
NCLASS = 4
STEPS = 2
NBOX = 3
CX = 128
CY = 64
N_SEC = 4


def line_operators(key, length):
    subkeys = jax.random.split(key, 3)
    positions = jnp.arange(length)
    offset = positions[:, None] - positions[None, :]
    implicit_side = jnp.where(offset == 0, 1.0, jnp.where(jnp.abs(offset) == 1, 1.0 / 3.0, 0.0))
    explicit_side = 7.0 / 9.0 * ((offset == -1).astype(jnp.float32) - (offset == 1).astype(jnp.float32)) + 1.0 / 36.0 * ((offset == -2).astype(jnp.float32) - (offset == 2).astype(jnp.float32))
    derivative = jnp.linalg.solve(implicit_side, explicit_side)
    courant = jnp.exp(jax.random.uniform(subkeys[0], (NCLASS, 3, 1, 1), minval=jnp.log(96.0), maxval=jnp.log(256.0)))
    damping = jax.random.uniform(subkeys[1], (NCLASS, 3, length), minval=0.0, maxval=0.3)
    identity = jnp.eye(length, dtype=jnp.float32)
    system = identity * (1.0 + damping)[..., None] + courant * derivative
    explicit = jnp.broadcast_to(identity - courant * derivative, system.shape)
    compact = jnp.linalg.solve(system, explicit)
    scatter_part = jax.random.truncated_normal(subkeys[2], -3.0, 3.0, (NCLASS, 3, length, length), dtype=jnp.float32)
    coupled = compact + 0.15 / jnp.sqrt(jnp.float32(length)) * scatter_part
    return coupled.astype(jnp.float32)


def draw_x_ops(key, part):
    return line_operators(jax.random.fold_in(key, 11), NX)


def draw_y_ops(key, part):
    return line_operators(jax.random.fold_in(key, 23), NY)


def draw_box_offset(key, part):
    subkeys = jax.random.split(jax.random.fold_in(key, 37), 4)
    column_x = jax.random.randint(subkeys[0], (NBOX,), 0, CX)
    column_y = jax.random.randint(subkeys[1], (NBOX,), 0, CY)
    pick_x = jax.random.randint(subkeys[2], (), 0, NBOX)
    pick_y = jax.random.randint(subkeys[3], (), 0, NBOX)
    members = jnp.arange(NBOX)
    column_x = jnp.where(members == pick_x, CX - 1, column_x)
    column_y = jnp.where(members == pick_y, CY - 1, column_y)
    return jnp.stack([column_x, column_y], axis=1).astype(jnp.int32)


def touch_ends(drawn, rng, low, largest):
    longest = drawn.shape.index(max(drawn.shape))
    spots = []
    for shift in (0, 1):
        where = [jax.random.randint(jax.random.fold_in(rng, axis), (), 0, length) for axis, length in enumerate(drawn.shape)]
        where[longest] = (where[longest] + shift) % drawn.shape[longest]
        spots.append(tuple(where))
    return drawn.at[spots[0]].set(low).at[spots[1]].set(largest)


def block_levels(rng, shape, pieces, low, top_value):
    factor_of, own = 1.0, jax.random.fold_in(rng, 6)
    for dim, shards_of in pieces:
        heights = jnp.exp(jax.random.uniform(jax.random.fold_in(own, dim), (shards_of,), jnp.float32, low / len(pieces), top_value / len(pieces)))
        factor_of = factor_of * jnp.repeat(heights, shape[dim] // shards_of).reshape([-1 if axis == dim else 1 for axis in range(len(shape))])
    return factor_of


def gaussian(rng, extent, deviation, reach, cuts=(), kind=jnp.bfloat16):
    values = jax.random.normal(rng, extent, jnp.float32) * deviation
    if len(cuts) > 0:
        values = block_levels(rng, extent, cuts, -0.22, 0.18) * values
    return jnp.clip(values, min=-reach, max=reach).astype(kind)


def setup_inputs(seed: int = 0) -> dict:
    splits = jax.random.split(jax.random.key(seed), 8)
    return {
        "fields": gaussian(splits[0], (N_SEC, 3, NX, NY * CZ), 1.0, 6.0, ((0, 4), (2, 2), (3, 4)), jnp.float32),
        "x_ops": draw_x_ops(jax.random.fold_in(splits[7], 71), 0),
        "y_ops": draw_y_ops(jax.random.fold_in(splits[7], 71), 0),
        "x_line_class": touch_ends(jax.random.randint(splits[3], (NY,), 0, NCLASS), jax.random.fold_in(splits[3], 1), 0, NCLASS - 1).astype(jnp.int32),
        "y_line_class": touch_ends(jax.random.randint(splits[4], (NX,), 0, NCLASS), jax.random.fold_in(splits[4], 1), 0, NCLASS - 1).astype(jnp.int32),
        "box_offset": draw_box_offset(jax.random.fold_in(splits[7], 71), 0),
        "coupling": gaussian(splits[6], (NBOX, 3, 3), 0.6, 3.0, (), jnp.float32),
    }


time_step = 0.2
viscosity = 0.25
highest = lax.Precision.HIGHEST

def flow_core(padded):
    centre = padded[:, 1:-1, 1:-1, :]
    ahead_x = padded[:, 2:, 1:-1, :]
    behind_x = padded[:, :-2, 1:-1, :]
    ahead_y = padded[:, 1:-1, 2:, :]
    behind_y = padded[:, 1:-1, :-2, :]
    ahead_z = jnp.roll(centre, -1, axis=3)
    behind_z = jnp.roll(centre, 1, axis=3)
    slope_x = 0.5 * (ahead_x - behind_x)
    slope_y = 0.5 * (ahead_y - behind_y)
    slope_z = 0.5 * (ahead_z - behind_z)
    laplace = ahead_x + behind_x + ahead_y + behind_y + ahead_z + behind_z - 6.0 * centre
    omega_x = slope_y[2] - slope_z[1]
    omega_y = slope_z[0] - slope_x[2]
    omega_z = slope_x[1] - slope_y[0]
    lamb_vector = jnp.stack([omega_y * centre[2] - omega_z * centre[1], omega_z * centre[0] - omega_x * centre[2], omega_x * centre[1] - omega_y * centre[0]])
    updated = centre + time_step * (viscosity * laplace - lamb_vector)
    return (updated, lamb_vector)

def place_source(padded_lamb, offset_x, offset_y, matrix, span_x, span_y, extent_x, extent_y):
    anchor = jnp.zeros((), jnp.int32)
    corner_x = (span_x - offset_x - 1).astype(jnp.int32)
    corner_y = (span_y - offset_y - 1).astype(jnp.int32)
    window = lax.dynamic_slice(padded_lamb, (anchor, corner_x, corner_y, anchor), (3, extent_x + 1, extent_y + 1, padded_lamb.shape[3]))
    averaged = 0.25 * (window[:, :-1, :-1] + window[:, 1:, :-1] + window[:, :-1, 1:] + window[:, 1:, 1:])
    return jnp.einsum('kj,jxyz->kxyz', matrix, averaged, precision=highest)

def sweep_x(amplitudes, x_ops, x_line_class):
    result = jnp.zeros_like(amplitudes)
    for category in range(NCLASS):
        partial_value = jnp.einsum('kij,kjyz->kiyz', x_ops[category], amplitudes, precision=highest)
        chosen = (x_line_class == category).astype(jnp.float32)
        result = result + partial_value * chosen[None, None, :, None]
    return result

def sweep_y(amplitudes, y_ops, y_line_class):
    result = jnp.zeros_like(amplitudes)
    for category in range(NCLASS):
        partial_value = jnp.einsum('kij,kxjz->kxiz', y_ops[category], amplitudes, precision=highest)
        chosen = (y_line_class == category).astype(jnp.float32)
        result = result + partial_value * chosen[None, :, None, None]
    return result

def reference(fields, x_ops, y_ops, x_line_class, y_line_class, box_offset, coupling):
    arrays = fields.reshape(N_SEC, 3, NX, NY, CZ)
    velocities = [arrays[member] for member in range(NBOX)]
    amplitudes = arrays[NBOX]
    for repeat in range(STEPS):
        source_sum = jnp.zeros_like(amplitudes)
        for member in range(NBOX):
            padded = jnp.pad(velocities[member], ((0, 0), (1, 1), (1, 1), (0, 0)))
            updated, lamb_vector = flow_core(padded)
            stretched = jnp.pad(lamb_vector, ((0, 0), (CX, 0), (CY, 0), (0, 0)))
            source_sum = source_sum + place_source(stretched, box_offset[member, 0], box_offset[member, 1], coupling[member], CX, CY, NX, NY)
            velocities[member] = updated
        amplitudes = amplitudes + time_step * source_sum
        amplitudes = sweep_y(sweep_x(amplitudes, x_ops, x_line_class), y_ops, y_line_class)
    return jnp.stack(velocities + [amplitudes]).reshape(N_SEC, 3, NX, NY * CZ)
```

```python
import jax
import jax.numpy as jnp
from jax import lax
from jax.experimental import pallas as pl
from jax.experimental.pallas import tpu as pltpu
from jax.sharding import PartitionSpec as P

CZ = 32
NCLASS = 4
STEPS = 2
TILE_X = 128
TILE_Y = 64
CHUNKS = 2

time_step = 0.2
viscosity = 0.25
vmem_limit = 56 * 1024 * 1024
f32 = jnp.float32
bf16 = jnp.bfloat16


def params():
    return pltpu.CompilerParams(vmem_limit_bytes=vmem_limit)


def iota(shape, dim):
    return lax.broadcasted_iota(jnp.int32, shape, dim)


def planes_kernel(field_ref, planes_ref, west_ref, east_ref, south_ref, north_ref, turned):
    comp = pl.program_id(0)
    turned[...] = field_ref[0].T
    lane = iota((TILE_Y, TILE_X), 1)

    @pl.when(comp == 0)
    def _():
        west_ref[...] = jnp.zeros_like(west_ref)
        east_ref[...] = jnp.zeros_like(east_ref)

    west = west_ref[...]
    east = east_ref[...]
    for z in range(CZ):
        plane = turned[pl.ds(z, TILE_Y, stride=CZ), :]
        planes_ref[z, 0] = plane
        here = lane == z * 3 + comp
        west = jnp.where(here, plane[:, 0:1], west)
        east = jnp.where(here, plane[:, TILE_X - 1 :], east)
        south_ref[0, pl.ds(z, 1), :] = plane[0:1, :]
        north_ref[0, pl.ds(z, 1), :] = plane[TILE_Y - 1 :, :]
    west_ref[...] = west
    east_ref[...] = east


def to_planes(field):
    whole = lambda c: (0, 0)
    return pl.pallas_call(
        planes_kernel,
        grid=(3,),
        in_specs=[pl.BlockSpec((1, TILE_X, TILE_Y * CZ), lambda c: (c, 0, 0))],
        out_specs=[
            pl.BlockSpec((CZ, 1, TILE_Y, TILE_X), lambda c: (0, c, 0, 0)),
            pl.BlockSpec((TILE_Y, TILE_X), whole),
            pl.BlockSpec((TILE_Y, TILE_X), whole),
            pl.BlockSpec((1, CZ, TILE_X), lambda c: (c, 0, 0)),
            pl.BlockSpec((1, CZ, TILE_X), lambda c: (c, 0, 0)),
        ],
        out_shape=[
            jax.ShapeDtypeStruct((CZ, 3, TILE_Y, TILE_X), f32),
            jax.ShapeDtypeStruct((TILE_Y, TILE_X), f32),
            jax.ShapeDtypeStruct((TILE_Y, TILE_X), f32),
            jax.ShapeDtypeStruct((3, CZ, TILE_X), f32),
            jax.ShapeDtypeStruct((3, CZ, TILE_X), f32),
        ],
        scratch_shapes=[pltpu.VMEM((TILE_Y * CZ, TILE_X), f32)],
        compiler_params=params(),
        name="to_planes",
    )(field)


def flow_kernel(per, last, flag_ref, u_ref, xlo_ref, xhi_ref, ylo_ref, yhi_ref, *outs):
    lamb_refs = outs[:CHUNKS]
    next_ref = outs[CHUNKS]
    group = pl.program_id(0)
    acoustic = flag_ref[0] > 0
    lane = iota((TILE_Y, TILE_X), 1)
    row = iota((TILE_Y, TILE_X), 0)
    turn = lax.rem(TILE_X - group * (per * 3), TILE_X)
    xlo = pltpu.roll(xlo_ref[...], turn, 1)
    xhi = pltpu.roll(xhi_ref[...], turn, 1)
    if not last:
        west_ref, east_ref, south_ref, north_ref = outs[CHUNKS + 1 :]

        @pl.when(group == 0)
        def _():
            west_ref[...] = jnp.zeros_like(west_ref)
            east_ref[...] = jnp.zeros_like(east_ref)

        west = west_ref[...]
        east = east_ref[...]
    for i in range(per):
        z = group * per + i
        above = lax.rem(z + 1, CZ)
        below = lax.rem(z + CZ - 1, CZ)
        centre, lap, dx, dy, dz = [], [], [], [], []
        for c in range(3):
            mid = u_ref[z, c]
            up = u_ref[above, c]
            down = u_ref[below, c]
            spot = i * 3 + c
            xm = jnp.where(lane == 0, xlo[:, spot : spot + 1], pltpu.roll(mid, 1, 1))
            xp = jnp.where(
                lane == TILE_X - 1, xhi[:, spot : spot + 1], pltpu.roll(mid, TILE_X - 1, 1)
            )
            ym = jnp.where(row == 0, ylo_ref[c, pl.ds(z, 1), :], pltpu.roll(mid, 1, 0))
            yp = jnp.where(
                row == TILE_Y - 1, yhi_ref[c, pl.ds(z, 1), :], pltpu.roll(mid, TILE_Y - 1, 0)
            )
            centre.append(mid)
            lap.append(xp + xm + yp + ym + up + down - 6.0 * mid)
            dx.append(0.5 * (xp - xm))
            dy.append(0.5 * (yp - ym))
            dz.append(0.5 * (up - down))
        ox = dy[2] - dz[1]
        oy = dz[0] - dx[2]
        oz = dx[1] - dy[0]
        lamb = (
            oy * centre[2] - oz * centre[1],
            oz * centre[0] - ox * centre[2],
            ox * centre[1] - oy * centre[0],
        )
        for c in range(3):
            moved = centre[c] + time_step * (viscosity * lap[c] - lamb[c])
            next_ref[i, c] = moved
            sent = lamb[c] if last else jnp.where(acoustic, centre[c], lamb[c])
            lamb_refs[i % CHUNKS][0, i // CHUNKS, c] = sent
            if not last:
                here = lane == z * 3 + c
                west = jnp.where(here, moved[:, 0:1], west)
                east = jnp.where(here, moved[:, TILE_X - 1 :], east)
                south_ref[c, pl.ds(z, 1), :] = moved[0:1, :]
                north_ref[c, pl.ds(z, 1), :] = moved[TILE_Y - 1 :, :]
    if not last:
        west_ref[...] = west
        east_ref[...] = east


def flow(flag, planes, halo, groups, last):
    per = CZ // groups
    halves = per // CHUNKS
    edge = pl.BlockSpec((TILE_Y, TILE_X), lambda g: (0, 0))
    side = pl.BlockSpec((3, CZ, TILE_X), lambda g: (0, 0, 0))
    out_specs = [
        pl.BlockSpec((1, halves, 3, TILE_Y, TILE_X), lambda g: (g, 0, 0, 0, 0))
    ] * CHUNKS + [pl.BlockSpec((per, 3, TILE_Y, TILE_X), lambda g: (g, 0, 0, 0))]
    out_shape = [
        jax.ShapeDtypeStruct((groups, halves, 3, TILE_Y, TILE_X), f32)
    ] * CHUNKS + [jax.ShapeDtypeStruct((CZ, 3, TILE_Y, TILE_X), f32)]
    if not last:
        out_specs += [edge, edge, side, side]
        out_shape += [jax.ShapeDtypeStruct((TILE_Y, TILE_X), f32)] * 2
        out_shape += [jax.ShapeDtypeStruct((3, CZ, TILE_X), f32)] * 2

    def body(*refs):
        flow_kernel(per, last, *refs)

    return pl.pallas_call(
        body,
        grid=(groups,),
        in_specs=[
            pl.BlockSpec(memory_space=pltpu.SMEM),
            pl.BlockSpec((CZ, 3, TILE_Y, TILE_X), lambda g: (0, 0, 0, 0)),
            edge,
            edge,
            side,
            side,
        ],
        out_specs=out_specs,
        out_shape=out_shape,
        compiler_params=params(),
        name="flow",
    )(flag, planes, *halo)


def exchange(west, east, south, north):
    def send(value, axis, step):
        count = lax.axis_size(axis)
        return lax.ppermute(
            value, axis, [(i, i + step) for i in range(count) if 0 <= i + step < count]
        )

    return (
        send(east, "gx", 1),
        send(west, "gx", -1),
        send(north, "gy", 1),
        send(south, "gy", -1),
    )


def place_kernel(gx, gy, first, ints_ref, matrix_ref, got_ref, far_ref, near_ref, rows):
    low = ints_ref[1]
    ox = ints_ref[2]
    oy = ints_ref[3]
    full_y = gy * TILE_Y
    lane = iota((full_y, TILE_X), 1)
    row = iota((full_y, TILE_X), 0)

    def tile(h, j, a):
        return jnp.concatenate([got_ref[a * gy + b, h, j] for b in range(gy)], axis=0)

    def work(h, out_ref):
        for a in range(gx):
            rows[0:TILE_Y, a * TILE_X : (a + 1) * TILE_X] = jnp.zeros((TILE_Y, TILE_X), f32)
        vectors = [[tile(h, j, a) for a in range(gx)] for j in range(3)]
        for k in range(3):
            mixed = [
                matrix_ref[k, 0] * vectors[0][a]
                + matrix_ref[k, 1] * vectors[1][a]
                + matrix_ref[k, 2] * vectors[2][a]
                for a in range(gx)
            ]
            before = jnp.zeros((full_y, TILE_X), f32)
            moved = []
            for a in range(gx):
                turned = pltpu.roll(mixed[a], ox, 1)
                moved.append(jnp.where(lane >= ox, turned, before))
                before = turned
            before = jnp.zeros((full_y, TILE_X), f32)
            for a in range(gx):
                turned = pltpu.roll(moved[a], 1, 1)
                pair = moved[a] + jnp.where(lane >= 1, turned, before)
                before = turned
                pair = pair + jnp.where(row >= 1, pltpu.roll(pair, 1, 0), 0.0)
                rows[TILE_Y : TILE_Y + full_y, a * TILE_X : (a + 1) * TILE_X] = pair
            start = TILE_Y - oy
            rest = lax.rem(start, 8)
            window = rows[pl.ds(pl.multiple_of(start - rest, 8), full_y + 8), :]
            window = window.reshape(full_y // 8 + 1, 8, gx * TILE_X)
            window = pltpu.roll(window, lax.rem(8 - rest, 8), 1)
            within = iota((full_y // 8, 8, gx * TILE_X), 1) < 8 - rest
            out_ref[k] = jnp.where(within, window[:-1], window[1:]).reshape(full_y, gx * TILE_X)

    def copy(h, out_ref):
        for k in range(3):
            for a in range(gx):
                out_ref[k, :, a * TILE_X : (a + 1) * TILE_X] = tile(h, k, a)

    if first:

        @pl.when(ints_ref[0] == 0)
        def _():
            work(low, far_ref)
            work(1 - low, near_ref)

        @pl.when(ints_ref[0] > 0)
        def _():
            copy(low, far_ref)
            copy(1 - low, near_ref)
    else:
        work(low, far_ref)
        work(1 - low, near_ref)


def place(ints, matrix, got, gx, gy, first):
    shape = (3, gy * TILE_Y, gx * TILE_X)

    def body(*refs):
        place_kernel(gx, gy, first, *refs)

    return pl.pallas_call(
        body,
        in_specs=[
            pl.BlockSpec(memory_space=pltpu.SMEM),
            pl.BlockSpec(memory_space=pltpu.SMEM),
            pl.BlockSpec(memory_space=pltpu.VMEM),
        ],
        out_specs=[pl.BlockSpec(memory_space=pltpu.VMEM)] * 2,
        out_shape=[jax.ShapeDtypeStruct(shape, f32)] * 2,
        scratch_shapes=[pltpu.VMEM((TILE_Y * (gy + 1) + 8, gx * TILE_X), f32)],
        compiler_params=params(),
        name="place",
    )(ints, matrix, got)


def split(value):
    high = value.astype(bf16)
    return high, (value - high.astype(f32)).astype(bf16)


def dot(a, b):
    return lax.dot_general(a, b, (((1,), (0,)), ((), ())), preferred_element_type=f32)


def x_ops_kernel(pos_ref, mine_ref, first_ref, second_ref, high_ref, low_ref):
    place_x = pos_ref[0]
    core = pos_ref[1]
    rows = mine_ref.shape[2]

    def put(cls, block, where):
        high, low = split(block.T)
        spot = pl.ds(pl.multiple_of(where * rows, rows), rows)
        high_ref[cls, 0, :, spot] = high
        low_ref[cls, 0, :, spot] = low

    for cls in range(NCLASS):
        put(cls, mine_ref[cls, 0], place_x)
    half = NCLASS // 2
    for cls in range(half):
        put(core * half + cls, first_ref[cls, 0], 1 - place_x)
        put((1 - core) * half + cls, second_ref[cls, 0], 1 - place_x)


def y_ops_kernel(pos_ref, b0_ref, b1_ref, b2_ref, b3_ref, high_ref, low_ref):
    me = pos_ref[2]
    rows = b0_ref.shape[2]
    for step, ref in enumerate((b0_ref, b1_ref, b2_ref, b3_ref)):
        spot = pl.ds(pl.multiple_of((me ^ step) * rows, rows), rows)
        for cls in range(NCLASS):
            high, low = split(ref[cls, 0])
            high_ref[cls, 0, spot, :] = high
            low_ref[cls, 0, spot, :] = low


def prepare_ops(kernel, pos, blocks, length, name):
    def spec(block):
        return pl.BlockSpec((block.shape[0], 1) + block.shape[2:], lambda k: (0, k, 0, 0))

    out = jax.ShapeDtypeStruct((NCLASS, 3, length, length), bf16)
    return pl.pallas_call(
        kernel,
        grid=(3,),
        in_specs=[pl.BlockSpec(memory_space=pltpu.SMEM)] + [spec(b) for b in blocks],
        out_specs=[spec(out)] * 2,
        out_shape=[out] * 2,
        compiler_params=params(),
        name=name,
    )(pos, *blocks)


def gathered_ops(x_ops, y_ops):
    place_x = lax.axis_index("gx")
    place_y = lax.axis_index("gy")
    core = lax.rem(place_y, 2)
    half = NCLASS // 2
    swap_x = [(0, 1), (1, 0)]
    beside = [(i, i ^ 1) for i in range(4)]
    across = [(i, i ^ 2) for i in range(4)]
    piece = lax.dynamic_slice_in_dim(x_ops, core * half, half, 0)
    got_x = lax.ppermute(piece, "gx", swap_x)
    got_y = lax.ppermute(y_ops, "gy", across)
    pair_x = lax.ppermute(got_x, "gy", beside)
    pair_y = lax.ppermute(y_ops, "gy", beside)
    cross_y = lax.ppermute(got_y, "gy", beside)
    pos = jnp.stack([place_x, core, place_y]).astype(jnp.int32)
    length = x_ops.shape[3]
    x_parts = prepare_ops(x_ops_kernel, pos, (x_ops, got_x, pair_x), length, "x_operators")
    y_parts = prepare_ops(
        y_ops_kernel, pos, (y_ops, pair_y, got_y, cross_y), y_ops.shape[3], "y_operators"
    )
    return x_parts, y_parts


def sweep_kernel(
    gx, gy, count, last, xclass_ref, yclass_ref, xh_ref, xl_ref, yh_ref, yl_ref, *refs
):
    ins = refs[: CHUNKS * count]
    outs = refs[CHUNKS * count :]
    xclass = xclass_ref[...]
    yclass = yclass_ref[...]
    for chunk in range(CHUNKS):
        state = ins[chunk * count][0]
        for extra in ins[chunk * count + 1 : (chunk + 1) * count]:
            state = state + extra[0]
        high, low = split(state)
        swept = jnp.zeros(state.shape, f32)
        for cls in range(NCLASS):
            part = dot(high, xh_ref[cls, 0]) + dot(low, xh_ref[cls, 0]) + dot(high, xl_ref[cls, 0])
            swept = jnp.where(xclass == cls, part, swept)
        high, low = split(swept)
        final = jnp.zeros(state.shape, f32)
        for cls in range(NCLASS):
            part = dot(yh_ref[cls, 0], high) + dot(yh_ref[cls, 0], low) + dot(yl_ref[cls, 0], high)
            final = jnp.where(yclass == cls, part, final)
        if last:
            for a in range(gx):
                for b in range(gy):
                    outs[0][a * gy + b, chunk, 0] = final[
                        b * TILE_Y : (b + 1) * TILE_Y, a * TILE_X : (a + 1) * TILE_X
                    ]
        else:
            outs[chunk][0] = final


def sweep(classes, x_parts, y_parts, terms, gx, gy, last):
    full_y, full_x = gy * TILE_Y, gx * TILE_X
    count = len(terms[0])
    field = pl.BlockSpec((1, full_y, full_x), lambda k: (k, 0, 0))
    xop = pl.BlockSpec((NCLASS, 1, full_x, full_x), lambda k: (0, k, 0, 0))
    yop = pl.BlockSpec((NCLASS, 1, full_y, full_y), lambda k: (0, k, 0, 0))
    if last:
        out_specs = pl.BlockSpec(
            (gx * gy, CHUNKS, 1, TILE_Y, TILE_X), lambda k: (0, 0, k, 0, 0)
        )
        out_shape = jax.ShapeDtypeStruct((gx * gy, CHUNKS, 3, TILE_Y, TILE_X), f32)
    else:
        out_specs = [field] * CHUNKS
        out_shape = [jax.ShapeDtypeStruct((3, full_y, full_x), f32)] * CHUNKS

    def body(*refs):
        sweep_kernel(gx, gy, count, last, *refs)

    return pl.pallas_call(
        body,
        grid=(3,),
        in_specs=[
            pl.BlockSpec((full_y, 1), lambda k: (0, 0)),
            pl.BlockSpec((1, full_x), lambda k: (0, 0)),
            xop,
            xop,
            yop,
            yop,
        ]
        + [field] * (CHUNKS * count),
        out_specs=out_specs,
        out_shape=out_shape,
        compiler_params=params(),
        name="sweep",
    )(*classes, *x_parts, *y_parts, *[t for chunk in terms for t in chunk])


def output_kernel(flag_ref, u_ref, first_ref, second_ref, out_ref, turned):
    groups = first_ref.shape[0]
    per = CZ // groups
    half = per // 2

    @pl.when(flag_ref[0] == 0)
    def _():
        for z in range(CZ):
            turned[pl.ds(z, TILE_Y, stride=CZ), :] = u_ref[z, 0]

    @pl.when(flag_ref[0] > 0)
    def _():
        for z in range(CZ):
            g, i = divmod(z, per)
            ref = first_ref if i < half else second_ref
            turned[pl.ds(z, TILE_Y, stride=CZ), :] = ref[g, i % half, 0]

    out_ref[0, 0] = turned[...].T


def to_output(flag, planes, first, second):
    part = pl.BlockSpec(first.shape[:2] + (1, TILE_Y, TILE_X), lambda c: (0, 0, c, 0, 0))
    return pl.pallas_call(
        output_kernel,
        grid=(3,),
        in_specs=[
            pl.BlockSpec(memory_space=pltpu.SMEM),
            pl.BlockSpec((CZ, 1, TILE_Y, TILE_X), lambda c: (0, c, 0, 0)),
            part,
            part,
        ],
        out_specs=pl.BlockSpec((1, 1, TILE_X, TILE_Y * CZ), lambda c: (0, c, 0, 0)),
        out_shape=jax.ShapeDtypeStruct((1, 3, TILE_X, TILE_Y * CZ), f32),
        scratch_shapes=[pltpu.VMEM((TILE_Y * CZ, TILE_X), f32)],
        compiler_params=params(),
        name="to_output",
    )(flag, planes, first, second)


def local(fields, x_ops, y_ops, x_line_class, y_line_class, box_offset, coupling):
    gx, gy = lax.axis_size("gx"), lax.axis_size("gy")
    groups = gx * gy
    sec = lax.axis_index("sec")
    active = (sec == 3).astype(jnp.int32)
    member = jnp.minimum(sec, 2)
    offsets = lax.dynamic_index_in_dim(box_offset, member, 0, keepdims=False)
    matrix = lax.dynamic_index_in_dim(coupling, member, 0, keepdims=False) * (0.25 * time_step)
    matrix = jnp.where(active > 0, jnp.zeros_like(matrix), matrix)
    flag = active.reshape(1)
    lower = (sec < 2).astype(jnp.int32)
    ints = jnp.stack([active, lower, offsets[0], offsets[1]])

    planes, *edges = to_planes(fields[0])
    halo = exchange(*edges)
    x_parts, y_parts = gathered_ops(x_ops, y_ops)
    xclass = lax.all_gather(x_line_class, "gy", axis=0, tiled=True).reshape(-1, 1)
    yclass = lax.all_gather(y_line_class, "gx", axis=0, tiled=True).reshape(1, -1)

    acoustic = None
    for repeat in range(STEPS):
        last = repeat == STEPS - 1
        outs = flow(flag, planes, halo, groups, last)
        planes = outs[CHUNKS]
        if not last:
            halo = exchange(*outs[CHUNKS + 1 :])
        terms = []
        for chunk in range(CHUNKS):
            got = lax.all_to_all(outs[chunk], ("gx", "gy"), 0, 0)
            far, near = place(ints, matrix, got, gx, gy, repeat == 0)
            passed = lax.ppermute(far, "sec", [(0, 1), (3, 2)] if repeat == 0 else [(0, 1)])
            passed = lax.ppermute(far + passed, "sec", [(1, 2), (2, 1)])
            passed = lax.ppermute(near + passed, "sec", [(1, 0), (2, 3)])
            term = (near, passed)
            if acoustic is not None:
                term = (acoustic[chunk],) + term
            terms.append(term)
        acoustic = sweep((xclass, yclass), x_parts, y_parts, terms, gx, gy, last)
    tiles = lax.all_to_all(acoustic, ("gx", "gy"), 0, 0)
    brought = lax.ppermute(tiles, "sec", [(0, 3)])
    return to_output(flag, planes, brought, tiles)


highest = lax.Precision.HIGHEST


def from_root(shard, axis, root):
    mine = lax.axis_index(axis) == root
    return lax.psum(jnp.where(mine, shard, jnp.zeros_like(shard)), axis)


def padded_2(block, sides, width):
    for axis, dim in sides:
        count = lax.axis_size(axis)
        forward = [(i, i + 1) for i in range(count - 1)]
        backward = [(target, source) for source, target in forward]
        low = lax.ppermute(
            lax.slice_in_dim(block, block.shape[dim] - width, None, axis=dim), axis, forward
        )
        high = lax.ppermute(lax.slice_in_dim(block, 0, width, axis=dim), axis, backward)
        block = jnp.concatenate([low, block, high], axis=dim)
    return block


def shifted(value, axis, steps):
    count = lax.axis_size(axis)
    initial, last = (max(0, -steps), min(count, count - steps))
    return lax.ppermute(value, axis, [(source, source + steps) for source in range(initial, last)])


def flow_core(padded):
    centre = padded[:, 1:-1, 1:-1, :]
    ahead_x = padded[:, 2:, 1:-1, :]
    behind_x = padded[:, :-2, 1:-1, :]
    ahead_y = padded[:, 1:-1, 2:, :]
    behind_y = padded[:, 1:-1, :-2, :]
    ahead_z = jnp.roll(centre, -1, axis=3)
    behind_z = jnp.roll(centre, 1, axis=3)
    slope_x = 0.5 * (ahead_x - behind_x)
    slope_y = 0.5 * (ahead_y - behind_y)
    slope_z = 0.5 * (ahead_z - behind_z)
    laplace = ahead_x + behind_x + ahead_y + behind_y + ahead_z + behind_z - 6.0 * centre
    omega_x = slope_y[2] - slope_z[1]
    omega_y = slope_z[0] - slope_x[2]
    omega_z = slope_x[1] - slope_y[0]
    lamb_vector = jnp.stack(
        [
            omega_y * centre[2] - omega_z * centre[1],
            omega_z * centre[0] - omega_x * centre[2],
            omega_x * centre[1] - omega_y * centre[0],
        ]
    )
    updated = centre + time_step * (viscosity * laplace - lamb_vector)
    return (updated, lamb_vector)


def skip_flow(padded):
    centre = padded[:, 1:-1, 1:-1, :]
    return (centre, jnp.zeros_like(centre))


def unchanged(accrued):
    return accrued


def place_source(padded_lamb, offset_x, offset_y, matrix, span_x, span_y, extent_x, extent_y):
    anchor = jnp.zeros((), jnp.int32)
    corner_x = span_x - offset_x - 1
    corner_y = span_y - offset_y - 1
    window = lax.dynamic_slice(
        padded_lamb,
        (anchor, corner_x, corner_y, anchor),
        (3, extent_x + 1, extent_y + 1, padded_lamb.shape[3]),
    )
    averaged = 0.25 * (
        window[:, :-1, :-1] + window[:, 1:, :-1] + window[:, :-1, 1:] + window[:, 1:, 1:]
    )
    return jnp.einsum("kj,jxyz->kxyz", matrix, averaged, precision=highest)


def sweep_lines_x(state, x_ops, select_x, active):
    initial = jnp.zeros(state.shape[1:], jnp.float32)

    def add_piece(running, portion, anchor):

        def work(accrued):
            partial_value = jnp.einsum("ckij,kjl->ckil", x_ops, portion[0], precision=highest)
            return jnp.sum(partial_value * select_x[:, None, None, :], axis=0)

        return lax.cond(active, work, unchanged, running)

    return add_piece(initial, lax.all_gather(state, "gx", axis=2, tiled=True), jnp.int32(0))


def sweep_lines_y(state, y_ops, select_y, active):
    initial = jnp.zeros(state.shape[1:], jnp.float32)

    def add_piece(running, portion, anchor):

        def work(accrued):
            partial_value = jnp.einsum("ckij,kxjz->ckxiz", y_ops, portion[0], precision=highest)
            return jnp.sum(partial_value * select_y[:, None, :, None, None], axis=0)

        return lax.cond(active, work, unchanged, running)

    return add_piece(initial, lax.all_gather(state, "gy", axis=3, tiled=True), jnp.int32(0))


def local_general(fields, x_ops, y_ops, x_line_class, y_line_class, box_offset, coupling):
    sections = lax.axis_size("sec")
    section_index = lax.axis_index("sec")
    active = section_index == sections - 1
    member = jnp.minimum(section_index, sections - 2)
    span_x = fields.shape[2]
    merged = fields.shape[3]
    span_y = merged // CZ
    classes = jnp.arange(NCLASS, dtype=jnp.int32)
    select_y = (classes[:, None] == y_line_class[None, :]).astype(jnp.float32)
    offsets = lax.dynamic_index_in_dim(box_offset, member, 0, keepdims=False)
    matrix = lax.dynamic_index_in_dim(coupling, member, 0, keepdims=False)
    current = fields[0].reshape(3, span_x, span_y, CZ)
    share = CZ // sections
    whole_start = from_root(current, "sec", sections - 1)
    acoustic = lax.dynamic_slice_in_dim(whole_start, section_index * share, share, 3)
    for repeat in range(STEPS):
        padded = padded_2(current, (("gx", 1), ("gy", 2)), 1)
        flowed, lamb_vector = lax.cond(active, skip_flow, flow_core, padded)
        left_tile = shifted(lamb_vector, "gx", 1)
        joined = jnp.concatenate([left_tile, lamb_vector], axis=1)
        lower_tile = shifted(joined, "gy", 1)
        joined = jnp.concatenate([lower_tile, joined], axis=2)
        contribution = place_source(
            joined, offsets[0], offsets[1], matrix, span_x, span_y, span_x, span_y
        )
        source = lax.psum_scatter(contribution, "sec", scatter_dimension=3, tiled=True)
        amplitudes_grid = acoustic + time_step * source
        busy = jnp.asarray(True)
        planes = amplitudes_grid.shape[3]
        merged_now = span_y * planes
        select_x = jnp.broadcast_to(
            (classes[:, None, None] == x_line_class[None, :, None]).astype(jnp.float32),
            (NCLASS, span_y, planes),
        ).reshape(NCLASS, merged_now)
        amplitudes = amplitudes_grid.reshape(1, 3, span_x, merged_now)
        swept_x = sweep_lines_x(amplitudes, x_ops, select_x, busy)
        acoustic = sweep_lines_y(
            swept_x.reshape(1, 3, span_x, span_y, planes), y_ops, select_y, busy
        )
        current = flowed
    whole_end = lax.all_gather(acoustic, "sec", axis=3, tiled=True)
    current = jnp.where(active, whole_end, current)
    return current.reshape(1, 3, span_x, merged)


def whole_planes_fit(mesh):
    sizes = dict(mesh.shape)
    return sizes["sec"] == 4 and sizes["gx"] == 2 and sizes["gy"] == 4


def solution(mesh):
    placed = (
        P("sec", None, "gx", "gy"),
        P(None, None, "gx", None),
        P(None, None, "gy", None),
        P("gy"),
        P("gx"),
        P(),
        P(),
    )
    return jax.shard_map(
        local if whole_planes_fit(mesh) else local_general,
        mesh=mesh,
        in_specs=placed,
        out_specs=P("sec", None, "gx", "gy"),
        check_vma=False,
    )
```

```python
import jax
import jax.numpy as jnp
from jax import lax
from jax.experimental import pallas as pl
from jax.experimental.pallas import tpu as pltpu
from jax.sharding import PartitionSpec as P

CZ = 32
NCLASS = 4
STEPS = 2
TILE_X = 128
TILE_Y = 64
CHUNKS = 2

time_step = 0.2
viscosity = 0.25
vmem_limit = 56 * 1024 * 1024
f32 = jnp.float32
bf16 = jnp.bfloat16


def params():
    return pltpu.CompilerParams(vmem_limit_bytes=vmem_limit)


def iota(shape, dim):
    return lax.broadcasted_iota(jnp.int32, shape, dim)


def edges_kernel(left_ref, right_ref, down_ref, up_ref, west_ref, east_ref, south_ref, north_ref, turned):
    comp = pl.program_id(0)
    lane = iota((TILE_Y, TILE_X), 1)
    for ref, which, out_ref in ((left_ref, 0, west_ref), (right_ref, 7, east_ref)):
        turned[:, 0:8] = ref[0].T

        @pl.when(comp == 0)
        def _():
            out_ref[...] = jnp.zeros_like(out_ref)

        gathered = out_ref[...]
        for z in range(CZ):
            column = turned[pl.ds(z, TILE_Y, stride=CZ), :][:, which : which + 1]
            gathered = jnp.where(lane == z * 3 + comp, column, gathered)
        out_ref[...] = gathered
    south_ref[0] = down_ref[0].T[0:CZ]
    north_ref[0] = up_ref[0].T[TILE_X - CZ :]


def tile_edges(field):
    merged = field.shape[2]
    edge = pl.BlockSpec((TILE_Y, TILE_X), lambda c: (0, 0))
    side = pl.BlockSpec((1, CZ, TILE_X), lambda c: (c, 0, 0))
    return pl.pallas_call(
        edges_kernel,
        grid=(3,),
        in_specs=[
            pl.BlockSpec((1, 8, merged), lambda c: (c, 0, 0)),
            pl.BlockSpec((1, 8, merged), lambda c: (c, TILE_X // 8 - 1, 0)),
            pl.BlockSpec((1, TILE_X, 128), lambda c: (c, 0, 0)),
            pl.BlockSpec((1, TILE_X, 128), lambda c: (c, 0, merged // 128 - 1)),
        ],
        out_specs=[edge, edge, side, side],
        out_shape=[jax.ShapeDtypeStruct((TILE_Y, TILE_X), f32)] * 2
        + [jax.ShapeDtypeStruct((3, CZ, TILE_X), f32)] * 2,
        scratch_shapes=[pltpu.VMEM((merged, 128), f32)],
        compiler_params=params(),
        name="tile_edges",
    )(field, field, field, field)


def planes_kernel(field_ref, planes_ref, turned):
    turned[...] = field_ref[0].T
    for z in range(CZ):
        planes_ref[z, 0] = turned[pl.ds(z, TILE_Y, stride=CZ), :]


def to_planes(field, waits):
    count = len(waits)

    def body(field_ref, *refs):
        planes_kernel(field_ref, *refs[count:])

    return pl.pallas_call(
        body,
        grid=(3,),
        in_specs=[pl.BlockSpec((1, TILE_X, TILE_Y * CZ), lambda c: (c, 0, 0))]
        + [pl.BlockSpec(memory_space=pl.ANY)] * count,
        out_specs=pl.BlockSpec((CZ, 1, TILE_Y, TILE_X), lambda c: (0, c, 0, 0)),
        out_shape=jax.ShapeDtypeStruct((CZ, 3, TILE_Y, TILE_X), f32),
        scratch_shapes=[pltpu.VMEM((TILE_Y * CZ, TILE_X), f32)],
        compiler_params=params(),
        name="to_planes",
    )(field, *waits)


def flow_kernel(per, want, flag_ref, u_ref, xlo_ref, xhi_ref, ylo_ref, yhi_ref, *outs):
    outs = list(outs)
    lamb_ref = outs.pop(0) if "lamb" in want else None
    next_ref = outs.pop(0) if "next" in want else None
    group = pl.program_id(0)
    acoustic = flag_ref[0] > 0
    lane = iota((TILE_Y, TILE_X), 1)
    row = iota((TILE_Y, TILE_X), 0)
    turn = lax.rem(TILE_X - group * (per * 3), TILE_X)
    xlo = pltpu.roll(xlo_ref[...], turn, 1)
    xhi = pltpu.roll(xhi_ref[...], turn, 1)
    if "edges" in want:
        west_ref, east_ref, south_ref, north_ref = outs

        @pl.when(group == 0)
        def _():
            west_ref[...] = jnp.zeros_like(west_ref)
            east_ref[...] = jnp.zeros_like(east_ref)

        west = west_ref[...]
        east = east_ref[...]
    for i in range(per):
        z = group * per + i
        above = lax.rem(z + 1, CZ)
        below = lax.rem(z + CZ - 1, CZ)
        centre, lap, dx, dy, dz = [], [], [], [], []
        for c in range(3):
            mid = u_ref[z, c]
            up = u_ref[above, c]
            down = u_ref[below, c]
            spot = i * 3 + c
            xm = jnp.where(lane == 0, xlo[:, spot : spot + 1], pltpu.roll(mid, 1, 1))
            xp = jnp.where(
                lane == TILE_X - 1, xhi[:, spot : spot + 1], pltpu.roll(mid, TILE_X - 1, 1)
            )
            ym = jnp.where(row == 0, ylo_ref[c, pl.ds(z, 1), :], pltpu.roll(mid, 1, 0))
            yp = jnp.where(
                row == TILE_Y - 1, yhi_ref[c, pl.ds(z, 1), :], pltpu.roll(mid, TILE_Y - 1, 0)
            )
            centre.append(mid)
            lap.append(xp + xm + yp + ym + up + down - 6.0 * mid)
            dx.append(0.5 * (xp - xm))
            dy.append(0.5 * (yp - ym))
            dz.append(0.5 * (up - down))
        ox = dy[2] - dz[1]
        oy = dz[0] - dx[2]
        oz = dx[1] - dy[0]
        lamb = (
            oy * centre[2] - oz * centre[1],
            oz * centre[0] - ox * centre[2],
            ox * centre[1] - oy * centre[0],
        )
        for c in range(3):
            if "lamb" in want:
                sent = jnp.where(acoustic, centre[c], lamb[c]) if "passed" in want else lamb[c]
                lamb_ref[0, i // CHUNKS, i % CHUNKS, c] = sent
            if "next" in want:
                moved = centre[c] + time_step * (viscosity * lap[c] - lamb[c])
                next_ref[i, c] = moved
            if "edges" in want:
                here = lane == z * 3 + c
                west = jnp.where(here, moved[:, 0:1], west)
                east = jnp.where(here, moved[:, TILE_X - 1 :], east)
                south_ref[c, pl.ds(z, 1), :] = moved[0:1, :]
                north_ref[c, pl.ds(z, 1), :] = moved[TILE_Y - 1 :, :]
    if "edges" in want:
        west_ref[...] = west
        east_ref[...] = east


def flow(flag, planes, halo, waits, groups, want):
    per = CZ // groups
    halves = per // CHUNKS
    edge = pl.BlockSpec((TILE_Y, TILE_X), lambda g: (0, 0))
    side = pl.BlockSpec((3, CZ, TILE_X), lambda g: (0, 0, 0))
    out_specs, out_shape = [], []
    if "lamb" in want:
        out_specs.append(
            pl.BlockSpec((1, halves, CHUNKS, 3, TILE_Y, TILE_X), lambda g: (g, 0, 0, 0, 0, 0))
        )
        out_shape.append(
            jax.ShapeDtypeStruct((groups, halves, CHUNKS, 3, TILE_Y, TILE_X), f32)
        )
    if "next" in want:
        out_specs.append(pl.BlockSpec((per, 3, TILE_Y, TILE_X), lambda g: (g, 0, 0, 0)))
        out_shape.append(jax.ShapeDtypeStruct((CZ, 3, TILE_Y, TILE_X), f32))
    if "edges" in want:
        out_specs += [edge, edge, side, side]
        out_shape += [jax.ShapeDtypeStruct((TILE_Y, TILE_X), f32)] * 2
        out_shape += [jax.ShapeDtypeStruct((3, CZ, TILE_X), f32)] * 2
    count = len(waits)

    def body(*refs):
        flow_kernel(per, want, *refs[:6], *refs[6 + count :])

    return pl.pallas_call(
        body,
        grid=(groups,),
        in_specs=[
            pl.BlockSpec(memory_space=pltpu.SMEM),
            pl.BlockSpec((CZ, 3, TILE_Y, TILE_X), lambda g: (0, 0, 0, 0)),
            edge,
            edge,
            side,
            side,
        ]
        + [pl.BlockSpec(memory_space=pl.ANY)] * count,
        out_specs=out_specs,
        out_shape=out_shape,
        compiler_params=params(),
        name="flow",
    )(flag, planes, *halo, *waits)


def exchange(west, east, south, north):
    def send(value, axis, step):
        count = lax.axis_size(axis)
        return lax.ppermute(
            value, axis, [(i, i + step) for i in range(count) if 0 <= i + step < count]
        )

    return (
        send(east, "gx", 1),
        send(west, "gx", -1),
        send(north, "gy", 1),
        send(south, "gy", -1),
    )


def place_kernel(gx, gy, first, ints_ref, matrix_ref, got_ref, far_ref, near_ref, rows):
    low = ints_ref[1]
    ox = ints_ref[2]
    oy = ints_ref[3]
    full_y = gy * TILE_Y
    lane = iota((full_y, TILE_X), 1)
    row = iota((full_y, TILE_X), 0)

    def tile(h, j, a):
        return jnp.concatenate([got_ref[a * gy + b, h, 0, j] for b in range(gy)], axis=0)

    def work(h, out_ref):
        for a in range(gx):
            rows[0:TILE_Y, a * TILE_X : (a + 1) * TILE_X] = jnp.zeros((TILE_Y, TILE_X), f32)
        vectors = [[tile(h, j, a) for a in range(gx)] for j in range(3)]
        for k in range(3):
            mixed = [
                matrix_ref[k, 0] * vectors[0][a]
                + matrix_ref[k, 1] * vectors[1][a]
                + matrix_ref[k, 2] * vectors[2][a]
                for a in range(gx)
            ]
            before = jnp.zeros((full_y, TILE_X), f32)
            moved = []
            for a in range(gx):
                turned = pltpu.roll(mixed[a], ox, 1)
                moved.append(jnp.where(lane >= ox, turned, before))
                before = turned
            before = jnp.zeros((full_y, TILE_X), f32)
            for a in range(gx):
                turned = pltpu.roll(moved[a], 1, 1)
                pair = moved[a] + jnp.where(lane >= 1, turned, before)
                before = turned
                pair = pair + jnp.where(row >= 1, pltpu.roll(pair, 1, 0), 0.0)
                rows[TILE_Y : TILE_Y + full_y, a * TILE_X : (a + 1) * TILE_X] = pair
            start = TILE_Y - oy
            rest = lax.rem(start, 8)
            window = rows[pl.ds(pl.multiple_of(start - rest, 8), full_y + 8), :]
            window = window.reshape(full_y // 8 + 1, 8, gx * TILE_X)
            window = pltpu.roll(window, lax.rem(8 - rest, 8), 1)
            within = iota((full_y // 8, 8, gx * TILE_X), 1) < 8 - rest
            out_ref[k] = jnp.where(within, window[:-1], window[1:]).reshape(full_y, gx * TILE_X)

    def copy(h, out_ref):
        for k in range(3):
            for a in range(gx):
                out_ref[k, :, a * TILE_X : (a + 1) * TILE_X] = tile(h, k, a)

    if first:

        @pl.when(ints_ref[0] == 0)
        def _():
            work(low, far_ref)
            work(1 - low, near_ref)

        @pl.when(ints_ref[0] > 0)
        def _():
            copy(low, far_ref)
            copy(1 - low, near_ref)
    else:
        work(low, far_ref)
        work(1 - low, near_ref)


def place(ints, matrix, got, chunk, waits, gx, gy, first):
    shape = (3, gy * TILE_Y, gx * TILE_X)
    count = len(waits)

    def body(*refs):
        place_kernel(gx, gy, first, *refs[:3], *refs[3 + count :])

    block = got.shape[:2] + (1,) + got.shape[3:]
    return pl.pallas_call(
        body,
        grid=(1,),
        in_specs=[
            pl.BlockSpec(memory_space=pltpu.SMEM),
            pl.BlockSpec(memory_space=pltpu.SMEM),
            pl.BlockSpec(block, lambda i: (0, 0, chunk, 0, 0, 0)),
        ]
        + [pl.BlockSpec(memory_space=pl.ANY)] * count,
        out_specs=[pl.BlockSpec(shape, lambda i: (0, 0, 0))] * 2,
        out_shape=[jax.ShapeDtypeStruct(shape, f32)] * 2,
        scratch_shapes=[pltpu.VMEM((TILE_Y * (gy + 1) + 8, gx * TILE_X), f32)],
        compiler_params=params(),
        name="place",
    )(ints, matrix, got, *waits)


def tie_kernel(*refs):
    pass


def after(value, earlier):
    anywhere = pl.BlockSpec(memory_space=pl.ANY)
    if not earlier:
        return value
    return pl.pallas_call(
        tie_kernel,
        in_specs=[anywhere] * (1 + len(earlier)),
        out_specs=anywhere,
        out_shape=jax.ShapeDtypeStruct(value.shape, value.dtype),
        input_output_aliases={0: 0},
        name="after",
    )(value, *earlier)


def split(value):
    high = value.astype(bf16)
    return high, (value - high.astype(f32)).astype(bf16)


def dot(a, b):
    return lax.dot_general(a, b, (((1,), (0,)), ((), ())), preferred_element_type=f32)


def x_ops_kernel(pos_ref, mine_ref, first_ref, second_ref, high_ref, low_ref):
    place_x = pos_ref[0]
    core = pos_ref[1]
    rows = mine_ref.shape[2]

    def put(cls, block, where):
        high, low = split(block.T)
        spot = pl.ds(pl.multiple_of(where * rows, rows), rows)
        high_ref[cls, 0, :, spot] = high
        low_ref[cls, 0, :, spot] = low

    for cls in range(NCLASS):
        put(cls, mine_ref[cls, 0], place_x)
    half = NCLASS // 2
    for cls in range(half):
        put(core * half + cls, first_ref[cls, 0], 1 - place_x)
        put((1 - core) * half + cls, second_ref[cls, 0], 1 - place_x)


def y_ops_kernel(pos_ref, b0_ref, b1_ref, b2_ref, b3_ref, high_ref, low_ref):
    me = pos_ref[2]
    rows = b0_ref.shape[2]
    for step, ref in enumerate((b0_ref, b1_ref, b2_ref, b3_ref)):
        spot = pl.ds(pl.multiple_of((me ^ step) * rows, rows), rows)
        for cls in range(NCLASS):
            high, low = split(ref[cls, 0])
            high_ref[cls, 0, spot, :] = high
            low_ref[cls, 0, spot, :] = low


def prepare_ops(kernel, pos, blocks, length, name):
    def spec(block):
        return pl.BlockSpec((block.shape[0], 1) + block.shape[2:], lambda k: (0, k, 0, 0))

    out = jax.ShapeDtypeStruct((NCLASS, 3, length, length), bf16)
    return pl.pallas_call(
        kernel,
        grid=(3,),
        in_specs=[pl.BlockSpec(memory_space=pltpu.SMEM)] + [spec(b) for b in blocks],
        out_specs=[spec(out)] * 2,
        out_shape=[out] * 2,
        compiler_params=params(),
        name=name,
    )(pos, *blocks)


def fetched_ops(x_ops, y_ops):
    core = lax.rem(lax.axis_index("gy"), 2)
    half = NCLASS // 2
    piece = lax.dynamic_slice_in_dim(x_ops, core * half, half, 0)
    got_x = lax.ppermute(piece, "gx", [(0, 1), (1, 0)])
    got_y = lax.ppermute(y_ops, "gy", [(i, i ^ 2) for i in range(4)])
    return got_x, got_y


def prepared_ops(x_ops, y_ops, fetched):
    got_x, got_y = fetched
    beside = [(i, i ^ 1) for i in range(4)]
    pair_x = lax.ppermute(got_x, "gy", beside)
    pair_y = lax.ppermute(y_ops, "gy", beside)
    cross_y = lax.ppermute(got_y, "gy", beside)
    place_y = lax.axis_index("gy")
    pos = jnp.stack([lax.axis_index("gx"), lax.rem(place_y, 2), place_y]).astype(jnp.int32)
    x_parts = prepare_ops(
        x_ops_kernel, pos, (x_ops, got_x, pair_x), x_ops.shape[3], "x_operators"
    )
    y_parts = prepare_ops(
        y_ops_kernel, pos, (y_ops, pair_y, got_y, cross_y), y_ops.shape[3], "y_operators"
    )
    return x_parts, y_parts


def gathered_classes(x_line_class, y_line_class):
    def rows(value, axis):
        count = lax.axis_size(axis)
        blocks = [value] + [
            lax.ppermute(value, axis, [(i, i ^ step) for i in range(count)])
            for step in range(1, count)
        ]
        order = jnp.arange(count) ^ lax.axis_index(axis)
        return jnp.take(jnp.stack(blocks), order, axis=0)

    return rows(x_line_class, "gy").reshape(-1, 1), rows(y_line_class, "gx").reshape(1, -1)


def sweep_kernel(gx, gy, count, last, xclass_ref, yclass_ref, xh_ref, xl_ref, yh_ref, yl_ref, *refs):
    ins = refs[:count]
    out_ref = refs[count]
    xclass = xclass_ref[...]
    yclass = yclass_ref[...]
    state = ins[0][0]
    for extra in ins[1:]:
        state = state + extra[0]
    high, low = split(state)
    swept = jnp.zeros(state.shape, f32)
    for cls in range(NCLASS):
        part = dot(high, xh_ref[cls, 0]) + dot(low, xh_ref[cls, 0]) + dot(high, xl_ref[cls, 0])
        swept = jnp.where(xclass == cls, part, swept)
    high, low = split(swept)
    final = jnp.zeros(state.shape, f32)
    for cls in range(NCLASS):
        part = dot(yh_ref[cls, 0], high) + dot(yh_ref[cls, 0], low) + dot(yl_ref[cls, 0], high)
        final = jnp.where(yclass == cls, part, final)
    if last:
        for a in range(gx):
            for b in range(gy):
                out_ref[a * gy + b, 0] = final[
                    b * TILE_Y : (b + 1) * TILE_Y, a * TILE_X : (a + 1) * TILE_X
                ]
    else:
        out_ref[0] = final


def sweep(classes, x_parts, y_parts, terms, gx, gy, last):
    full_y, full_x = gy * TILE_Y, gx * TILE_X
    count = len(terms)
    field = pl.BlockSpec((1, full_y, full_x), lambda k: (k, 0, 0))
    xop = pl.BlockSpec((NCLASS, 1, full_x, full_x), lambda k: (0, k, 0, 0))
    yop = pl.BlockSpec((NCLASS, 1, full_y, full_y), lambda k: (0, k, 0, 0))
    if last:
        out_specs = pl.BlockSpec((gx * gy, 1, TILE_Y, TILE_X), lambda k: (0, k, 0, 0))
        out_shape = jax.ShapeDtypeStruct((gx * gy, 3, TILE_Y, TILE_X), f32)
    else:
        out_specs = field
        out_shape = jax.ShapeDtypeStruct((3, full_y, full_x), f32)

    def body(*refs):
        sweep_kernel(gx, gy, count, last, *refs)

    return pl.pallas_call(
        body,
        grid=(3,),
        in_specs=[
            pl.BlockSpec((full_y, 1), lambda k: (0, 0)),
            pl.BlockSpec((1, full_x), lambda k: (0, 0)),
            xop,
            xop,
            yop,
            yop,
        ]
        + [field] * count,
        out_specs=out_specs,
        out_shape=out_shape,
        compiler_params=params(),
        name="sweep",
    )(*classes, *x_parts, *y_parts, *terms)


def output_kernel(flag_ref, u_ref, *refs):
    parts = refs[: 2 * CHUNKS]
    out_ref, turned = refs[2 * CHUNKS :]
    per = CZ // parts[0].shape[0]

    @pl.when(flag_ref[0] == 0)
    def _():
        for z in range(CZ):
            turned[pl.ds(z, TILE_Y, stride=CZ), :] = u_ref[z, 0]

    @pl.when(flag_ref[0] > 0)
    def _():
        for z in range(CZ):
            g, i = divmod(z, per)
            turned[pl.ds(z, TILE_Y, stride=CZ), :] = parts[i][g, 0]

    out_ref[0, 0] = turned[...].T


def to_output(flag, planes, parts):
    part = pl.BlockSpec(parts[0].shape[:1] + (1, TILE_Y, TILE_X), lambda c: (0, c, 0, 0))
    return pl.pallas_call(
        output_kernel,
        grid=(3,),
        in_specs=[
            pl.BlockSpec(memory_space=pltpu.SMEM),
            pl.BlockSpec((CZ, 1, TILE_Y, TILE_X), lambda c: (0, c, 0, 0)),
        ]
        + [part] * (2 * CHUNKS),
        out_specs=pl.BlockSpec((1, 1, TILE_X, TILE_Y * CZ), lambda c: (0, c, 0, 0)),
        out_shape=jax.ShapeDtypeStruct((1, 3, TILE_X, TILE_Y * CZ), f32),
        scratch_shapes=[pltpu.VMEM((TILE_Y * CZ, TILE_X), f32)],
        compiler_params=params(),
        name="to_output",
    )(flag, planes, *parts)


def local(fields, x_ops, y_ops, x_line_class, y_line_class, box_offset, coupling):
    gx, gy = lax.axis_size("gx"), lax.axis_size("gy")
    groups = gx * gy
    sec = lax.axis_index("sec")
    active = (sec == 3).astype(jnp.int32)
    member = jnp.minimum(sec, 2)
    offsets = lax.dynamic_index_in_dim(box_offset, member, 0, keepdims=False)
    matrix = lax.dynamic_index_in_dim(coupling, member, 0, keepdims=False) * (0.25 * time_step)
    matrix = jnp.where(active > 0, jnp.zeros_like(matrix), matrix)
    flag = active.reshape(1)
    lower = (sec < 2).astype(jnp.int32)
    ints = jnp.stack([active, lower, offsets[0], offsets[1]])

    halo = exchange(*tile_edges(fields[0]))
    fetched = fetched_ops(x_ops, y_ops)
    classes = gathered_classes(x_line_class, y_line_class)
    planes = to_planes(fields[0], ())

    waits = (*fetched, *classes)
    (lamb,) = flow(flag, planes, halo, waits, groups, ("lamb", "passed"))
    gots = [lax.all_to_all(lamb, ("gx", "gy"), 0, 0)]
    planes, *edges = flow(flag, planes, halo, (lamb,), groups, ("next", "edges"))
    halo = exchange(*edges)
    fetched = [after(value, [planes]) for value in fetched]
    x_parts, y_parts = prepared_ops(x_ops, y_ops, fetched)
    lamb, planes = flow(flag, planes, halo, (*x_parts, *y_parts), groups, ("lamb", "next"))
    gots[0] = after(gots[0], [lamb])
    gots.append(lax.all_to_all(after(lamb, [gots[0]]), ("gx", "gy"), 0, 0))

    total = STEPS * CHUNKS
    fars, nears, firsts, seconds, thirds, ends = ([None] * total for _ in range(6))
    token = []

    def placed(n):
        first = n < CHUNKS
        got = gots[n // CHUNKS]
        fars[n], nears[n] = place(ints, matrix, got, n % CHUNKS, token, gx, gy, first)
        firsts[n] = lax.ppermute(fars[n], "sec", [(0, 1), (3, 2)] if first else [(0, 1)])
        return fars[n]

    def first_hop(n):
        value = fars[n] + after(firsts[n], token)
        seconds[n] = lax.ppermute(value, "sec", [(1, 2), (2, 1)])
        return value

    def second_hop(n):
        value = nears[n] + after(seconds[n], token)
        thirds[n] = lax.ppermute(value, "sec", [(1, 0), (2, 3)])
        return value

    def swept(n):
        terms = (nears[n], after(thirds[n], token))
        if n >= CHUNKS:
            terms += (ends[n - CHUNKS],)
        ends[n] = sweep(classes, x_parts, y_parts, terms, gx, gy, n >= total - CHUNKS)
        return ends[n]

    order = (
        (placed, 0), (placed, 1), (first_hop, 0), (first_hop, 1), (second_hop, 0),
        (placed, 2), (placed, 3), (second_hop, 1), (first_hop, 2), (swept, 0),
        (first_hop, 3), (second_hop, 2), (swept, 1), (second_hop, 3), (swept, 2), (swept, 3),
    )
    for work, n in order:
        token = [work(n)]
    tiles = [lax.all_to_all(value, ("gx", "gy"), 0, 0) for value in ends[-CHUNKS:]]
    brought = [lax.ppermute(value, "sec", [(0, 3)]) for value in tiles]
    return to_output(flag, planes, brought + tiles)


highest = lax.Precision.HIGHEST


def from_root(shard, axis, root):
    mine = lax.axis_index(axis) == root
    return lax.psum(jnp.where(mine, shard, jnp.zeros_like(shard)), axis)


def padded_2(block, sides, width):
    for axis, dim in sides:
        count = lax.axis_size(axis)
        forward = [(i, i + 1) for i in range(count - 1)]
        backward = [(target, source) for source, target in forward]
        low = lax.ppermute(
            lax.slice_in_dim(block, block.shape[dim] - width, None, axis=dim), axis, forward
        )
        high = lax.ppermute(lax.slice_in_dim(block, 0, width, axis=dim), axis, backward)
        block = jnp.concatenate([low, block, high], axis=dim)
    return block


def shifted(value, axis, steps):
    count = lax.axis_size(axis)
    initial, last = (max(0, -steps), min(count, count - steps))
    return lax.ppermute(value, axis, [(source, source + steps) for source in range(initial, last)])


def flow_core(padded):
    centre = padded[:, 1:-1, 1:-1, :]
    ahead_x = padded[:, 2:, 1:-1, :]
    behind_x = padded[:, :-2, 1:-1, :]
    ahead_y = padded[:, 1:-1, 2:, :]
    behind_y = padded[:, 1:-1, :-2, :]
    ahead_z = jnp.roll(centre, -1, axis=3)
    behind_z = jnp.roll(centre, 1, axis=3)
    slope_x = 0.5 * (ahead_x - behind_x)
    slope_y = 0.5 * (ahead_y - behind_y)
    slope_z = 0.5 * (ahead_z - behind_z)
    laplace = ahead_x + behind_x + ahead_y + behind_y + ahead_z + behind_z - 6.0 * centre
    omega_x = slope_y[2] - slope_z[1]
    omega_y = slope_z[0] - slope_x[2]
    omega_z = slope_x[1] - slope_y[0]
    lamb_vector = jnp.stack(
        [
            omega_y * centre[2] - omega_z * centre[1],
            omega_z * centre[0] - omega_x * centre[2],
            omega_x * centre[1] - omega_y * centre[0],
        ]
    )
    updated = centre + time_step * (viscosity * laplace - lamb_vector)
    return (updated, lamb_vector)


def skip_flow(padded):
    centre = padded[:, 1:-1, 1:-1, :]
    return (centre, jnp.zeros_like(centre))


def unchanged(accrued):
    return accrued


def place_source(padded_lamb, offset_x, offset_y, matrix, span_x, span_y, extent_x, extent_y):
    anchor = jnp.zeros((), jnp.int32)
    corner_x = span_x - offset_x - 1
    corner_y = span_y - offset_y - 1
    window = lax.dynamic_slice(
        padded_lamb,
        (anchor, corner_x, corner_y, anchor),
        (3, extent_x + 1, extent_y + 1, padded_lamb.shape[3]),
    )
    averaged = 0.25 * (
        window[:, :-1, :-1] + window[:, 1:, :-1] + window[:, :-1, 1:] + window[:, 1:, 1:]
    )
    return jnp.einsum("kj,jxyz->kxyz", matrix, averaged, precision=highest)


def sweep_lines_x(state, x_ops, select_x, active):
    initial = jnp.zeros(state.shape[1:], jnp.float32)

    def add_piece(running, portion, anchor):

        def work(accrued):
            partial_value = jnp.einsum("ckij,kjl->ckil", x_ops, portion[0], precision=highest)
            return jnp.sum(partial_value * select_x[:, None, None, :], axis=0)

        return lax.cond(active, work, unchanged, running)

    return add_piece(initial, lax.all_gather(state, "gx", axis=2, tiled=True), jnp.int32(0))


def sweep_lines_y(state, y_ops, select_y, active):
    initial = jnp.zeros(state.shape[1:], jnp.float32)

    def add_piece(running, portion, anchor):

        def work(accrued):
            partial_value = jnp.einsum("ckij,kxjz->ckxiz", y_ops, portion[0], precision=highest)
            return jnp.sum(partial_value * select_y[:, None, :, None, None], axis=0)

        return lax.cond(active, work, unchanged, running)

    return add_piece(initial, lax.all_gather(state, "gy", axis=3, tiled=True), jnp.int32(0))


def local_general(fields, x_ops, y_ops, x_line_class, y_line_class, box_offset, coupling):
    sections = lax.axis_size("sec")
    section_index = lax.axis_index("sec")
    active = section_index == sections - 1
    member = jnp.minimum(section_index, sections - 2)
    span_x = fields.shape[2]
    merged = fields.shape[3]
    span_y = merged // CZ
    classes = jnp.arange(NCLASS, dtype=jnp.int32)
    select_y = (classes[:, None] == y_line_class[None, :]).astype(jnp.float32)
    offsets = lax.dynamic_index_in_dim(box_offset, member, 0, keepdims=False)
    matrix = lax.dynamic_index_in_dim(coupling, member, 0, keepdims=False)
    current = fields[0].reshape(3, span_x, span_y, CZ)
    share = CZ // sections
    whole_start = from_root(current, "sec", sections - 1)
    acoustic = lax.dynamic_slice_in_dim(whole_start, section_index * share, share, 3)
    for repeat in range(STEPS):
        padded = padded_2(current, (("gx", 1), ("gy", 2)), 1)
        flowed, lamb_vector = lax.cond(active, skip_flow, flow_core, padded)
        left_tile = shifted(lamb_vector, "gx", 1)
        joined = jnp.concatenate([left_tile, lamb_vector], axis=1)
        lower_tile = shifted(joined, "gy", 1)
        joined = jnp.concatenate([lower_tile, joined], axis=2)
        contribution = place_source(
            joined, offsets[0], offsets[1], matrix, span_x, span_y, span_x, span_y
        )
        source = lax.psum_scatter(contribution, "sec", scatter_dimension=3, tiled=True)
        amplitudes_grid = acoustic + time_step * source
        busy = jnp.asarray(True)
        planes = amplitudes_grid.shape[3]
        merged_now = span_y * planes
        select_x = jnp.broadcast_to(
            (classes[:, None, None] == x_line_class[None, :, None]).astype(jnp.float32),
            (NCLASS, span_y, planes),
        ).reshape(NCLASS, merged_now)
        amplitudes = amplitudes_grid.reshape(1, 3, span_x, merged_now)
        swept_x = sweep_lines_x(amplitudes, x_ops, select_x, busy)
        acoustic = sweep_lines_y(
            swept_x.reshape(1, 3, span_x, span_y, planes), y_ops, select_y, busy
        )
        current = flowed
    whole_end = lax.all_gather(acoustic, "sec", axis=3, tiled=True)
    current = jnp.where(active, whole_end, current)
    return current.reshape(1, 3, span_x, merged)


def whole_planes_fit(mesh):
    sizes = dict(mesh.shape)
    return sizes["sec"] == 4 and sizes["gx"] == 2 and sizes["gy"] == 4


def solution(mesh):
    placed = (
        P("sec", None, "gx", "gy"),
        P(None, None, "gx", None),
        P(None, None, "gy", None),
        P("gy"),
        P("gx"),
        P(),
        P(),
    )
    return jax.shard_map(
        local if whole_planes_fit(mesh) else local_general,
        mesh=mesh,
        in_specs=placed,
        out_specs=P("sec", None, "gx", "gy"),
        check_vma=False,
    )
```

```python
import jax
import jax.numpy as jnp
from jax import lax
from jax.experimental import pallas as pl
from jax.experimental.pallas import tpu as pltpu
from jax.sharding import PartitionSpec as P

CZ = 32
NCLASS = 4
STEPS = 2
TILE_X = 128
TILE_Y = 64
CHUNKS = 2

time_step = 0.2
viscosity = 0.25
vmem_limit = 56 * 1024 * 1024
f32 = jnp.float32
bf16 = jnp.bfloat16


def params():
    return pltpu.CompilerParams(vmem_limit_bytes=vmem_limit)


def iota(shape, dim):
    return lax.broadcasted_iota(jnp.int32, shape, dim)


def edges_kernel(left_ref, right_ref, down_ref, up_ref, west_ref, east_ref, south_ref, north_ref, rows, spread):
    comp = pl.program_id(0)
    count = TILE_X // CZ
    tiles = TILE_Y // count
    lane = iota((TILE_Y, TILE_X), 1)
    mine = lane // CZ == comp
    for ref, which, out_ref in ((left_ref, 0, west_ref), (right_ref, 7, east_ref)):
        for t in range(tiles):
            rows[t : t + 1, :] = ref[0, which : which + 1, t * TILE_X : (t + 1) * TILE_X]
        for r in range(count):
            turned = pltpu.roll(rows[...], lax.rem((comp - r + count) * CZ, TILE_X), 1)
            spread[pl.ds(r, tiles, stride=count), :] = turned

        @pl.when(comp == 0)
        def _():
            out_ref[...] = jnp.zeros_like(out_ref)

        out_ref[...] = jnp.where(mine, spread[...], out_ref[...])
    south_ref[0] = down_ref[0].T[0:CZ]
    north_ref[0] = up_ref[0].T[TILE_X - CZ :]


def tile_edges(field):
    merged = field.shape[2]
    edge = pl.BlockSpec((TILE_Y, TILE_X), lambda c: (0, 0))
    side = pl.BlockSpec((1, CZ, TILE_X), lambda c: (c, 0, 0))
    return pl.pallas_call(
        edges_kernel,
        grid=(3,),
        in_specs=[
            pl.BlockSpec((1, 8, merged), lambda c: (c, 0, 0)),
            pl.BlockSpec((1, 8, merged), lambda c: (c, TILE_X // 8 - 1, 0)),
            pl.BlockSpec((1, TILE_X, 128), lambda c: (c, 0, 0)),
            pl.BlockSpec((1, TILE_X, 128), lambda c: (c, 0, merged // 128 - 1)),
        ],
        out_specs=[edge, edge, side, side],
        out_shape=[jax.ShapeDtypeStruct((TILE_Y, TILE_X), f32)] * 2
        + [jax.ShapeDtypeStruct((3, CZ, TILE_X), f32)] * 2,
        scratch_shapes=[
            pltpu.VMEM((merged // TILE_X, TILE_X), f32),
            pltpu.VMEM((TILE_Y, TILE_X), f32),
        ],
        compiler_params=params(),
        name="tile_edges",
    )(field, field, field, field)


def planes_kernel(field_ref, planes_ref, turned):
    turned[...] = field_ref[0].T
    for z in range(CZ):
        planes_ref[z, 0] = turned[pl.ds(z, TILE_Y, stride=CZ), :]


def to_planes(field, waits):
    count = len(waits)

    def body(field_ref, *refs):
        planes_kernel(field_ref, *refs[count:])

    return pl.pallas_call(
        body,
        grid=(3,),
        in_specs=[pl.BlockSpec((1, TILE_X, TILE_Y * CZ), lambda c: (c, 0, 0))]
        + [pl.BlockSpec(memory_space=pl.ANY)] * count,
        out_specs=pl.BlockSpec((CZ, 1, TILE_Y, TILE_X), lambda c: (0, c, 0, 0)),
        out_shape=jax.ShapeDtypeStruct((CZ, 3, TILE_Y, TILE_X), f32),
        scratch_shapes=[pltpu.VMEM((TILE_Y * CZ, TILE_X), f32)],
        compiler_params=params(),
        name="to_planes",
    )(field, *waits)


def flow_kernel(per, want, flag_ref, u_ref, xlo_ref, xhi_ref, ylo_ref, yhi_ref, *outs):
    outs = list(outs)
    lamb_ref = outs.pop(0) if "lamb" in want else None
    next_ref = outs.pop(0) if "next" in want else None
    group = pl.program_id(0)
    acoustic = flag_ref[0] > 0
    lane = iota((TILE_Y, TILE_X), 1)
    row = iota((TILE_Y, TILE_X), 0)
    turn = lax.rem(TILE_X - group * per, TILE_X)
    xlo = pltpu.roll(xlo_ref[...], turn, 1)
    xhi = pltpu.roll(xhi_ref[...], turn, 1)
    if "edges" in want:
        west_ref, east_ref, south_ref, north_ref = outs

        @pl.when(group == 0)
        def _():
            west_ref[...] = jnp.zeros_like(west_ref)
            east_ref[...] = jnp.zeros_like(east_ref)

        west = west_ref[...]
        east = east_ref[...]
    for i in range(per):
        z = group * per + i
        above = lax.rem(z + 1, CZ)
        below = lax.rem(z + CZ - 1, CZ)
        centre, lap, dx, dy, dz = [], [], [], [], []
        for c in range(3):
            mid = u_ref[z, c]
            up = u_ref[above, c]
            down = u_ref[below, c]
            spot = c * CZ + i
            xm = jnp.where(lane == 0, xlo[:, spot : spot + 1], pltpu.roll(mid, 1, 1))
            xp = jnp.where(
                lane == TILE_X - 1, xhi[:, spot : spot + 1], pltpu.roll(mid, TILE_X - 1, 1)
            )
            ym = jnp.where(row == 0, ylo_ref[c, pl.ds(z, 1), :], pltpu.roll(mid, 1, 0))
            yp = jnp.where(
                row == TILE_Y - 1, yhi_ref[c, pl.ds(z, 1), :], pltpu.roll(mid, TILE_Y - 1, 0)
            )
            centre.append(mid)
            lap.append(xp + xm + yp + ym + up + down - 6.0 * mid)
            dx.append(0.5 * (xp - xm))
            dy.append(0.5 * (yp - ym))
            dz.append(0.5 * (up - down))
        ox = dy[2] - dz[1]
        oy = dz[0] - dx[2]
        oz = dx[1] - dy[0]
        lamb = (
            oy * centre[2] - oz * centre[1],
            oz * centre[0] - ox * centre[2],
            ox * centre[1] - oy * centre[0],
        )
        for c in range(3):
            if "lamb" in want:
                sent = jnp.where(acoustic, centre[c], lamb[c]) if "passed" in want else lamb[c]
                lamb_ref[0, i // CHUNKS, i % CHUNKS, c] = sent
            if "next" in want:
                moved = centre[c] + time_step * (viscosity * lap[c] - lamb[c])
                next_ref[i, c] = moved
            if "edges" in want:
                here = lane == c * CZ + z
                west = jnp.where(here, moved[:, 0:1], west)
                east = jnp.where(here, moved[:, TILE_X - 1 :], east)
                south_ref[c, pl.ds(z, 1), :] = moved[0:1, :]
                north_ref[c, pl.ds(z, 1), :] = moved[TILE_Y - 1 :, :]
    if "edges" in want:
        west_ref[...] = west
        east_ref[...] = east


def flow(flag, planes, halo, waits, groups, want):
    per = CZ // groups
    halves = per // CHUNKS
    edge = pl.BlockSpec((TILE_Y, TILE_X), lambda g: (0, 0))
    side = pl.BlockSpec((3, CZ, TILE_X), lambda g: (0, 0, 0))
    out_specs, out_shape = [], []
    if "lamb" in want:
        out_specs.append(
            pl.BlockSpec((1, halves, CHUNKS, 3, TILE_Y, TILE_X), lambda g: (g, 0, 0, 0, 0, 0))
        )
        out_shape.append(
            jax.ShapeDtypeStruct((groups, halves, CHUNKS, 3, TILE_Y, TILE_X), f32)
        )
    if "next" in want:
        out_specs.append(pl.BlockSpec((per, 3, TILE_Y, TILE_X), lambda g: (g, 0, 0, 0)))
        out_shape.append(jax.ShapeDtypeStruct((CZ, 3, TILE_Y, TILE_X), f32))
    if "edges" in want:
        out_specs += [edge, edge, side, side]
        out_shape += [jax.ShapeDtypeStruct((TILE_Y, TILE_X), f32)] * 2
        out_shape += [jax.ShapeDtypeStruct((3, CZ, TILE_X), f32)] * 2
    count = len(waits)

    def body(*refs):
        flow_kernel(per, want, *refs[:6], *refs[6 + count :])

    return pl.pallas_call(
        body,
        grid=(groups,),
        in_specs=[
            pl.BlockSpec(memory_space=pltpu.SMEM),
            pl.BlockSpec((CZ, 3, TILE_Y, TILE_X), lambda g: (0, 0, 0, 0)),
            edge,
            edge,
            side,
            side,
        ]
        + [pl.BlockSpec(memory_space=pl.ANY)] * count,
        out_specs=out_specs,
        out_shape=out_shape,
        compiler_params=params(),
        name="flow",
    )(flag, planes, *halo, *waits)


def exchange(west, east, south, north):
    def send(value, axis, step):
        count = lax.axis_size(axis)
        return lax.ppermute(
            value, axis, [(i, i + step) for i in range(count) if 0 <= i + step < count]
        )

    return (
        send(east, "gx", 1),
        send(west, "gx", -1),
        send(north, "gy", 1),
        send(south, "gy", -1),
    )


def place_kernel(gx, gy, first, ints_ref, matrix_ref, got_ref, far_ref, near_ref, rows):
    low = ints_ref[1]
    ox = ints_ref[2]
    oy = ints_ref[3]
    full_y = gy * TILE_Y
    lane = iota((full_y, TILE_X), 1)
    row = iota((full_y, TILE_X), 0)

    def tile(h, j, a):
        return jnp.concatenate([got_ref[a * gy + b, h, 0, j] for b in range(gy)], axis=0)

    def work(h, out_ref):
        for a in range(gx):
            rows[0:TILE_Y, a * TILE_X : (a + 1) * TILE_X] = jnp.zeros((TILE_Y, TILE_X), f32)
        vectors = [[tile(h, j, a) for a in range(gx)] for j in range(3)]
        for k in range(3):
            mixed = [
                matrix_ref[k, 0] * vectors[0][a]
                + matrix_ref[k, 1] * vectors[1][a]
                + matrix_ref[k, 2] * vectors[2][a]
                for a in range(gx)
            ]
            before = jnp.zeros((full_y, TILE_X), f32)
            moved = []
            for a in range(gx):
                turned = pltpu.roll(mixed[a], ox, 1)
                moved.append(jnp.where(lane >= ox, turned, before))
                before = turned
            before = jnp.zeros((full_y, TILE_X), f32)
            for a in range(gx):
                turned = pltpu.roll(moved[a], 1, 1)
                pair = moved[a] + jnp.where(lane >= 1, turned, before)
                before = turned
                pair = pair + jnp.where(row >= 1, pltpu.roll(pair, 1, 0), 0.0)
                rows[TILE_Y : TILE_Y + full_y, a * TILE_X : (a + 1) * TILE_X] = pair
            start = TILE_Y - oy
            rest = lax.rem(start, 8)
            window = rows[pl.ds(pl.multiple_of(start - rest, 8), full_y + 8), :]
            window = window.reshape(full_y // 8 + 1, 8, gx * TILE_X)
            window = pltpu.roll(window, lax.rem(8 - rest, 8), 1)
            within = iota((full_y // 8, 8, gx * TILE_X), 1) < 8 - rest
            out_ref[k] = jnp.where(within, window[:-1], window[1:]).reshape(full_y, gx * TILE_X)

    def copy(h, out_ref):
        for k in range(3):
            for a in range(gx):
                out_ref[k, :, a * TILE_X : (a + 1) * TILE_X] = tile(h, k, a)

    if first:

        @pl.when(ints_ref[0] == 0)
        def _():
            work(low, far_ref)
            work(1 - low, near_ref)

        @pl.when(ints_ref[0] > 0)
        def _():
            copy(low, far_ref)
            copy(1 - low, near_ref)
    else:
        work(low, far_ref)
        work(1 - low, near_ref)


def place(ints, matrix, got, chunk, waits, gx, gy, first):
    shape = (3, gy * TILE_Y, gx * TILE_X)
    count = len(waits)

    def body(*refs):
        place_kernel(gx, gy, first, *refs[:3], *refs[3 + count :])

    block = got.shape[:2] + (1,) + got.shape[3:]
    return pl.pallas_call(
        body,
        grid=(1,),
        in_specs=[
            pl.BlockSpec(memory_space=pltpu.SMEM),
            pl.BlockSpec(memory_space=pltpu.SMEM),
            pl.BlockSpec(block, lambda i: (0, 0, chunk, 0, 0, 0)),
        ]
        + [pl.BlockSpec(memory_space=pl.ANY)] * count,
        out_specs=[pl.BlockSpec(shape, lambda i: (0, 0, 0))] * 2,
        out_shape=[jax.ShapeDtypeStruct(shape, f32)] * 2,
        scratch_shapes=[pltpu.VMEM((TILE_Y * (gy + 1) + 8, gx * TILE_X), f32)],
        compiler_params=params(),
        name="place",
    )(ints, matrix, got, *waits)


def tie_kernel(*refs):
    pass


def after(value, earlier):
    anywhere = pl.BlockSpec(memory_space=pl.ANY)
    if not earlier:
        return value
    return pl.pallas_call(
        tie_kernel,
        in_specs=[anywhere] * (1 + len(earlier)),
        out_specs=anywhere,
        out_shape=jax.ShapeDtypeStruct(value.shape, value.dtype),
        input_output_aliases={0: 0},
        name="after",
    )(value, *earlier)


def split(value):
    high = value.astype(bf16)
    return high, (value - high.astype(f32)).astype(bf16)


def dot(a, b):
    return lax.dot_general(a, b, (((1,), (0,)), ((), ())), preferred_element_type=f32)


def x_ops_kernel(pos_ref, mine_ref, first_ref, second_ref, high_ref, low_ref):
    place_x = pos_ref[0]
    core = pos_ref[1]
    rows = mine_ref.shape[2]

    def put(cls, block, where):
        high, low = split(block.T)
        spot = pl.ds(pl.multiple_of(where * rows, rows), rows)
        high_ref[cls, 0, :, spot] = high
        low_ref[cls, 0, :, spot] = low

    for cls in range(NCLASS):
        put(cls, mine_ref[cls, 0], place_x)
    half = NCLASS // 2
    for cls in range(half):
        put(core * half + cls, first_ref[cls, 0], 1 - place_x)
        put((1 - core) * half + cls, second_ref[cls, 0], 1 - place_x)


def y_ops_kernel(pos_ref, b0_ref, b1_ref, b2_ref, b3_ref, high_ref, low_ref):
    me = pos_ref[2]
    rows = b0_ref.shape[2]
    for step, ref in enumerate((b0_ref, b1_ref, b2_ref, b3_ref)):
        spot = pl.ds(pl.multiple_of((me ^ step) * rows, rows), rows)
        for cls in range(NCLASS):
            high, low = split(ref[cls, 0])
            high_ref[cls, 0, spot, :] = high
            low_ref[cls, 0, spot, :] = low


def prepare_ops(kernel, pos, blocks, length, name):
    def spec(block):
        return pl.BlockSpec((block.shape[0], 1) + block.shape[2:], lambda k: (0, k, 0, 0))

    out = jax.ShapeDtypeStruct((NCLASS, 3, length, length), bf16)
    return pl.pallas_call(
        kernel,
        grid=(3,),
        in_specs=[pl.BlockSpec(memory_space=pltpu.SMEM)] + [spec(b) for b in blocks],
        out_specs=[spec(out)] * 2,
        out_shape=[out] * 2,
        compiler_params=params(),
        name=name,
    )(pos, *blocks)


def fetched_ops(x_ops, y_ops, earlier):
    core = lax.rem(lax.axis_index("gy"), 2)
    half = NCLASS // 2
    piece = lax.dynamic_slice_in_dim(x_ops, core * half, half, 0)
    got_x = lax.ppermute(after(piece, earlier), "gx", [(0, 1), (1, 0)])
    got_y = lax.ppermute(after(y_ops, earlier), "gy", [(i, i ^ 2) for i in range(4)])
    return got_x, got_y


def paired_ops(y_ops, got_x, got_y):
    beside = [(i, i ^ 1) for i in range(4)]
    return [lax.ppermute(value, "gy", beside) for value in (got_x, y_ops, got_y)]


def prepared_ops(x_ops, y_ops, fetched, paired):
    got_x, got_y = fetched
    pair_x, pair_y, cross_y = paired
    place_y = lax.axis_index("gy")
    pos = jnp.stack([lax.axis_index("gx"), lax.rem(place_y, 2), place_y]).astype(jnp.int32)
    x_parts = prepare_ops(
        x_ops_kernel, pos, (x_ops, got_x, pair_x), x_ops.shape[3], "x_operators"
    )
    y_parts = prepare_ops(
        y_ops_kernel, pos, (y_ops, pair_y, got_y, cross_y), y_ops.shape[3], "y_operators"
    )
    return x_parts, y_parts


def gathered_classes(x_line_class, y_line_class):
    def rows(value, axis):
        count = lax.axis_size(axis)
        blocks = [value] + [
            lax.ppermute(value, axis, [(i, i ^ step) for i in range(count)])
            for step in range(1, count)
        ]
        order = jnp.arange(count) ^ lax.axis_index(axis)
        return jnp.take(jnp.stack(blocks), order, axis=0)

    return rows(x_line_class, "gy").reshape(-1, 1), rows(y_line_class, "gx").reshape(1, -1)


def sweep_kernel(gx, gy, count, last, xclass_ref, yclass_ref, xh_ref, xl_ref, yh_ref, yl_ref, *refs):
    ins = refs[:count]
    out_ref = refs[count]
    xclass = xclass_ref[...]
    yclass = yclass_ref[...]
    state = ins[0][0]
    for extra in ins[1:]:
        state = state + extra[0]
    high, low = split(state)
    swept = jnp.zeros(state.shape, f32)
    for cls in range(NCLASS):
        part = dot(high, xh_ref[cls, 0]) + dot(low, xh_ref[cls, 0]) + dot(high, xl_ref[cls, 0])
        swept = jnp.where(xclass == cls, part, swept)
    high, low = split(swept)
    final = jnp.zeros(state.shape, f32)
    for cls in range(NCLASS):
        part = dot(yh_ref[cls, 0], high) + dot(yh_ref[cls, 0], low) + dot(yl_ref[cls, 0], high)
        final = jnp.where(yclass == cls, part, final)
    if last:
        for a in range(gx):
            for b in range(gy):
                out_ref[a * gy + b, 0] = final[
                    b * TILE_Y : (b + 1) * TILE_Y, a * TILE_X : (a + 1) * TILE_X
                ]
    else:
        out_ref[0] = final


def sweep(classes, x_parts, y_parts, terms, gx, gy, last):
    full_y, full_x = gy * TILE_Y, gx * TILE_X
    count = len(terms)
    field = pl.BlockSpec((1, full_y, full_x), lambda k: (k, 0, 0))
    xop = pl.BlockSpec((NCLASS, 1, full_x, full_x), lambda k: (0, k, 0, 0))
    yop = pl.BlockSpec((NCLASS, 1, full_y, full_y), lambda k: (0, k, 0, 0))
    if last:
        out_specs = pl.BlockSpec((gx * gy, 1, TILE_Y, TILE_X), lambda k: (0, k, 0, 0))
        out_shape = jax.ShapeDtypeStruct((gx * gy, 3, TILE_Y, TILE_X), f32)
    else:
        out_specs = field
        out_shape = jax.ShapeDtypeStruct((3, full_y, full_x), f32)

    def body(*refs):
        sweep_kernel(gx, gy, count, last, *refs)

    return pl.pallas_call(
        body,
        grid=(3,),
        in_specs=[
            pl.BlockSpec((full_y, 1), lambda k: (0, 0)),
            pl.BlockSpec((1, full_x), lambda k: (0, 0)),
            xop,
            xop,
            yop,
            yop,
        ]
        + [field] * count,
        out_specs=out_specs,
        out_shape=out_shape,
        compiler_params=params(),
        name="sweep",
    )(*classes, *x_parts, *y_parts, *terms)


def output_kernel(flag_ref, u_ref, *refs):
    parts = refs[: 2 * CHUNKS]
    out_ref, turned = refs[2 * CHUNKS :]
    per = CZ // parts[0].shape[0]

    @pl.when(flag_ref[0] == 0)
    def _():
        for z in range(CZ):
            turned[pl.ds(z, TILE_Y, stride=CZ), :] = u_ref[z, 0]

    @pl.when(flag_ref[0] > 0)
    def _():
        for z in range(CZ):
            g, i = divmod(z, per)
            turned[pl.ds(z, TILE_Y, stride=CZ), :] = parts[i][g, 0]

    out_ref[0, 0] = turned[...].T


def to_output(flag, planes, parts):
    part = pl.BlockSpec(parts[0].shape[:1] + (1, TILE_Y, TILE_X), lambda c: (0, c, 0, 0))
    return pl.pallas_call(
        output_kernel,
        grid=(3,),
        in_specs=[
            pl.BlockSpec(memory_space=pltpu.SMEM),
            pl.BlockSpec((CZ, 1, TILE_Y, TILE_X), lambda c: (0, c, 0, 0)),
        ]
        + [part] * (2 * CHUNKS),
        out_specs=pl.BlockSpec((1, 1, TILE_X, TILE_Y * CZ), lambda c: (0, c, 0, 0)),
        out_shape=jax.ShapeDtypeStruct((1, 3, TILE_X, TILE_Y * CZ), f32),
        scratch_shapes=[pltpu.VMEM((TILE_Y * CZ, TILE_X), f32)],
        compiler_params=params(),
        name="to_output",
    )(flag, planes, *parts)


def local(fields, x_ops, y_ops, x_line_class, y_line_class, box_offset, coupling):
    gx, gy = lax.axis_size("gx"), lax.axis_size("gy")
    groups = gx * gy
    sec = lax.axis_index("sec")
    active = (sec == 3).astype(jnp.int32)
    member = jnp.minimum(sec, 2)
    offsets = lax.dynamic_index_in_dim(box_offset, member, 0, keepdims=False)
    matrix = lax.dynamic_index_in_dim(coupling, member, 0, keepdims=False) * (0.25 * time_step)
    matrix = jnp.where(active > 0, jnp.zeros_like(matrix), matrix)
    flag = active.reshape(1)
    lower = (sec < 2).astype(jnp.int32)
    ints = jnp.stack([active, lower, offsets[0], offsets[1]])

    edges = tile_edges(fields[0])
    planes = to_planes(fields[0], [edges[0]])
    halo = [after(value, [planes]) for value in exchange(*edges)]

    (lamb,) = flow(flag, planes, halo, (), groups, ("lamb", "passed"))
    gots = [lax.all_to_all(lamb, ("gx", "gy"), 0, 0)]
    waits = (lamb, ints, matrix)
    planes, *edges = flow(flag, planes, halo, waits, groups, ("next", "edges"))
    halo = exchange(*edges)
    lamb, planes = flow(flag, planes, halo, (), groups, ("lamb", "next"))
    gots[0] = after(gots[0], [lamb])
    gots.append(lax.all_to_all(after(lamb, [gots[0]]), ("gx", "gy"), 0, 0))
    fetched = list(fetched_ops(x_ops, y_ops, [gots[1]]))

    total = STEPS * CHUNKS
    fars, nears, firsts, seconds, thirds, ends = ([None] * total for _ in range(6))
    lines, beside, parts = [], [], []
    token = []

    def placed(n):
        first = n < CHUNKS
        got = gots[n // CHUNKS]
        fars[n], nears[n] = place(ints, matrix, got, n % CHUNKS, token, gx, gy, first)
        firsts[n] = lax.ppermute(fars[n], "sec", [(0, 1), (3, 2)] if first else [(0, 1)])
        return [fars[n]]

    def classes(n):
        lines.extend(gathered_classes(after(x_line_class, token), after(y_line_class, token)))
        return token

    def paired(n):
        fetched[:] = [after(value, token) for value in fetched]
        beside.extend(paired_ops(y_ops, *fetched))
        return token

    def prepared(n):
        brought = [after(value, token) for value in beside]
        parts.extend(prepared_ops(x_ops, y_ops, fetched, brought))
        return [*parts[0], *parts[1]]

    def first_hop(n):
        value = fars[n] + after(firsts[n], token)
        seconds[n] = lax.ppermute(value, "sec", [(1, 2), (2, 1)])
        return [value]

    def second_hop(n):
        value = nears[n] + after(seconds[n], token)
        thirds[n] = lax.ppermute(value, "sec", [(1, 0), (2, 3)])
        return [value]

    def arrived(n):
        thirds[n] = after(thirds[n], token)
        return [thirds[n]]

    def swept(n):
        terms = (nears[n], after(thirds[n], token))
        if n >= CHUNKS:
            terms += (ends[n - CHUNKS],)
        ends[n] = sweep(lines, *parts, terms, gx, gy, n >= total - CHUNKS)
        return [ends[n]]

    order = (
        (placed, 0), (placed, 1), (first_hop, 0), (placed, 2), (first_hop, 1), (second_hop, 0),
        (placed, 3), (first_hop, 2), (paired, 0), (arrived, 0), (second_hop, 1), (classes, 0),
        (prepared, 0), (first_hop, 3), (second_hop, 2), (arrived, 1), (swept, 0),
        (second_hop, 3), (swept, 2), (swept, 1), (swept, 3),
    )
    for work, n in order:
        token = work(n)
    tiles = [lax.all_to_all(value, ("gx", "gy"), 0, 0) for value in ends[-CHUNKS:]]
    brought = [lax.ppermute(value, "sec", [(0, 3)]) for value in tiles]
    return to_output(flag, planes, brought + tiles)


highest = lax.Precision.HIGHEST


def from_root(shard, axis, root):
    mine = lax.axis_index(axis) == root
    return lax.psum(jnp.where(mine, shard, jnp.zeros_like(shard)), axis)


def padded_2(block, sides, width):
    for axis, dim in sides:
        count = lax.axis_size(axis)
        forward = [(i, i + 1) for i in range(count - 1)]
        backward = [(target, source) for source, target in forward]
        low = lax.ppermute(
            lax.slice_in_dim(block, block.shape[dim] - width, None, axis=dim), axis, forward
        )
        high = lax.ppermute(lax.slice_in_dim(block, 0, width, axis=dim), axis, backward)
        block = jnp.concatenate([low, block, high], axis=dim)
    return block


def shifted(value, axis, steps):
    count = lax.axis_size(axis)
    initial, last = (max(0, -steps), min(count, count - steps))
    return lax.ppermute(value, axis, [(source, source + steps) for source in range(initial, last)])


def flow_core(padded):
    centre = padded[:, 1:-1, 1:-1, :]
    ahead_x = padded[:, 2:, 1:-1, :]
    behind_x = padded[:, :-2, 1:-1, :]
    ahead_y = padded[:, 1:-1, 2:, :]
    behind_y = padded[:, 1:-1, :-2, :]
    ahead_z = jnp.roll(centre, -1, axis=3)
    behind_z = jnp.roll(centre, 1, axis=3)
    slope_x = 0.5 * (ahead_x - behind_x)
    slope_y = 0.5 * (ahead_y - behind_y)
    slope_z = 0.5 * (ahead_z - behind_z)
    laplace = ahead_x + behind_x + ahead_y + behind_y + ahead_z + behind_z - 6.0 * centre
    omega_x = slope_y[2] - slope_z[1]
    omega_y = slope_z[0] - slope_x[2]
    omega_z = slope_x[1] - slope_y[0]
    lamb_vector = jnp.stack(
        [
            omega_y * centre[2] - omega_z * centre[1],
            omega_z * centre[0] - omega_x * centre[2],
            omega_x * centre[1] - omega_y * centre[0],
        ]
    )
    updated = centre + time_step * (viscosity * laplace - lamb_vector)
    return (updated, lamb_vector)


def skip_flow(padded):
    centre = padded[:, 1:-1, 1:-1, :]
    return (centre, jnp.zeros_like(centre))


def unchanged(accrued):
    return accrued


def place_source(padded_lamb, offset_x, offset_y, matrix, span_x, span_y, extent_x, extent_y):
    anchor = jnp.zeros((), jnp.int32)
    corner_x = span_x - offset_x - 1
    corner_y = span_y - offset_y - 1
    window = lax.dynamic_slice(
        padded_lamb,
        (anchor, corner_x, corner_y, anchor),
        (3, extent_x + 1, extent_y + 1, padded_lamb.shape[3]),
    )
    averaged = 0.25 * (
        window[:, :-1, :-1] + window[:, 1:, :-1] + window[:, :-1, 1:] + window[:, 1:, 1:]
    )
    return jnp.einsum("kj,jxyz->kxyz", matrix, averaged, precision=highest)


def sweep_lines_x(state, x_ops, select_x, active):
    initial = jnp.zeros(state.shape[1:], jnp.float32)

    def add_piece(running, portion, anchor):

        def work(accrued):
            partial_value = jnp.einsum("ckij,kjl->ckil", x_ops, portion[0], precision=highest)
            return jnp.sum(partial_value * select_x[:, None, None, :], axis=0)

        return lax.cond(active, work, unchanged, running)

    return add_piece(initial, lax.all_gather(state, "gx", axis=2, tiled=True), jnp.int32(0))


def sweep_lines_y(state, y_ops, select_y, active):
    initial = jnp.zeros(state.shape[1:], jnp.float32)

    def add_piece(running, portion, anchor):

        def work(accrued):
            partial_value = jnp.einsum("ckij,kxjz->ckxiz", y_ops, portion[0], precision=highest)
            return jnp.sum(partial_value * select_y[:, None, :, None, None], axis=0)

        return lax.cond(active, work, unchanged, running)

    return add_piece(initial, lax.all_gather(state, "gy", axis=3, tiled=True), jnp.int32(0))


def local_general(fields, x_ops, y_ops, x_line_class, y_line_class, box_offset, coupling):
    sections = lax.axis_size("sec")
    section_index = lax.axis_index("sec")
    active = section_index == sections - 1
    member = jnp.minimum(section_index, sections - 2)
    span_x = fields.shape[2]
    merged = fields.shape[3]
    span_y = merged // CZ
    classes = jnp.arange(NCLASS, dtype=jnp.int32)
    select_y = (classes[:, None] == y_line_class[None, :]).astype(jnp.float32)
    offsets = lax.dynamic_index_in_dim(box_offset, member, 0, keepdims=False)
    matrix = lax.dynamic_index_in_dim(coupling, member, 0, keepdims=False)
    current = fields[0].reshape(3, span_x, span_y, CZ)
    share = CZ // sections
    whole_start = from_root(current, "sec", sections - 1)
    acoustic = lax.dynamic_slice_in_dim(whole_start, section_index * share, share, 3)
    for repeat in range(STEPS):
        padded = padded_2(current, (("gx", 1), ("gy", 2)), 1)
        flowed, lamb_vector = lax.cond(active, skip_flow, flow_core, padded)
        left_tile = shifted(lamb_vector, "gx", 1)
        joined = jnp.concatenate([left_tile, lamb_vector], axis=1)
        lower_tile = shifted(joined, "gy", 1)
        joined = jnp.concatenate([lower_tile, joined], axis=2)
        contribution = place_source(
            joined, offsets[0], offsets[1], matrix, span_x, span_y, span_x, span_y
        )
        source = lax.psum_scatter(contribution, "sec", scatter_dimension=3, tiled=True)
        amplitudes_grid = acoustic + time_step * source
        busy = jnp.asarray(True)
        planes = amplitudes_grid.shape[3]
        merged_now = span_y * planes
        select_x = jnp.broadcast_to(
            (classes[:, None, None] == x_line_class[None, :, None]).astype(jnp.float32),
            (NCLASS, span_y, planes),
        ).reshape(NCLASS, merged_now)
        amplitudes = amplitudes_grid.reshape(1, 3, span_x, merged_now)
        swept_x = sweep_lines_x(amplitudes, x_ops, select_x, busy)
        acoustic = sweep_lines_y(
            swept_x.reshape(1, 3, span_x, span_y, planes), y_ops, select_y, busy
        )
        current = flowed
    whole_end = lax.all_gather(acoustic, "sec", axis=3, tiled=True)
    current = jnp.where(active, whole_end, current)
    return current.reshape(1, 3, span_x, merged)


def whole_planes_fit(mesh):
    sizes = dict(mesh.shape)
    return sizes["sec"] == 4 and sizes["gx"] == 2 and sizes["gy"] == 4


def solution(mesh):
    placed = (
        P("sec", None, "gx", "gy"),
        P(None, None, "gx", None),
        P(None, None, "gy", None),
        P("gy"),
        P("gx"),
        P(),
        P(),
    )
    return jax.shard_map(
        local if whole_planes_fit(mesh) else local_general,
        mesh=mesh,
        in_specs=placed,
        out_specs=P("sec", None, "gx", "gy"),
        check_vma=False,
    )
```

```python
import jax
import jax.numpy as jnp
from jax import lax
from jax.experimental import pallas as pl
from jax.experimental.pallas import tpu as pltpu
from jax.sharding import PartitionSpec as P

CZ = 32
NCLASS = 4
STEPS = 2
TILE_X = 128
TILE_Y = 64
CHUNKS = 2

time_step = 0.2
viscosity = 0.25
vmem_limit = 56 * 1024 * 1024
f32 = jnp.float32
bf16 = jnp.bfloat16


def params():
    return pltpu.CompilerParams(vmem_limit_bytes=vmem_limit)


def iota(shape, dim):
    return lax.broadcasted_iota(jnp.int32, shape, dim)


def edges_kernel(left_ref, right_ref, down_ref, up_ref, west_ref, east_ref, south_ref, north_ref, rows, spread):
    comp = pl.program_id(0)
    count = TILE_X // CZ
    tiles = TILE_Y // count
    lane = iota((TILE_Y, TILE_X), 1)
    mine = lane // CZ == comp
    for ref, which, out_ref in ((left_ref, 0, west_ref), (right_ref, 7, east_ref)):
        for t in range(tiles):
            rows[t : t + 1, :] = ref[0, which : which + 1, t * TILE_X : (t + 1) * TILE_X]
        for r in range(count):
            turned = pltpu.roll(rows[...], lax.rem((comp - r + count) * CZ, TILE_X), 1)
            spread[pl.ds(r, tiles, stride=count), :] = turned

        @pl.when(comp == 0)
        def _():
            out_ref[...] = jnp.zeros_like(out_ref)

        out_ref[...] = jnp.where(mine, spread[...], out_ref[...])
    south_ref[0] = down_ref[0].T[0:CZ]
    north_ref[0] = up_ref[0].T[TILE_X - CZ :]


def tile_edges(field):
    merged = field.shape[2]
    edge = pl.BlockSpec((TILE_Y, TILE_X), lambda c: (0, 0))
    side = pl.BlockSpec((1, CZ, TILE_X), lambda c: (c, 0, 0))
    return pl.pallas_call(
        edges_kernel,
        grid=(3,),
        in_specs=[
            pl.BlockSpec((1, 8, merged), lambda c: (c, 0, 0)),
            pl.BlockSpec((1, 8, merged), lambda c: (c, TILE_X // 8 - 1, 0)),
            pl.BlockSpec((1, TILE_X, 128), lambda c: (c, 0, 0)),
            pl.BlockSpec((1, TILE_X, 128), lambda c: (c, 0, merged // 128 - 1)),
        ],
        out_specs=[edge, edge, side, side],
        out_shape=[jax.ShapeDtypeStruct((TILE_Y, TILE_X), f32)] * 2
        + [jax.ShapeDtypeStruct((3, CZ, TILE_X), f32)] * 2,
        scratch_shapes=[
            pltpu.VMEM((merged // TILE_X, TILE_X), f32),
            pltpu.VMEM((TILE_Y, TILE_X), f32),
        ],
        compiler_params=params(),
        name="tile_edges",
    )(field, field, field, field)


def planes_kernel(field_ref, planes_ref, turned):
    turned[...] = field_ref[0].T
    for z in range(CZ):
        planes_ref[z, 0] = turned[pl.ds(z, TILE_Y, stride=CZ), :]


def to_planes(field, waits):
    count = len(waits)

    def body(field_ref, *refs):
        planes_kernel(field_ref, *refs[count:])

    return pl.pallas_call(
        body,
        grid=(3,),
        in_specs=[pl.BlockSpec((1, TILE_X, TILE_Y * CZ), lambda c: (c, 0, 0))]
        + [pl.BlockSpec(memory_space=pl.ANY)] * count,
        out_specs=pl.BlockSpec((CZ, 1, TILE_Y, TILE_X), lambda c: (0, c, 0, 0)),
        out_shape=jax.ShapeDtypeStruct((CZ, 3, TILE_Y, TILE_X), f32),
        scratch_shapes=[pltpu.VMEM((TILE_Y * CZ, TILE_X), f32)],
        compiler_params=params(),
        name="to_planes",
    )(field, *waits)


def flow_kernel(per, want, flag_ref, u_ref, xlo_ref, xhi_ref, ylo_ref, yhi_ref, *outs):
    outs = list(outs)
    lamb_ref = outs.pop(0) if "lamb" in want else None
    next_ref = outs.pop(0) if "next" in want else None
    group = pl.program_id(0)
    acoustic = flag_ref[0] > 0
    lane = iota((TILE_Y, TILE_X), 1)
    row = iota((TILE_Y, TILE_X), 0)
    turn = lax.rem(TILE_X - group * per, TILE_X)
    xlo = pltpu.roll(xlo_ref[...], turn, 1)
    xhi = pltpu.roll(xhi_ref[...], turn, 1)
    if "edges" in want:
        west_ref, east_ref, south_ref, north_ref = outs

        @pl.when(group == 0)
        def _():
            west_ref[...] = jnp.zeros_like(west_ref)
            east_ref[...] = jnp.zeros_like(east_ref)

        west = west_ref[...]
        east = east_ref[...]
    for i in range(per):
        z = group * per + i
        above = lax.rem(z + 1, CZ)
        below = lax.rem(z + CZ - 1, CZ)
        centre, lap, dx, dy, dz = [], [], [], [], []
        for c in range(3):
            mid = u_ref[z, c]
            up = u_ref[above, c]
            down = u_ref[below, c]
            spot = c * CZ + i
            xm = jnp.where(lane == 0, xlo[:, spot : spot + 1], pltpu.roll(mid, 1, 1))
            xp = jnp.where(
                lane == TILE_X - 1, xhi[:, spot : spot + 1], pltpu.roll(mid, TILE_X - 1, 1)
            )
            ym = jnp.where(row == 0, ylo_ref[c, pl.ds(z, 1), :], pltpu.roll(mid, 1, 0))
            yp = jnp.where(
                row == TILE_Y - 1, yhi_ref[c, pl.ds(z, 1), :], pltpu.roll(mid, TILE_Y - 1, 0)
            )
            centre.append(mid)
            lap.append(xp + xm + yp + ym + up + down - 6.0 * mid)
            dx.append(0.5 * (xp - xm))
            dy.append(0.5 * (yp - ym))
            dz.append(0.5 * (up - down))
        ox = dy[2] - dz[1]
        oy = dz[0] - dx[2]
        oz = dx[1] - dy[0]
        lamb = (
            oy * centre[2] - oz * centre[1],
            oz * centre[0] - ox * centre[2],
            ox * centre[1] - oy * centre[0],
        )
        for c in range(3):
            if "lamb" in want:
                sent = jnp.where(acoustic, centre[c], lamb[c]) if "passed" in want else lamb[c]
                lamb_ref[0, i // CHUNKS, i % CHUNKS, c] = sent
            if "next" in want:
                moved = centre[c] + time_step * (viscosity * lap[c] - lamb[c])
                next_ref[i, c] = moved
            if "edges" in want:
                here = lane == c * CZ + z
                west = jnp.where(here, moved[:, 0:1], west)
                east = jnp.where(here, moved[:, TILE_X - 1 :], east)
                south_ref[c, pl.ds(z, 1), :] = moved[0:1, :]
                north_ref[c, pl.ds(z, 1), :] = moved[TILE_Y - 1 :, :]
    if "edges" in want:
        west_ref[...] = west
        east_ref[...] = east


def flow(flag, planes, halo, waits, groups, want):
    per = CZ // groups
    halves = per // CHUNKS
    edge = pl.BlockSpec((TILE_Y, TILE_X), lambda g: (0, 0))
    side = pl.BlockSpec((3, CZ, TILE_X), lambda g: (0, 0, 0))
    out_specs, out_shape = [], []
    if "lamb" in want:
        out_specs.append(
            pl.BlockSpec((1, halves, CHUNKS, 3, TILE_Y, TILE_X), lambda g: (g, 0, 0, 0, 0, 0))
        )
        out_shape.append(
            jax.ShapeDtypeStruct((groups, halves, CHUNKS, 3, TILE_Y, TILE_X), f32)
        )
    if "next" in want:
        out_specs.append(pl.BlockSpec((per, 3, TILE_Y, TILE_X), lambda g: (g, 0, 0, 0)))
        out_shape.append(jax.ShapeDtypeStruct((CZ, 3, TILE_Y, TILE_X), f32))
    if "edges" in want:
        out_specs += [edge, edge, side, side]
        out_shape += [jax.ShapeDtypeStruct((TILE_Y, TILE_X), f32)] * 2
        out_shape += [jax.ShapeDtypeStruct((3, CZ, TILE_X), f32)] * 2
    count = len(waits)

    def body(*refs):
        flow_kernel(per, want, *refs[:6], *refs[6 + count :])

    return pl.pallas_call(
        body,
        grid=(groups,),
        in_specs=[
            pl.BlockSpec(memory_space=pltpu.SMEM),
            pl.BlockSpec((CZ, 3, TILE_Y, TILE_X), lambda g: (0, 0, 0, 0)),
            edge,
            edge,
            side,
            side,
        ]
        + [pl.BlockSpec(memory_space=pl.ANY)] * count,
        out_specs=out_specs,
        out_shape=out_shape,
        compiler_params=params(),
        name="flow",
    )(flag, planes, *halo, *waits)


def exchange(west, east, south, north):
    def send(value, axis, step):
        count = lax.axis_size(axis)
        return lax.ppermute(
            value, axis, [(i, i + step) for i in range(count) if 0 <= i + step < count]
        )

    return (
        send(east, "gx", 1),
        send(west, "gx", -1),
        send(north, "gy", 1),
        send(south, "gy", -1),
    )


def place_kernel(gx, gy, first, ints_ref, matrix_ref, got_ref, far_ref, near_ref, rows):
    low = ints_ref[1]
    ox = ints_ref[2]
    oy = ints_ref[3]
    full_y = gy * TILE_Y
    lane = iota((full_y, TILE_X), 1)
    row = iota((full_y, TILE_X), 0)

    def tile(h, j, a):
        return jnp.concatenate([got_ref[a * gy + b, h, 0, j] for b in range(gy)], axis=0)

    def work(h, out_ref):
        for a in range(gx):
            rows[0:TILE_Y, a * TILE_X : (a + 1) * TILE_X] = jnp.zeros((TILE_Y, TILE_X), f32)
        vectors = [[tile(h, j, a) for a in range(gx)] for j in range(3)]
        for k in range(3):
            mixed = [
                matrix_ref[k, 0] * vectors[0][a]
                + matrix_ref[k, 1] * vectors[1][a]
                + matrix_ref[k, 2] * vectors[2][a]
                for a in range(gx)
            ]
            before = jnp.zeros((full_y, TILE_X), f32)
            moved = []
            for a in range(gx):
                turned = pltpu.roll(mixed[a], ox, 1)
                moved.append(jnp.where(lane >= ox, turned, before))
                before = turned
            before = jnp.zeros((full_y, TILE_X), f32)
            for a in range(gx):
                turned = pltpu.roll(moved[a], 1, 1)
                pair = moved[a] + jnp.where(lane >= 1, turned, before)
                before = turned
                pair = pair + jnp.where(row >= 1, pltpu.roll(pair, 1, 0), 0.0)
                rows[TILE_Y : TILE_Y + full_y, a * TILE_X : (a + 1) * TILE_X] = pair
            start = TILE_Y - oy
            rest = lax.rem(start, 8)
            window = rows[pl.ds(pl.multiple_of(start - rest, 8), full_y + 8), :]
            window = window.reshape(full_y // 8 + 1, 8, gx * TILE_X)
            window = pltpu.roll(window, lax.rem(8 - rest, 8), 1)
            within = iota((full_y // 8, 8, gx * TILE_X), 1) < 8 - rest
            out_ref[k] = jnp.where(within, window[:-1], window[1:]).reshape(full_y, gx * TILE_X)

    def copy(h, out_ref):
        for k in range(3):
            for a in range(gx):
                out_ref[k, :, a * TILE_X : (a + 1) * TILE_X] = tile(h, k, a)

    if first:

        @pl.when(ints_ref[0] == 0)
        def _():
            work(low, far_ref)
            work(1 - low, near_ref)

        @pl.when(ints_ref[0] > 0)
        def _():
            copy(low, far_ref)
            copy(1 - low, near_ref)
    else:
        work(low, far_ref)
        work(1 - low, near_ref)


def place(ints, matrix, got, chunk, waits, gx, gy, first):
    shape = (3, gy * TILE_Y, gx * TILE_X)
    count = len(waits)

    def body(*refs):
        place_kernel(gx, gy, first, *refs[:3], *refs[3 + count :])

    block = got.shape[:2] + (1,) + got.shape[3:]
    return pl.pallas_call(
        body,
        grid=(1,),
        in_specs=[
            pl.BlockSpec(memory_space=pltpu.SMEM),
            pl.BlockSpec(memory_space=pltpu.SMEM),
            pl.BlockSpec(block, lambda i: (0, 0, chunk, 0, 0, 0)),
        ]
        + [pl.BlockSpec(memory_space=pl.ANY)] * count,
        out_specs=[pl.BlockSpec(shape, lambda i: (0, 0, 0))] * 2,
        out_shape=[jax.ShapeDtypeStruct(shape, f32)] * 2,
        scratch_shapes=[pltpu.VMEM((TILE_Y * (gy + 1) + 8, gx * TILE_X), f32)],
        compiler_params=params(),
        name="place",
    )(ints, matrix, got, *waits)


def tie_kernel(*refs):
    pass


def after(value, earlier):
    anywhere = pl.BlockSpec(memory_space=pl.ANY)
    if not earlier:
        return value
    return pl.pallas_call(
        tie_kernel,
        in_specs=[anywhere] * (1 + len(earlier)),
        out_specs=anywhere,
        out_shape=jax.ShapeDtypeStruct(value.shape, value.dtype),
        input_output_aliases={0: 0},
        name="after",
    )(value, *earlier)


def split(value):
    high = value.astype(bf16)
    return high, (value - high.astype(f32)).astype(bf16)


def dot(a, b):
    return lax.dot_general(a, b, (((1,), (0,)), ((), ())), preferred_element_type=f32)


def x_ops_kernel(pos_ref, mine_ref, first_ref, second_ref, high_ref, low_ref):
    place_x = pos_ref[0]
    core = pos_ref[1]
    rows = mine_ref.shape[2]

    def put(cls, block, where):
        high, low = split(block.T)
        spot = pl.ds(pl.multiple_of(where * rows, rows), rows)
        high_ref[cls, 0, :, spot] = high
        low_ref[cls, 0, :, spot] = low

    for cls in range(NCLASS):
        put(cls, mine_ref[cls, 0], place_x)
    half = NCLASS // 2
    for cls in range(half):
        put(core * half + cls, first_ref[cls, 0], 1 - place_x)
        put((1 - core) * half + cls, second_ref[cls, 0], 1 - place_x)


def y_ops_kernel(pos_ref, b0_ref, b1_ref, b2_ref, b3_ref, high_ref, low_ref):
    me = pos_ref[2]
    rows = b0_ref.shape[2]
    for step, ref in enumerate((b0_ref, b1_ref, b2_ref, b3_ref)):
        spot = pl.ds(pl.multiple_of((me ^ step) * rows, rows), rows)
        for cls in range(NCLASS):
            high, low = split(ref[cls, 0])
            high_ref[cls, 0, spot, :] = high
            low_ref[cls, 0, spot, :] = low


def prepare_ops(kernel, pos, blocks, length, name):
    def spec(block):
        return pl.BlockSpec((block.shape[0], 1) + block.shape[2:], lambda k: (0, k, 0, 0))

    out = jax.ShapeDtypeStruct((NCLASS, 3, length, length), bf16)
    return pl.pallas_call(
        kernel,
        grid=(3,),
        in_specs=[pl.BlockSpec(memory_space=pltpu.SMEM)] + [spec(b) for b in blocks],
        out_specs=[spec(out)] * 2,
        out_shape=[out] * 2,
        compiler_params=params(),
        name=name,
    )(pos, *blocks)


def fetched_ops(x_ops, y_ops, earlier):
    core = lax.rem(lax.axis_index("gy"), 2)
    half = NCLASS // 2
    piece = lax.dynamic_slice_in_dim(x_ops, core * half, half, 0)
    sent = [after(piece, earlier), after(y_ops, earlier)]
    got_x = lax.ppermute(sent[0], "gx", [(0, 1), (1, 0)])
    got_y = lax.ppermute(sent[1], "gy", [(i, i ^ 2) for i in range(4)])
    return [got_x, got_y], sent


def paired_ops(y_ops, got_x, got_y):
    beside = [(i, i ^ 1) for i in range(4)]
    return [lax.ppermute(value, "gy", beside) for value in (got_x, y_ops, got_y)]


def prepared_ops(x_ops, y_ops, fetched, paired):
    got_x, got_y = fetched
    pair_x, pair_y, cross_y = paired
    place_y = lax.axis_index("gy")
    pos = jnp.stack([lax.axis_index("gx"), lax.rem(place_y, 2), place_y]).astype(jnp.int32)
    x_parts = prepare_ops(
        x_ops_kernel, pos, (x_ops, got_x, pair_x), x_ops.shape[3], "x_operators"
    )
    y_parts = prepare_ops(
        y_ops_kernel, pos, (y_ops, pair_y, got_y, cross_y), y_ops.shape[3], "y_operators"
    )
    return x_parts, y_parts


def gathered_classes(x_line_class, y_line_class):
    def rows(value, axis):
        count = lax.axis_size(axis)
        blocks = [value] + [
            lax.ppermute(value, axis, [(i, i ^ step) for i in range(count)])
            for step in range(1, count)
        ]
        order = jnp.arange(count) ^ lax.axis_index(axis)
        return jnp.take(jnp.stack(blocks), order, axis=0)

    return rows(x_line_class, "gy").reshape(-1, 1), rows(y_line_class, "gx").reshape(1, -1)


def sweep_kernel(gx, gy, count, last, xclass_ref, yclass_ref, xh_ref, xl_ref, yh_ref, yl_ref, *refs):
    ins = refs[:count]
    out_ref = refs[count]
    xclass = xclass_ref[...]
    yclass = yclass_ref[...]
    state = ins[0][0]
    for extra in ins[1:]:
        state = state + extra[0]
    high, low = split(state)
    swept = jnp.zeros(state.shape, f32)
    for cls in range(NCLASS):
        part = dot(high, xh_ref[cls, 0]) + dot(low, xh_ref[cls, 0]) + dot(high, xl_ref[cls, 0])
        swept = jnp.where(xclass == cls, part, swept)
    high, low = split(swept)
    final = jnp.zeros(state.shape, f32)
    for cls in range(NCLASS):
        part = dot(yh_ref[cls, 0], high) + dot(yh_ref[cls, 0], low) + dot(yl_ref[cls, 0], high)
        final = jnp.where(yclass == cls, part, final)
    if last:
        for a in range(gx):
            for b in range(gy):
                out_ref[a * gy + b, 0] = final[
                    b * TILE_Y : (b + 1) * TILE_Y, a * TILE_X : (a + 1) * TILE_X
                ]
    else:
        out_ref[0] = final


def sweep(classes, x_parts, y_parts, terms, gx, gy, last):
    full_y, full_x = gy * TILE_Y, gx * TILE_X
    count = len(terms)
    field = pl.BlockSpec((1, full_y, full_x), lambda k: (k, 0, 0))
    xop = pl.BlockSpec((NCLASS, 1, full_x, full_x), lambda k: (0, k, 0, 0))
    yop = pl.BlockSpec((NCLASS, 1, full_y, full_y), lambda k: (0, k, 0, 0))
    if last:
        out_specs = pl.BlockSpec((gx * gy, 1, TILE_Y, TILE_X), lambda k: (0, k, 0, 0))
        out_shape = jax.ShapeDtypeStruct((gx * gy, 3, TILE_Y, TILE_X), f32)
    else:
        out_specs = field
        out_shape = jax.ShapeDtypeStruct((3, full_y, full_x), f32)

    def body(*refs):
        sweep_kernel(gx, gy, count, last, *refs)

    return pl.pallas_call(
        body,
        grid=(3,),
        in_specs=[
            pl.BlockSpec((full_y, 1), lambda k: (0, 0)),
            pl.BlockSpec((1, full_x), lambda k: (0, 0)),
            xop,
            xop,
            yop,
            yop,
        ]
        + [field] * count,
        out_specs=out_specs,
        out_shape=out_shape,
        compiler_params=params(),
        name="sweep",
    )(*classes, *x_parts, *y_parts, *terms)


def output_kernel(flag_ref, u_ref, *refs):
    parts = refs[: 2 * CHUNKS]
    out_ref, turned = refs[2 * CHUNKS :]
    per = CZ // parts[0].shape[0]

    @pl.when(flag_ref[0] == 0)
    def _():
        for z in range(CZ):
            turned[pl.ds(z, TILE_Y, stride=CZ), :] = u_ref[z, 0]

    @pl.when(flag_ref[0] > 0)
    def _():
        for z in range(CZ):
            g, i = divmod(z, per)
            turned[pl.ds(z, TILE_Y, stride=CZ), :] = parts[i][g, 0]

    out_ref[0, 0] = turned[...].T


def to_output(flag, planes, parts):
    part = pl.BlockSpec(parts[0].shape[:1] + (1, TILE_Y, TILE_X), lambda c: (0, c, 0, 0))
    return pl.pallas_call(
        output_kernel,
        grid=(3,),
        in_specs=[
            pl.BlockSpec(memory_space=pltpu.SMEM),
            pl.BlockSpec((CZ, 1, TILE_Y, TILE_X), lambda c: (0, c, 0, 0)),
        ]
        + [part] * (2 * CHUNKS),
        out_specs=pl.BlockSpec((1, 1, TILE_X, TILE_Y * CZ), lambda c: (0, c, 0, 0)),
        out_shape=jax.ShapeDtypeStruct((1, 3, TILE_X, TILE_Y * CZ), f32),
        scratch_shapes=[pltpu.VMEM((TILE_Y * CZ, TILE_X), f32)],
        compiler_params=params(),
        name="to_output",
    )(flag, planes, *parts)


def local(fields, x_ops, y_ops, x_line_class, y_line_class, box_offset, coupling):
    gx, gy = lax.axis_size("gx"), lax.axis_size("gy")
    groups = gx * gy
    sec = lax.axis_index("sec")
    active = (sec == 3).astype(jnp.int32)
    member = jnp.minimum(sec, 2)
    offsets = lax.dynamic_index_in_dim(box_offset, member, 0, keepdims=False)
    matrix = lax.dynamic_index_in_dim(coupling, member, 0, keepdims=False) * (0.25 * time_step)
    matrix = jnp.where(active > 0, jnp.zeros_like(matrix), matrix)
    flag = active.reshape(1)
    lower = (sec < 2).astype(jnp.int32)
    ints = jnp.stack([active, lower, offsets[0], offsets[1]])

    edges = tile_edges(fields[0])
    planes = to_planes(fields[0], [edges[0]])
    halo = [after(value, [planes]) for value in exchange(*edges)]

    (lamb,) = flow(flag, planes, halo, (), groups, ("lamb", "passed"))
    gots = [lax.all_to_all(lamb, ("gx", "gy"), 0, 0)]
    waits = (lamb, ints, matrix)
    planes, *edges = flow(flag, planes, halo, waits, groups, ("next", "edges"))
    halo = exchange(*edges)
    lamb, planes = flow(flag, planes, halo, (), groups, ("lamb", "next"))
    gots[0] = after(gots[0], [lamb])
    gots.append(lax.all_to_all(after(lamb, [gots[0]]), ("gx", "gy"), 0, 0))
    fetched, taken = fetched_ops(x_ops, y_ops, [planes])

    total = STEPS * CHUNKS
    fars, nears, firsts, seconds, thirds, ends = ([None] * total for _ in range(6))
    lines = gathered_classes(x_line_class, y_line_class)
    beside, parts = [], []
    token = list(lines)

    def placed(n):
        first = n < CHUNKS
        got = gots[n // CHUNKS]
        waits = token + taken if n == CHUNKS else token
        fars[n], nears[n] = place(ints, matrix, got, n % CHUNKS, waits, gx, gy, first)
        firsts[n] = lax.ppermute(fars[n], "sec", [(0, 1), (3, 2)] if first else [(0, 1)])
        return [fars[n]]

    def paired(n):
        fetched[:] = [after(value, token) for value in fetched]
        beside.extend(paired_ops(y_ops, *fetched))
        return token

    def prepared(n):
        brought = [after(value, token) for value in beside]
        parts.extend(prepared_ops(x_ops, y_ops, fetched, brought))
        return [*parts[0], *parts[1]]

    def first_hop(n):
        value = fars[n] + after(firsts[n], token)
        seconds[n] = lax.ppermute(value, "sec", [(1, 2), (2, 1)])
        return [value]

    def second_hop(n):
        value = nears[n] + after(seconds[n], token)
        thirds[n] = lax.ppermute(value, "sec", [(1, 0), (2, 3)])
        return [value]

    def arrived(n):
        thirds[n] = after(thirds[n], token)
        return [thirds[n]]

    def swept(n):
        terms = (nears[n], after(thirds[n], token))
        if n >= CHUNKS:
            terms += (ends[n - CHUNKS],)
        ends[n] = sweep(lines, *parts, terms, gx, gy, n >= total - CHUNKS)
        return [ends[n]]

    order = (
        (placed, 0), (placed, 1), (first_hop, 0), (placed, 2), (first_hop, 1), (second_hop, 0),
        (placed, 3), (first_hop, 2), (second_hop, 1), (arrived, 0), (paired, 0), (first_hop, 3),
        (second_hop, 2), (arrived, 1), (prepared, 0), (swept, 0), (second_hop, 3),
        (swept, 2), (swept, 1), (swept, 3),
    )
    for work, n in order:
        token = work(n)
    tiles = [lax.all_to_all(value, ("gx", "gy"), 0, 0) for value in ends[-CHUNKS:]]
    brought = [lax.ppermute(value, "sec", [(0, 3)]) for value in tiles]
    return to_output(flag, planes, brought + tiles)


highest = lax.Precision.HIGHEST


def from_root(shard, axis, root):
    mine = lax.axis_index(axis) == root
    return lax.psum(jnp.where(mine, shard, jnp.zeros_like(shard)), axis)


def padded_2(block, sides, width):
    for axis, dim in sides:
        count = lax.axis_size(axis)
        forward = [(i, i + 1) for i in range(count - 1)]
        backward = [(target, source) for source, target in forward]
        low = lax.ppermute(
            lax.slice_in_dim(block, block.shape[dim] - width, None, axis=dim), axis, forward
        )
        high = lax.ppermute(lax.slice_in_dim(block, 0, width, axis=dim), axis, backward)
        block = jnp.concatenate([low, block, high], axis=dim)
    return block


def shifted(value, axis, steps):
    count = lax.axis_size(axis)
    initial, last = (max(0, -steps), min(count, count - steps))
    return lax.ppermute(value, axis, [(source, source + steps) for source in range(initial, last)])


def flow_core(padded):
    centre = padded[:, 1:-1, 1:-1, :]
    ahead_x = padded[:, 2:, 1:-1, :]
    behind_x = padded[:, :-2, 1:-1, :]
    ahead_y = padded[:, 1:-1, 2:, :]
    behind_y = padded[:, 1:-1, :-2, :]
    ahead_z = jnp.roll(centre, -1, axis=3)
    behind_z = jnp.roll(centre, 1, axis=3)
    slope_x = 0.5 * (ahead_x - behind_x)
    slope_y = 0.5 * (ahead_y - behind_y)
    slope_z = 0.5 * (ahead_z - behind_z)
    laplace = ahead_x + behind_x + ahead_y + behind_y + ahead_z + behind_z - 6.0 * centre
    omega_x = slope_y[2] - slope_z[1]
    omega_y = slope_z[0] - slope_x[2]
    omega_z = slope_x[1] - slope_y[0]
    lamb_vector = jnp.stack(
        [
            omega_y * centre[2] - omega_z * centre[1],
            omega_z * centre[0] - omega_x * centre[2],
            omega_x * centre[1] - omega_y * centre[0],
        ]
    )
    updated = centre + time_step * (viscosity * laplace - lamb_vector)
    return (updated, lamb_vector)


def skip_flow(padded):
    centre = padded[:, 1:-1, 1:-1, :]
    return (centre, jnp.zeros_like(centre))


def unchanged(accrued):
    return accrued


def place_source(padded_lamb, offset_x, offset_y, matrix, span_x, span_y, extent_x, extent_y):
    anchor = jnp.zeros((), jnp.int32)
    corner_x = span_x - offset_x - 1
    corner_y = span_y - offset_y - 1
    window = lax.dynamic_slice(
        padded_lamb,
        (anchor, corner_x, corner_y, anchor),
        (3, extent_x + 1, extent_y + 1, padded_lamb.shape[3]),
    )
    averaged = 0.25 * (
        window[:, :-1, :-1] + window[:, 1:, :-1] + window[:, :-1, 1:] + window[:, 1:, 1:]
    )
    return jnp.einsum("kj,jxyz->kxyz", matrix, averaged, precision=highest)


def sweep_lines_x(state, x_ops, select_x, active):
    initial = jnp.zeros(state.shape[1:], jnp.float32)

    def add_piece(running, portion, anchor):

        def work(accrued):
            partial_value = jnp.einsum("ckij,kjl->ckil", x_ops, portion[0], precision=highest)
            return jnp.sum(partial_value * select_x[:, None, None, :], axis=0)

        return lax.cond(active, work, unchanged, running)

    return add_piece(initial, lax.all_gather(state, "gx", axis=2, tiled=True), jnp.int32(0))


def sweep_lines_y(state, y_ops, select_y, active):
    initial = jnp.zeros(state.shape[1:], jnp.float32)

    def add_piece(running, portion, anchor):

        def work(accrued):
            partial_value = jnp.einsum("ckij,kxjz->ckxiz", y_ops, portion[0], precision=highest)
            return jnp.sum(partial_value * select_y[:, None, :, None, None], axis=0)

        return lax.cond(active, work, unchanged, running)

    return add_piece(initial, lax.all_gather(state, "gy", axis=3, tiled=True), jnp.int32(0))


def local_general(fields, x_ops, y_ops, x_line_class, y_line_class, box_offset, coupling):
    sections = lax.axis_size("sec")
    section_index = lax.axis_index("sec")
    active = section_index == sections - 1
    member = jnp.minimum(section_index, sections - 2)
    span_x = fields.shape[2]
    merged = fields.shape[3]
    span_y = merged // CZ
    classes = jnp.arange(NCLASS, dtype=jnp.int32)
    select_y = (classes[:, None] == y_line_class[None, :]).astype(jnp.float32)
    offsets = lax.dynamic_index_in_dim(box_offset, member, 0, keepdims=False)
    matrix = lax.dynamic_index_in_dim(coupling, member, 0, keepdims=False)
    current = fields[0].reshape(3, span_x, span_y, CZ)
    share = CZ // sections
    whole_start = from_root(current, "sec", sections - 1)
    acoustic = lax.dynamic_slice_in_dim(whole_start, section_index * share, share, 3)
    for repeat in range(STEPS):
        padded = padded_2(current, (("gx", 1), ("gy", 2)), 1)
        flowed, lamb_vector = lax.cond(active, skip_flow, flow_core, padded)
        left_tile = shifted(lamb_vector, "gx", 1)
        joined = jnp.concatenate([left_tile, lamb_vector], axis=1)
        lower_tile = shifted(joined, "gy", 1)
        joined = jnp.concatenate([lower_tile, joined], axis=2)
        contribution = place_source(
            joined, offsets[0], offsets[1], matrix, span_x, span_y, span_x, span_y
        )
        source = lax.psum_scatter(contribution, "sec", scatter_dimension=3, tiled=True)
        amplitudes_grid = acoustic + time_step * source
        busy = jnp.asarray(True)
        planes = amplitudes_grid.shape[3]
        merged_now = span_y * planes
        select_x = jnp.broadcast_to(
            (classes[:, None, None] == x_line_class[None, :, None]).astype(jnp.float32),
            (NCLASS, span_y, planes),
        ).reshape(NCLASS, merged_now)
        amplitudes = amplitudes_grid.reshape(1, 3, span_x, merged_now)
        swept_x = sweep_lines_x(amplitudes, x_ops, select_x, busy)
        acoustic = sweep_lines_y(
            swept_x.reshape(1, 3, span_x, span_y, planes), y_ops, select_y, busy
        )
        current = flowed
    whole_end = lax.all_gather(acoustic, "sec", axis=3, tiled=True)
    current = jnp.where(active, whole_end, current)
    return current.reshape(1, 3, span_x, merged)


def whole_planes_fit(mesh):
    sizes = dict(mesh.shape)
    return sizes["sec"] == 4 and sizes["gx"] == 2 and sizes["gy"] == 4


def solution(mesh):
    placed = (
        P("sec", None, "gx", "gy"),
        P(None, None, "gx", None),
        P(None, None, "gy", None),
        P("gy"),
        P("gx"),
        P(),
        P(),
    )
    return jax.shard_map(
        local if whole_planes_fit(mesh) else local_general,
        mesh=mesh,
        in_specs=placed,
        out_specs=P("sec", None, "gx", "gy"),
        check_vma=False,
    )
```

```python
import jax
import jax.numpy as jnp
from jax import lax
from jax.experimental import pallas as pl
from jax.experimental.pallas import tpu as pltpu
from jax.sharding import PartitionSpec as P

CZ = 32
NCLASS = 4
STEPS = 2
TILE_X = 128
TILE_Y = 64
CHUNKS = 2

time_step = 0.2
viscosity = 0.25
vmem_limit = 56 * 1024 * 1024
f32 = jnp.float32
bf16 = jnp.bfloat16


def params():
    return pltpu.CompilerParams(vmem_limit_bytes=vmem_limit)


def iota(shape, dim):
    return lax.broadcasted_iota(jnp.int32, shape, dim)


def edges_kernel(left_ref, right_ref, down_ref, up_ref, west_ref, east_ref, south_ref, north_ref, rows, spread):
    comp = pl.program_id(0)
    count = TILE_X // CZ
    tiles = TILE_Y // count
    lane = iota((TILE_Y, TILE_X), 1)
    mine = lane // CZ == comp
    for ref, which, out_ref in ((left_ref, 0, west_ref), (right_ref, 7, east_ref)):
        for t in range(tiles):
            rows[t : t + 1, :] = ref[0, which : which + 1, t * TILE_X : (t + 1) * TILE_X]
        for r in range(count):
            turned = pltpu.roll(rows[...], lax.rem((comp - r + count) * CZ, TILE_X), 1)
            spread[pl.ds(r, tiles, stride=count), :] = turned

        @pl.when(comp == 0)
        def _():
            out_ref[...] = jnp.zeros_like(out_ref)

        out_ref[...] = jnp.where(mine, spread[...], out_ref[...])
    south_ref[0] = down_ref[0].T[0:CZ]
    north_ref[0] = up_ref[0].T[TILE_X - CZ :]


def tile_edges(field):
    merged = field.shape[2]
    edge = pl.BlockSpec((TILE_Y, TILE_X), lambda c: (0, 0))
    side = pl.BlockSpec((1, CZ, TILE_X), lambda c: (c, 0, 0))
    return pl.pallas_call(
        edges_kernel,
        grid=(3,),
        in_specs=[
            pl.BlockSpec((1, 8, merged), lambda c: (c, 0, 0)),
            pl.BlockSpec((1, 8, merged), lambda c: (c, TILE_X // 8 - 1, 0)),
            pl.BlockSpec((1, TILE_X, 128), lambda c: (c, 0, 0)),
            pl.BlockSpec((1, TILE_X, 128), lambda c: (c, 0, merged // 128 - 1)),
        ],
        out_specs=[edge, edge, side, side],
        out_shape=[jax.ShapeDtypeStruct((TILE_Y, TILE_X), f32)] * 2
        + [jax.ShapeDtypeStruct((3, CZ, TILE_X), f32)] * 2,
        scratch_shapes=[
            pltpu.VMEM((merged // TILE_X, TILE_X), f32),
            pltpu.VMEM((TILE_Y, TILE_X), f32),
        ],
        compiler_params=params(),
        name="tile_edges",
    )(field, field, field, field)


def planes_kernel(field_ref, planes_ref, turned):
    turned[...] = field_ref[0].T
    for z in range(CZ):
        planes_ref[z, 0] = turned[pl.ds(z, TILE_Y, stride=CZ), :]


def to_planes(field, waits):
    count = len(waits)

    def body(field_ref, *refs):
        planes_kernel(field_ref, *refs[count:])

    return pl.pallas_call(
        body,
        grid=(3,),
        in_specs=[pl.BlockSpec((1, TILE_X, TILE_Y * CZ), lambda c: (c, 0, 0))]
        + [pl.BlockSpec(memory_space=pl.ANY)] * count,
        out_specs=pl.BlockSpec((CZ, 1, TILE_Y, TILE_X), lambda c: (0, c, 0, 0)),
        out_shape=jax.ShapeDtypeStruct((CZ, 3, TILE_Y, TILE_X), f32),
        scratch_shapes=[pltpu.VMEM((TILE_Y * CZ, TILE_X), f32)],
        compiler_params=params(),
        name="to_planes",
    )(field, *waits)


def flow_kernel(per, want, flag_ref, u_ref, xlo_ref, xhi_ref, ylo_ref, yhi_ref, *outs):
    outs = list(outs)
    lamb_ref = outs.pop(0) if "lamb" in want else None
    next_ref = outs.pop(0) if "next" in want else None
    group = pl.program_id(0)
    acoustic = flag_ref[0] > 0
    lane = iota((TILE_Y, TILE_X), 1)
    row = iota((TILE_Y, TILE_X), 0)
    turn = lax.rem(TILE_X - group * per, TILE_X)
    xlo = pltpu.roll(xlo_ref[...], turn, 1)
    xhi = pltpu.roll(xhi_ref[...], turn, 1)
    if "edges" in want:
        west_ref, east_ref, south_ref, north_ref = outs

        @pl.when(group == 0)
        def _():
            west_ref[...] = jnp.zeros_like(west_ref)
            east_ref[...] = jnp.zeros_like(east_ref)

        west = west_ref[...]
        east = east_ref[...]
    for i in range(per):
        z = group * per + i
        above = lax.rem(z + 1, CZ)
        below = lax.rem(z + CZ - 1, CZ)
        centre, lap, dx, dy, dz = [], [], [], [], []
        for c in range(3):
            mid = u_ref[z, c]
            up = u_ref[above, c]
            down = u_ref[below, c]
            spot = c * CZ + i
            xm = jnp.where(lane == 0, xlo[:, spot : spot + 1], pltpu.roll(mid, 1, 1))
            xp = jnp.where(
                lane == TILE_X - 1, xhi[:, spot : spot + 1], pltpu.roll(mid, TILE_X - 1, 1)
            )
            ym = jnp.where(row == 0, ylo_ref[c, pl.ds(z, 1), :], pltpu.roll(mid, 1, 0))
            yp = jnp.where(
                row == TILE_Y - 1, yhi_ref[c, pl.ds(z, 1), :], pltpu.roll(mid, TILE_Y - 1, 0)
            )
            centre.append(mid)
            lap.append(xp + xm + yp + ym + up + down - 6.0 * mid)
            dx.append(0.5 * (xp - xm))
            dy.append(0.5 * (yp - ym))
            dz.append(0.5 * (up - down))
        ox = dy[2] - dz[1]
        oy = dz[0] - dx[2]
        oz = dx[1] - dy[0]
        lamb = (
            oy * centre[2] - oz * centre[1],
            oz * centre[0] - ox * centre[2],
            ox * centre[1] - oy * centre[0],
        )
        for c in range(3):
            if "lamb" in want:
                sent = jnp.where(acoustic, centre[c], lamb[c]) if "passed" in want else lamb[c]
                lamb_ref[0, i // CHUNKS, i % CHUNKS, c] = sent
            if "next" in want:
                moved = centre[c] + time_step * (viscosity * lap[c] - lamb[c])
                next_ref[i, c] = moved
            if "edges" in want:
                here = lane == c * CZ + z
                west = jnp.where(here, moved[:, 0:1], west)
                east = jnp.where(here, moved[:, TILE_X - 1 :], east)
                south_ref[c, pl.ds(z, 1), :] = moved[0:1, :]
                north_ref[c, pl.ds(z, 1), :] = moved[TILE_Y - 1 :, :]
    if "edges" in want:
        west_ref[...] = west
        east_ref[...] = east


def flow(flag, planes, halo, waits, groups, want):
    per = CZ // groups
    halves = per // CHUNKS
    edge = pl.BlockSpec((TILE_Y, TILE_X), lambda g: (0, 0))
    side = pl.BlockSpec((3, CZ, TILE_X), lambda g: (0, 0, 0))
    out_specs, out_shape = [], []
    if "lamb" in want:
        out_specs.append(
            pl.BlockSpec((1, halves, CHUNKS, 3, TILE_Y, TILE_X), lambda g: (g, 0, 0, 0, 0, 0))
        )
        out_shape.append(
            jax.ShapeDtypeStruct((groups, halves, CHUNKS, 3, TILE_Y, TILE_X), f32)
        )
    if "next" in want:
        out_specs.append(pl.BlockSpec((per, 3, TILE_Y, TILE_X), lambda g: (g, 0, 0, 0)))
        out_shape.append(jax.ShapeDtypeStruct((CZ, 3, TILE_Y, TILE_X), f32))
    if "edges" in want:
        out_specs += [edge, edge, side, side]
        out_shape += [jax.ShapeDtypeStruct((TILE_Y, TILE_X), f32)] * 2
        out_shape += [jax.ShapeDtypeStruct((3, CZ, TILE_X), f32)] * 2
    count = len(waits)

    def body(*refs):
        flow_kernel(per, want, *refs[:6], *refs[6 + count :])

    return pl.pallas_call(
        body,
        grid=(groups,),
        in_specs=[
            pl.BlockSpec(memory_space=pltpu.SMEM),
            pl.BlockSpec((CZ, 3, TILE_Y, TILE_X), lambda g: (0, 0, 0, 0)),
            edge,
            edge,
            side,
            side,
        ]
        + [pl.BlockSpec(memory_space=pl.ANY)] * count,
        out_specs=out_specs,
        out_shape=out_shape,
        compiler_params=params(),
        name="flow",
    )(flag, planes, *halo, *waits)


def exchange(west, east, south, north):
    def send(value, axis, step):
        count = lax.axis_size(axis)
        return lax.ppermute(
            value, axis, [(i, i + step) for i in range(count) if 0 <= i + step < count]
        )

    return (
        send(east, "gx", 1),
        send(west, "gx", -1),
        send(north, "gy", 1),
        send(south, "gy", -1),
    )


def place_kernel(gx, gy, first, ints_ref, matrix_ref, got_ref, far_ref, near_ref, rows):
    low = ints_ref[1]
    ox = ints_ref[2]
    oy = ints_ref[3]
    full_y = gy * TILE_Y
    lane = iota((full_y, TILE_X), 1)
    row = iota((full_y, TILE_X), 0)

    def tile(h, j, a):
        return jnp.concatenate([got_ref[a * gy + b, h, 0, j] for b in range(gy)], axis=0)

    def work(h, out_ref):
        for a in range(gx):
            rows[0:TILE_Y, a * TILE_X : (a + 1) * TILE_X] = jnp.zeros((TILE_Y, TILE_X), f32)
        vectors = [[tile(h, j, a) for a in range(gx)] for j in range(3)]
        for k in range(3):
            mixed = [
                matrix_ref[k, 0] * vectors[0][a]
                + matrix_ref[k, 1] * vectors[1][a]
                + matrix_ref[k, 2] * vectors[2][a]
                for a in range(gx)
            ]
            before = jnp.zeros((full_y, TILE_X), f32)
            moved = []
            for a in range(gx):
                turned = pltpu.roll(mixed[a], ox, 1)
                moved.append(jnp.where(lane >= ox, turned, before))
                before = turned
            before = jnp.zeros((full_y, TILE_X), f32)
            for a in range(gx):
                turned = pltpu.roll(moved[a], 1, 1)
                pair = moved[a] + jnp.where(lane >= 1, turned, before)
                before = turned
                pair = pair + jnp.where(row >= 1, pltpu.roll(pair, 1, 0), 0.0)
                rows[TILE_Y : TILE_Y + full_y, a * TILE_X : (a + 1) * TILE_X] = pair
            start = TILE_Y - oy
            rest = lax.rem(start, 8)
            window = rows[pl.ds(pl.multiple_of(start - rest, 8), full_y + 8), :]
            window = window.reshape(full_y // 8 + 1, 8, gx * TILE_X)
            window = pltpu.roll(window, lax.rem(8 - rest, 8), 1)
            within = iota((full_y // 8, 8, gx * TILE_X), 1) < 8 - rest
            out_ref[k] = jnp.where(within, window[:-1], window[1:]).reshape(full_y, gx * TILE_X)

    def copy(h, out_ref):
        for k in range(3):
            for a in range(gx):
                out_ref[k, :, a * TILE_X : (a + 1) * TILE_X] = tile(h, k, a)

    if first:

        @pl.when(ints_ref[0] == 0)
        def _():
            work(low, far_ref)
            work(1 - low, near_ref)

        @pl.when(ints_ref[0] > 0)
        def _():
            copy(low, far_ref)
            copy(1 - low, near_ref)
    else:
        work(low, far_ref)
        work(1 - low, near_ref)


def place(ints, matrix, got, chunk, waits, gx, gy, first):
    shape = (3, gy * TILE_Y, gx * TILE_X)
    count = len(waits)

    def body(*refs):
        place_kernel(gx, gy, first, *refs[:3], *refs[3 + count :])

    block = got.shape[:2] + (1,) + got.shape[3:]
    return pl.pallas_call(
        body,
        grid=(1,),
        in_specs=[
            pl.BlockSpec(memory_space=pltpu.SMEM),
            pl.BlockSpec(memory_space=pltpu.SMEM),
            pl.BlockSpec(block, lambda i: (0, 0, chunk, 0, 0, 0)),
        ]
        + [pl.BlockSpec(memory_space=pl.ANY)] * count,
        out_specs=[pl.BlockSpec(shape, lambda i: (0, 0, 0))] * 2,
        out_shape=[jax.ShapeDtypeStruct(shape, f32)] * 2,
        scratch_shapes=[pltpu.VMEM((TILE_Y * (gy + 1) + 8, gx * TILE_X), f32)],
        compiler_params=params(),
        name="place",
    )(ints, matrix, got, *waits)


def tie_kernel(*refs):
    pass


def after(value, earlier):
    anywhere = pl.BlockSpec(memory_space=pl.ANY)
    if not earlier:
        return value
    return pl.pallas_call(
        tie_kernel,
        in_specs=[anywhere] * (1 + len(earlier)),
        out_specs=anywhere,
        out_shape=jax.ShapeDtypeStruct(value.shape, value.dtype),
        input_output_aliases={0: 0},
        name="after",
    )(value, *earlier)


def split(value):
    high = value.astype(bf16)
    return high, (value - high.astype(f32)).astype(bf16)


def dot(a, b):
    return lax.dot_general(a, b, (((1,), (0,)), ((), ())), preferred_element_type=f32)


def x_ops_kernel(pos_ref, mine_ref, first_ref, second_ref, high_ref, low_ref):
    place_x = pos_ref[0]
    core = pos_ref[1]
    rows = mine_ref.shape[2]

    def put(cls, block, where):
        high, low = split(block.T)
        spot = pl.ds(pl.multiple_of(where * rows, rows), rows)
        high_ref[cls, 0, :, spot] = high
        low_ref[cls, 0, :, spot] = low

    for cls in range(NCLASS):
        put(cls, mine_ref[cls, 0], place_x)
    half = NCLASS // 2
    for cls in range(half):
        put(core * half + cls, first_ref[cls, 0], 1 - place_x)
        put((1 - core) * half + cls, second_ref[cls, 0], 1 - place_x)


def y_ops_kernel(pos_ref, b0_ref, b1_ref, b2_ref, b3_ref, high_ref, low_ref):
    me = pos_ref[2]
    rows = b0_ref.shape[2]
    for step, ref in enumerate((b0_ref, b1_ref, b2_ref, b3_ref)):
        spot = pl.ds(pl.multiple_of((me ^ step) * rows, rows), rows)
        for cls in range(NCLASS):
            high, low = split(ref[cls, 0])
            high_ref[cls, 0, spot, :] = high
            low_ref[cls, 0, spot, :] = low


def ops_kernel(pos_ref, *refs):
    x_ops_kernel(pos_ref, *refs[:3], *refs[7:9])
    y_ops_kernel(pos_ref, *refs[3:7], *refs[9:])


def prepare_ops(pos, x_blocks, y_blocks):
    def spec(block):
        return pl.BlockSpec((block.shape[0], 1) + block.shape[2:], lambda k: (0, k, 0, 0))

    blocks = (*x_blocks, *y_blocks)
    out = [
        jax.ShapeDtypeStruct((NCLASS, 3, length, length), bf16)
        for length in (x_blocks[0].shape[3], y_blocks[0].shape[3])
        for _ in range(2)
    ]
    parts = pl.pallas_call(
        ops_kernel,
        grid=(3,),
        in_specs=[pl.BlockSpec(memory_space=pltpu.SMEM)] + [spec(b) for b in blocks],
        out_specs=[spec(o) for o in out],
        out_shape=out,
        compiler_params=params(),
        name="operators",
    )(pos, *blocks)
    return parts[:2], parts[2:]


def fetched_ops(x_ops, y_ops, earlier):
    core = lax.rem(lax.axis_index("gy"), 2)
    half = NCLASS // 2
    piece = lax.dynamic_slice_in_dim(x_ops, core * half, half, 0)
    sent = [after(piece, earlier), after(y_ops, earlier)]
    got_x = lax.ppermute(sent[0], "gx", [(0, 1), (1, 0)])
    got_y = lax.ppermute(sent[1], "gy", [(i, i ^ 2) for i in range(4)])
    return [got_x, got_y], sent


def paired_ops(y_ops, got_x, got_y):
    beside = [(i, i ^ 1) for i in range(4)]
    return [lax.ppermute(value, "gy", beside) for value in (got_x, y_ops, got_y)]


def prepared_ops(x_ops, y_ops, fetched, paired):
    got_x, got_y = fetched
    pair_x, pair_y, cross_y = paired
    place_y = lax.axis_index("gy")
    pos = jnp.stack([lax.axis_index("gx"), lax.rem(place_y, 2), place_y]).astype(jnp.int32)
    return prepare_ops(pos, (x_ops, got_x, pair_x), (y_ops, pair_y, got_y, cross_y))


def gathered_classes(x_line_class, y_line_class):
    def rows(value, axis):
        count = lax.axis_size(axis)
        blocks = [value] + [
            lax.ppermute(value, axis, [(i, i ^ step) for i in range(count)])
            for step in range(1, count)
        ]
        order = jnp.arange(count) ^ lax.axis_index(axis)
        return jnp.take(jnp.stack(blocks), order, axis=0)

    return rows(x_line_class, "gy").reshape(-1, 1), rows(y_line_class, "gx").reshape(1, -1)


def sweep_kernel(gx, gy, count, last, xclass_ref, yclass_ref, xh_ref, xl_ref, yh_ref, yl_ref, *refs):
    ins = refs[:count]
    out_ref = refs[count]
    xclass = xclass_ref[...]
    yclass = yclass_ref[...]
    state = ins[0][0]
    for extra in ins[1:]:
        state = state + extra[0]
    high, low = split(state)
    swept = jnp.zeros(state.shape, f32)
    for cls in range(NCLASS):
        part = dot(high, xh_ref[cls, 0]) + dot(low, xh_ref[cls, 0]) + dot(high, xl_ref[cls, 0])
        swept = jnp.where(xclass == cls, part, swept)
    high, low = split(swept)
    final = jnp.zeros(state.shape, f32)
    for cls in range(NCLASS):
        part = dot(yh_ref[cls, 0], high) + dot(yh_ref[cls, 0], low) + dot(yl_ref[cls, 0], high)
        final = jnp.where(yclass == cls, part, final)
    if last:
        for a in range(gx):
            for b in range(gy):
                out_ref[a * gy + b, 0] = final[
                    b * TILE_Y : (b + 1) * TILE_Y, a * TILE_X : (a + 1) * TILE_X
                ]
    else:
        out_ref[0] = final


def sweep(classes, x_parts, y_parts, terms, gx, gy, last):
    full_y, full_x = gy * TILE_Y, gx * TILE_X
    count = len(terms)
    field = pl.BlockSpec((1, full_y, full_x), lambda k: (k, 0, 0))
    xop = pl.BlockSpec((NCLASS, 1, full_x, full_x), lambda k: (0, k, 0, 0))
    yop = pl.BlockSpec((NCLASS, 1, full_y, full_y), lambda k: (0, k, 0, 0))
    if last:
        out_specs = pl.BlockSpec((gx * gy, 1, TILE_Y, TILE_X), lambda k: (0, k, 0, 0))
        out_shape = jax.ShapeDtypeStruct((gx * gy, 3, TILE_Y, TILE_X), f32)
    else:
        out_specs = field
        out_shape = jax.ShapeDtypeStruct((3, full_y, full_x), f32)

    def body(*refs):
        sweep_kernel(gx, gy, count, last, *refs)

    return pl.pallas_call(
        body,
        grid=(3,),
        in_specs=[
            pl.BlockSpec((full_y, 1), lambda k: (0, 0)),
            pl.BlockSpec((1, full_x), lambda k: (0, 0)),
            xop,
            xop,
            yop,
            yop,
        ]
        + [field] * count,
        out_specs=out_specs,
        out_shape=out_shape,
        compiler_params=params(),
        name="sweep",
    )(*classes, *x_parts, *y_parts, *terms)


def output_kernel(flag_ref, u_ref, *refs):
    parts = refs[: 2 * CHUNKS]
    out_ref, turned = refs[2 * CHUNKS :]
    per = CZ // parts[0].shape[0]

    @pl.when(flag_ref[0] == 0)
    def _():
        for z in range(CZ):
            turned[pl.ds(z, TILE_Y, stride=CZ), :] = u_ref[z, 0]

    @pl.when(flag_ref[0] > 0)
    def _():
        for z in range(CZ):
            g, i = divmod(z, per)
            turned[pl.ds(z, TILE_Y, stride=CZ), :] = parts[i][g, 0]

    out_ref[0, 0] = turned[...].T


def to_output(flag, planes, parts):
    part = pl.BlockSpec(parts[0].shape[:1] + (1, TILE_Y, TILE_X), lambda c: (0, c, 0, 0))
    return pl.pallas_call(
        output_kernel,
        grid=(3,),
        in_specs=[
            pl.BlockSpec(memory_space=pltpu.SMEM),
            pl.BlockSpec((CZ, 1, TILE_Y, TILE_X), lambda c: (0, c, 0, 0)),
        ]
        + [part] * (2 * CHUNKS),
        out_specs=pl.BlockSpec((1, 1, TILE_X, TILE_Y * CZ), lambda c: (0, c, 0, 0)),
        out_shape=jax.ShapeDtypeStruct((1, 3, TILE_X, TILE_Y * CZ), f32),
        scratch_shapes=[pltpu.VMEM((TILE_Y * CZ, TILE_X), f32)],
        compiler_params=params(),
        name="to_output",
    )(flag, planes, *parts)


def local(fields, x_ops, y_ops, x_line_class, y_line_class, box_offset, coupling):
    gx, gy = lax.axis_size("gx"), lax.axis_size("gy")
    groups = gx * gy
    sec = lax.axis_index("sec")
    active = (sec == 3).astype(jnp.int32)
    member = jnp.minimum(sec, 2)
    offsets = lax.dynamic_index_in_dim(box_offset, member, 0, keepdims=False)
    matrix = lax.dynamic_index_in_dim(coupling, member, 0, keepdims=False) * (0.25 * time_step)
    matrix = jnp.where(active > 0, jnp.zeros_like(matrix), matrix)
    flag = active.reshape(1)
    lower = (sec < 2).astype(jnp.int32)
    ints = jnp.stack([active, lower, offsets[0], offsets[1]])

    edges = tile_edges(fields[0])
    planes = to_planes(fields[0], [edges[0]])
    halo = [after(value, [planes]) for value in exchange(*edges)]

    (lamb,) = flow(flag, planes, halo, (), groups, ("lamb", "passed"))
    gots = [lax.all_to_all(lamb, ("gx", "gy"), 0, 0)]
    waits = (lamb, ints, matrix)
    planes, *edges = flow(flag, planes, halo, waits, groups, ("next", "edges"))
    halo = exchange(*edges)
    lamb, planes = flow(flag, planes, halo, (), groups, ("lamb", "next"))
    gots[0] = after(gots[0], [lamb])
    gots.append(lax.all_to_all(after(lamb, [gots[0]]), ("gx", "gy"), 0, 0))
    fetched, taken = fetched_ops(x_ops, y_ops, [planes])

    total = STEPS * CHUNKS
    fars, nears, firsts, seconds, thirds, ends = ([None] * total for _ in range(6))
    lines = gathered_classes(x_line_class, y_line_class)
    beside, parts = [], []
    token = list(lines)

    def placed(n):
        first = n < CHUNKS
        got = gots[n // CHUNKS]
        waits = token + taken if n == CHUNKS else token
        fars[n], nears[n] = place(ints, matrix, got, n % CHUNKS, waits, gx, gy, first)
        firsts[n] = lax.ppermute(fars[n], "sec", [(0, 1), (3, 2)] if first else [(0, 1)])
        return [fars[n]]

    def paired(n):
        fetched[:] = [after(value, token) for value in fetched]
        beside.extend(paired_ops(y_ops, *fetched))
        return token

    def prepared(n):
        brought = [after(value, token) for value in beside]
        parts.extend(prepared_ops(x_ops, y_ops, fetched, brought))
        return [*parts[0], *parts[1]]

    def first_hop(n):
        value = fars[n] + after(firsts[n], token)
        seconds[n] = lax.ppermute(value, "sec", [(1, 2), (2, 1)])
        return [value]

    def second_hop(n):
        value = nears[n] + after(seconds[n], token)
        thirds[n] = lax.ppermute(value, "sec", [(1, 0), (2, 3)])
        return [value]

    def arrived(n):
        thirds[n] = after(thirds[n], token)
        return [thirds[n]]

    def swept(n):
        terms = (nears[n], after(thirds[n], token))
        if n >= CHUNKS:
            terms += (ends[n - CHUNKS],)
        ends[n] = sweep(lines, *parts, terms, gx, gy, n >= total - CHUNKS)
        return [ends[n]]

    order = (
        (placed, 0), (placed, 1), (first_hop, 0), (placed, 2), (first_hop, 1), (second_hop, 0),
        (placed, 3), (first_hop, 2), (second_hop, 1), (arrived, 0), (paired, 0), (first_hop, 3),
        (second_hop, 2), (arrived, 1), (prepared, 0), (swept, 0), (second_hop, 3),
        (swept, 2), (swept, 1), (swept, 3),
    )
    for work, n in order:
        token = work(n)
    tiles = [lax.all_to_all(value, ("gx", "gy"), 0, 0) for value in ends[-CHUNKS:]]
    brought = [lax.ppermute(value, "sec", [(0, 3)]) for value in tiles]
    return to_output(flag, planes, brought + tiles)


highest = lax.Precision.HIGHEST


def from_root(shard, axis, root):
    mine = lax.axis_index(axis) == root
    return lax.psum(jnp.where(mine, shard, jnp.zeros_like(shard)), axis)


def padded_2(block, sides, width):
    for axis, dim in sides:
        count = lax.axis_size(axis)
        forward = [(i, i + 1) for i in range(count - 1)]
        backward = [(target, source) for source, target in forward]
        low = lax.ppermute(
            lax.slice_in_dim(block, block.shape[dim] - width, None, axis=dim), axis, forward
        )
        high = lax.ppermute(lax.slice_in_dim(block, 0, width, axis=dim), axis, backward)
        block = jnp.concatenate([low, block, high], axis=dim)
    return block


def shifted(value, axis, steps):
    count = lax.axis_size(axis)
    initial, last = (max(0, -steps), min(count, count - steps))
    return lax.ppermute(value, axis, [(source, source + steps) for source in range(initial, last)])


def flow_core(padded):
    centre = padded[:, 1:-1, 1:-1, :]
    ahead_x = padded[:, 2:, 1:-1, :]
    behind_x = padded[:, :-2, 1:-1, :]
    ahead_y = padded[:, 1:-1, 2:, :]
    behind_y = padded[:, 1:-1, :-2, :]
    ahead_z = jnp.roll(centre, -1, axis=3)
    behind_z = jnp.roll(centre, 1, axis=3)
    slope_x = 0.5 * (ahead_x - behind_x)
    slope_y = 0.5 * (ahead_y - behind_y)
    slope_z = 0.5 * (ahead_z - behind_z)
    laplace = ahead_x + behind_x + ahead_y + behind_y + ahead_z + behind_z - 6.0 * centre
    omega_x = slope_y[2] - slope_z[1]
    omega_y = slope_z[0] - slope_x[2]
    omega_z = slope_x[1] - slope_y[0]
    lamb_vector = jnp.stack(
        [
            omega_y * centre[2] - omega_z * centre[1],
            omega_z * centre[0] - omega_x * centre[2],
            omega_x * centre[1] - omega_y * centre[0],
        ]
    )
    updated = centre + time_step * (viscosity * laplace - lamb_vector)
    return (updated, lamb_vector)


def skip_flow(padded):
    centre = padded[:, 1:-1, 1:-1, :]
    return (centre, jnp.zeros_like(centre))


def unchanged(accrued):
    return accrued


def place_source(padded_lamb, offset_x, offset_y, matrix, span_x, span_y, extent_x, extent_y):
    anchor = jnp.zeros((), jnp.int32)
    corner_x = span_x - offset_x - 1
    corner_y = span_y - offset_y - 1
    window = lax.dynamic_slice(
        padded_lamb,
        (anchor, corner_x, corner_y, anchor),
        (3, extent_x + 1, extent_y + 1, padded_lamb.shape[3]),
    )
    averaged = 0.25 * (
        window[:, :-1, :-1] + window[:, 1:, :-1] + window[:, :-1, 1:] + window[:, 1:, 1:]
    )
    return jnp.einsum("kj,jxyz->kxyz", matrix, averaged, precision=highest)


def sweep_lines_x(state, x_ops, select_x, active):
    initial = jnp.zeros(state.shape[1:], jnp.float32)

    def add_piece(running, portion, anchor):

        def work(accrued):
            partial_value = jnp.einsum("ckij,kjl->ckil", x_ops, portion[0], precision=highest)
            return jnp.sum(partial_value * select_x[:, None, None, :], axis=0)

        return lax.cond(active, work, unchanged, running)

    return add_piece(initial, lax.all_gather(state, "gx", axis=2, tiled=True), jnp.int32(0))


def sweep_lines_y(state, y_ops, select_y, active):
    initial = jnp.zeros(state.shape[1:], jnp.float32)

    def add_piece(running, portion, anchor):

        def work(accrued):
            partial_value = jnp.einsum("ckij,kxjz->ckxiz", y_ops, portion[0], precision=highest)
            return jnp.sum(partial_value * select_y[:, None, :, None, None], axis=0)

        return lax.cond(active, work, unchanged, running)

    return add_piece(initial, lax.all_gather(state, "gy", axis=3, tiled=True), jnp.int32(0))


def local_general(fields, x_ops, y_ops, x_line_class, y_line_class, box_offset, coupling):
    sections = lax.axis_size("sec")
    section_index = lax.axis_index("sec")
    active = section_index == sections - 1
    member = jnp.minimum(section_index, sections - 2)
    span_x = fields.shape[2]
    merged = fields.shape[3]
    span_y = merged // CZ
    classes = jnp.arange(NCLASS, dtype=jnp.int32)
    select_y = (classes[:, None] == y_line_class[None, :]).astype(jnp.float32)
    offsets = lax.dynamic_index_in_dim(box_offset, member, 0, keepdims=False)
    matrix = lax.dynamic_index_in_dim(coupling, member, 0, keepdims=False)
    current = fields[0].reshape(3, span_x, span_y, CZ)
    share = CZ // sections
    whole_start = from_root(current, "sec", sections - 1)
    acoustic = lax.dynamic_slice_in_dim(whole_start, section_index * share, share, 3)
    for repeat in range(STEPS):
        padded = padded_2(current, (("gx", 1), ("gy", 2)), 1)
        flowed, lamb_vector = lax.cond(active, skip_flow, flow_core, padded)
        left_tile = shifted(lamb_vector, "gx", 1)
        joined = jnp.concatenate([left_tile, lamb_vector], axis=1)
        lower_tile = shifted(joined, "gy", 1)
        joined = jnp.concatenate([lower_tile, joined], axis=2)
        contribution = place_source(
            joined, offsets[0], offsets[1], matrix, span_x, span_y, span_x, span_y
        )
        source = lax.psum_scatter(contribution, "sec", scatter_dimension=3, tiled=True)
        amplitudes_grid = acoustic + time_step * source
        busy = jnp.asarray(True)
        planes = amplitudes_grid.shape[3]
        merged_now = span_y * planes
        select_x = jnp.broadcast_to(
            (classes[:, None, None] == x_line_class[None, :, None]).astype(jnp.float32),
            (NCLASS, span_y, planes),
        ).reshape(NCLASS, merged_now)
        amplitudes = amplitudes_grid.reshape(1, 3, span_x, merged_now)
        swept_x = sweep_lines_x(amplitudes, x_ops, select_x, busy)
        acoustic = sweep_lines_y(
            swept_x.reshape(1, 3, span_x, span_y, planes), y_ops, select_y, busy
        )
        current = flowed
    whole_end = lax.all_gather(acoustic, "sec", axis=3, tiled=True)
    current = jnp.where(active, whole_end, current)
    return current.reshape(1, 3, span_x, merged)


def whole_planes_fit(mesh):
    sizes = dict(mesh.shape)
    return sizes["sec"] == 4 and sizes["gx"] == 2 and sizes["gy"] == 4


def solution(mesh):
    placed = (
        P("sec", None, "gx", "gy"),
        P(None, None, "gx", None),
        P(None, None, "gy", None),
        P("gy"),
        P("gx"),
        P(),
        P(),
    )
    return jax.shard_map(
        local if whole_planes_fit(mesh) else local_general,
        mesh=mesh,
        in_specs=placed,
        out_specs=P("sec", None, "gx", "gy"),
        check_vma=False,
    )
```

```python
import jax
import jax.numpy as jnp
from jax import lax
from jax.experimental import pallas as pl
from jax.experimental.pallas import tpu as pltpu
from jax.sharding import PartitionSpec as P

CZ = 32
NCLASS = 4
STEPS = 2
TILE_X = 128
TILE_Y = 64
CHUNKS = 2

time_step = 0.2
viscosity = 0.25
vmem_limit = 56 * 1024 * 1024
f32 = jnp.float32
bf16 = jnp.bfloat16


def params():
    return pltpu.CompilerParams(vmem_limit_bytes=vmem_limit)


def iota(shape, dim):
    return lax.broadcasted_iota(jnp.int32, shape, dim)


def edges_kernel(left_ref, right_ref, down_ref, up_ref, west_ref, east_ref, south_ref, north_ref, rows, spread):
    comp = pl.program_id(0)
    count = TILE_X // CZ
    tiles = TILE_Y // count
    lane = iota((TILE_Y, TILE_X), 1)
    mine = lane // CZ == comp
    for ref, which, out_ref in ((left_ref, 0, west_ref), (right_ref, 7, east_ref)):
        for t in range(tiles):
            rows[t : t + 1, :] = ref[0, which : which + 1, t * TILE_X : (t + 1) * TILE_X]
        for r in range(count):
            turned = pltpu.roll(rows[...], lax.rem((comp - r + count) * CZ, TILE_X), 1)
            spread[pl.ds(r, tiles, stride=count), :] = turned

        @pl.when(comp == 0)
        def _():
            out_ref[...] = jnp.zeros_like(out_ref)

        out_ref[...] = jnp.where(mine, spread[...], out_ref[...])
    south_ref[0] = down_ref[0].T[0:CZ]
    north_ref[0] = up_ref[0].T[TILE_X - CZ :]


def tile_edges(field):
    merged = field.shape[2]
    edge = pl.BlockSpec((TILE_Y, TILE_X), lambda c: (0, 0))
    side = pl.BlockSpec((1, CZ, TILE_X), lambda c: (c, 0, 0))
    return pl.pallas_call(
        edges_kernel,
        grid=(3,),
        in_specs=[
            pl.BlockSpec((1, 8, merged), lambda c: (c, 0, 0)),
            pl.BlockSpec((1, 8, merged), lambda c: (c, TILE_X // 8 - 1, 0)),
            pl.BlockSpec((1, TILE_X, 128), lambda c: (c, 0, 0)),
            pl.BlockSpec((1, TILE_X, 128), lambda c: (c, 0, merged // 128 - 1)),
        ],
        out_specs=[edge, edge, side, side],
        out_shape=[jax.ShapeDtypeStruct((TILE_Y, TILE_X), f32)] * 2
        + [jax.ShapeDtypeStruct((3, CZ, TILE_X), f32)] * 2,
        scratch_shapes=[
            pltpu.VMEM((merged // TILE_X, TILE_X), f32),
            pltpu.VMEM((TILE_Y, TILE_X), f32),
        ],
        compiler_params=params(),
        name="tile_edges",
    )(field, field, field, field)


def planes_kernel(field_ref, planes_ref, turned):
    turned[...] = field_ref[0].T
    for z in range(CZ):
        planes_ref[z, 0] = turned[pl.ds(z, TILE_Y, stride=CZ), :]


def to_planes(field, waits):
    count = len(waits)

    def body(field_ref, *refs):
        planes_kernel(field_ref, *refs[count:])

    return pl.pallas_call(
        body,
        grid=(3,),
        in_specs=[pl.BlockSpec((1, TILE_X, TILE_Y * CZ), lambda c: (c, 0, 0))]
        + [pl.BlockSpec(memory_space=pl.ANY)] * count,
        out_specs=pl.BlockSpec((CZ, 1, TILE_Y, TILE_X), lambda c: (0, c, 0, 0)),
        out_shape=jax.ShapeDtypeStruct((CZ, 3, TILE_Y, TILE_X), f32),
        scratch_shapes=[pltpu.VMEM((TILE_Y * CZ, TILE_X), f32)],
        compiler_params=params(),
        name="to_planes",
    )(field, *waits)


def flow_kernel(per, want, flag_ref, u_ref, xlo_ref, xhi_ref, ylo_ref, yhi_ref, *outs):
    outs = list(outs)
    lamb_ref = outs.pop(0) if "lamb" in want else None
    next_ref = outs.pop(0) if "next" in want else None
    group = pl.program_id(0)
    acoustic = flag_ref[0] > 0
    lane = iota((TILE_Y, TILE_X), 1)
    row = iota((TILE_Y, TILE_X), 0)
    turn = lax.rem(TILE_X - group * per, TILE_X)
    xlo = pltpu.roll(xlo_ref[...], turn, 1)
    xhi = pltpu.roll(xhi_ref[...], turn, 1)
    if "edges" in want:
        west_ref, east_ref, south_ref, north_ref = outs

        @pl.when(group == 0)
        def _():
            west_ref[...] = jnp.zeros_like(west_ref)
            east_ref[...] = jnp.zeros_like(east_ref)

        west = west_ref[...]
        east = east_ref[...]
    for i in range(per):
        z = group * per + i
        above = lax.rem(z + 1, CZ)
        below = lax.rem(z + CZ - 1, CZ)
        centre, lap, dx, dy, dz = [], [], [], [], []
        for c in range(3):
            mid = u_ref[z, c]
            up = u_ref[above, c]
            down = u_ref[below, c]
            spot = c * CZ + i
            xm = jnp.where(lane == 0, xlo[:, spot : spot + 1], pltpu.roll(mid, 1, 1))
            xp = jnp.where(
                lane == TILE_X - 1, xhi[:, spot : spot + 1], pltpu.roll(mid, TILE_X - 1, 1)
            )
            ym = jnp.where(row == 0, ylo_ref[c, pl.ds(z, 1), :], pltpu.roll(mid, 1, 0))
            yp = jnp.where(
                row == TILE_Y - 1, yhi_ref[c, pl.ds(z, 1), :], pltpu.roll(mid, TILE_Y - 1, 0)
            )
            centre.append(mid)
            lap.append(xp + xm + yp + ym + up + down - 6.0 * mid)
            dx.append(0.5 * (xp - xm))
            dy.append(0.5 * (yp - ym))
            dz.append(0.5 * (up - down))
        ox = dy[2] - dz[1]
        oy = dz[0] - dx[2]
        oz = dx[1] - dy[0]
        lamb = (
            oy * centre[2] - oz * centre[1],
            oz * centre[0] - ox * centre[2],
            ox * centre[1] - oy * centre[0],
        )
        for c in range(3):
            if "lamb" in want:
                sent = jnp.where(acoustic, centre[c], lamb[c]) if "passed" in want else lamb[c]
                lamb_ref[0, i // CHUNKS, i % CHUNKS, c] = sent
            if "next" in want:
                moved = centre[c] + time_step * (viscosity * lap[c] - lamb[c])
                next_ref[i, c] = moved
            if "edges" in want:
                here = lane == c * CZ + z
                west = jnp.where(here, moved[:, 0:1], west)
                east = jnp.where(here, moved[:, TILE_X - 1 :], east)
                south_ref[c, pl.ds(z, 1), :] = moved[0:1, :]
                north_ref[c, pl.ds(z, 1), :] = moved[TILE_Y - 1 :, :]
    if "edges" in want:
        west_ref[...] = west
        east_ref[...] = east


def flow(flag, planes, halo, waits, groups, want):
    per = CZ // groups
    halves = per // CHUNKS
    edge = pl.BlockSpec((TILE_Y, TILE_X), lambda g: (0, 0))
    side = pl.BlockSpec((3, CZ, TILE_X), lambda g: (0, 0, 0))
    out_specs, out_shape = [], []
    if "lamb" in want:
        out_specs.append(
            pl.BlockSpec((1, halves, CHUNKS, 3, TILE_Y, TILE_X), lambda g: (g, 0, 0, 0, 0, 0))
        )
        out_shape.append(
            jax.ShapeDtypeStruct((groups, halves, CHUNKS, 3, TILE_Y, TILE_X), f32)
        )
    if "next" in want:
        out_specs.append(pl.BlockSpec((per, 3, TILE_Y, TILE_X), lambda g: (g, 0, 0, 0)))
        out_shape.append(jax.ShapeDtypeStruct((CZ, 3, TILE_Y, TILE_X), f32))
    if "edges" in want:
        out_specs += [edge, edge, side, side]
        out_shape += [jax.ShapeDtypeStruct((TILE_Y, TILE_X), f32)] * 2
        out_shape += [jax.ShapeDtypeStruct((3, CZ, TILE_X), f32)] * 2
    count = len(waits)

    def body(*refs):
        flow_kernel(per, want, *refs[:6], *refs[6 + count :])

    return pl.pallas_call(
        body,
        grid=(groups,),
        in_specs=[
            pl.BlockSpec(memory_space=pltpu.SMEM),
            pl.BlockSpec((CZ, 3, TILE_Y, TILE_X), lambda g: (0, 0, 0, 0)),
            edge,
            edge,
            side,
            side,
        ]
        + [pl.BlockSpec(memory_space=pl.ANY)] * count,
        out_specs=out_specs,
        out_shape=out_shape,
        compiler_params=params(),
        name="flow",
    )(flag, planes, *halo, *waits)


def exchange(west, east, south, north):
    def send(value, axis, step):
        count = lax.axis_size(axis)
        return lax.ppermute(
            value, axis, [(i, i + step) for i in range(count) if 0 <= i + step < count]
        )

    return (
        send(east, "gx", 1),
        send(west, "gx", -1),
        send(north, "gy", 1),
        send(south, "gy", -1),
    )


def place_kernel(gx, gy, first, ints_ref, matrix_ref, got_ref, far_ref, near_ref, rows):
    low = ints_ref[1]
    ox = ints_ref[2]
    oy = ints_ref[3]
    full_y = gy * TILE_Y
    lane = iota((full_y, TILE_X), 1)
    row = iota((full_y, TILE_X), 0)

    def tile(h, j, a):
        return jnp.concatenate([got_ref[a * gy + b, h, 0, j] for b in range(gy)], axis=0)

    def work(h, out_ref):
        for a in range(gx):
            rows[0:TILE_Y, a * TILE_X : (a + 1) * TILE_X] = jnp.zeros((TILE_Y, TILE_X), f32)
        vectors = [[tile(h, j, a) for a in range(gx)] for j in range(3)]
        for k in range(3):
            mixed = [
                matrix_ref[k, 0] * vectors[0][a]
                + matrix_ref[k, 1] * vectors[1][a]
                + matrix_ref[k, 2] * vectors[2][a]
                for a in range(gx)
            ]
            before = jnp.zeros((full_y, TILE_X), f32)
            moved = []
            for a in range(gx):
                turned = pltpu.roll(mixed[a], ox, 1)
                moved.append(jnp.where(lane >= ox, turned, before))
                before = turned
            before = jnp.zeros((full_y, TILE_X), f32)
            for a in range(gx):
                turned = pltpu.roll(moved[a], 1, 1)
                pair = moved[a] + jnp.where(lane >= 1, turned, before)
                before = turned
                pair = pair + jnp.where(row >= 1, pltpu.roll(pair, 1, 0), 0.0)
                rows[TILE_Y : TILE_Y + full_y, a * TILE_X : (a + 1) * TILE_X] = pair
            start = TILE_Y - oy
            rest = lax.rem(start, 8)
            window = rows[pl.ds(pl.multiple_of(start - rest, 8), full_y + 8), :]
            window = window.reshape(full_y // 8 + 1, 8, gx * TILE_X)
            window = pltpu.roll(window, lax.rem(8 - rest, 8), 1)
            within = iota((full_y // 8, 8, gx * TILE_X), 1) < 8 - rest
            out_ref[k] = jnp.where(within, window[:-1], window[1:]).reshape(full_y, gx * TILE_X)

    def copy(h, out_ref):
        for k in range(3):
            for a in range(gx):
                out_ref[k, :, a * TILE_X : (a + 1) * TILE_X] = tile(h, k, a)

    if first:

        @pl.when(ints_ref[0] == 0)
        def _():
            work(low, far_ref)
            work(1 - low, near_ref)

        @pl.when(ints_ref[0] > 0)
        def _():
            copy(low, far_ref)
            copy(1 - low, near_ref)
    else:
        work(low, far_ref)
        work(1 - low, near_ref)


def place(ints, matrix, got, chunk, waits, gx, gy, first):
    shape = (3, gy * TILE_Y, gx * TILE_X)
    count = len(waits)

    def body(*refs):
        place_kernel(gx, gy, first, *refs[:3], *refs[3 + count :])

    block = got.shape[:2] + (1,) + got.shape[3:]
    return pl.pallas_call(
        body,
        grid=(1,),
        in_specs=[
            pl.BlockSpec(memory_space=pltpu.SMEM),
            pl.BlockSpec(memory_space=pltpu.SMEM),
            pl.BlockSpec(block, lambda i: (0, 0, chunk, 0, 0, 0)),
        ]
        + [pl.BlockSpec(memory_space=pl.ANY)] * count,
        out_specs=[pl.BlockSpec(shape, lambda i: (0, 0, 0))] * 2,
        out_shape=[jax.ShapeDtypeStruct(shape, f32)] * 2,
        scratch_shapes=[pltpu.VMEM((TILE_Y * (gy + 1) + 8, gx * TILE_X), f32)],
        compiler_params=params(),
        name="place",
    )(ints, matrix, got, *waits)


def tie_kernel(*refs):
    pass


def after(value, earlier):
    anywhere = pl.BlockSpec(memory_space=pl.ANY)
    if not earlier:
        return value
    return pl.pallas_call(
        tie_kernel,
        in_specs=[anywhere] * (1 + len(earlier)),
        out_specs=anywhere,
        out_shape=jax.ShapeDtypeStruct(value.shape, value.dtype),
        input_output_aliases={0: 0},
        name="after",
    )(value, *earlier)


def split(value):
    high = value.astype(bf16)
    return high, (value - high.astype(f32)).astype(bf16)


def dot(a, b):
    return lax.dot_general(a, b, (((1,), (0,)), ((), ())), preferred_element_type=f32)


def x_ops_kernel(pos_ref, mine_ref, first_ref, second_ref, high_ref, low_ref):
    place_x = pos_ref[0]
    core = pos_ref[1]
    rows = mine_ref.shape[2]

    def put(cls, block, where):
        high, low = split(block.T)
        spot = pl.ds(pl.multiple_of(where * rows, rows), rows)
        high_ref[cls, 0, :, spot] = high
        low_ref[cls, 0, :, spot] = low

    for cls in range(NCLASS):
        put(cls, mine_ref[cls, 0], place_x)
    half = NCLASS // 2
    for cls in range(half):
        put(core * half + cls, first_ref[cls, 0], 1 - place_x)
        put((1 - core) * half + cls, second_ref[cls, 0], 1 - place_x)


def y_ops_kernel(pos_ref, b0_ref, b1_ref, b2_ref, b3_ref, high_ref, low_ref):
    me = pos_ref[2]
    rows = b0_ref.shape[2]
    for step, ref in enumerate((b0_ref, b1_ref, b2_ref, b3_ref)):
        spot = pl.ds(pl.multiple_of((me ^ step) * rows, rows), rows)
        for cls in range(NCLASS):
            high, low = split(ref[cls, 0])
            high_ref[cls, 0, spot, :] = high
            low_ref[cls, 0, spot, :] = low


def ops_kernel(pos_ref, *refs):
    x_ops_kernel(pos_ref, *refs[:3], *refs[7:9])
    y_ops_kernel(pos_ref, *refs[3:7], *refs[9:])


def prepare_ops(pos, x_blocks, y_blocks):
    def spec(block):
        return pl.BlockSpec((block.shape[0], 1) + block.shape[2:], lambda k: (0, k, 0, 0))

    blocks = (*x_blocks, *y_blocks)
    out = [
        jax.ShapeDtypeStruct((NCLASS, 3, length, length), bf16)
        for length in (x_blocks[0].shape[3], y_blocks[0].shape[3])
        for _ in range(2)
    ]
    parts = pl.pallas_call(
        ops_kernel,
        grid=(3,),
        in_specs=[pl.BlockSpec(memory_space=pltpu.SMEM)] + [spec(b) for b in blocks],
        out_specs=[spec(o) for o in out],
        out_shape=out,
        compiler_params=params(),
        name="operators",
    )(pos, *blocks)
    return parts[:2], parts[2:]


def fetched_ops(x_ops, y_ops, earlier):
    core = lax.rem(lax.axis_index("gy"), 2)
    half = NCLASS // 2
    piece = lax.dynamic_slice_in_dim(x_ops, core * half, half, 0)
    sent = [after(piece, earlier), after(y_ops, earlier)]
    got_x = lax.ppermute(sent[0], "gx", [(0, 1), (1, 0)])
    got_y = lax.ppermute(sent[1], "gy", [(i, i ^ 2) for i in range(4)])
    return [got_x, got_y], sent


def paired_ops(y_ops, got_x, got_y):
    beside = [(i, i ^ 1) for i in range(4)]
    return [lax.ppermute(value, "gy", beside) for value in (got_x, y_ops, got_y)]


def prepared_ops(x_ops, y_ops, fetched, paired):
    got_x, got_y = fetched
    pair_x, pair_y, cross_y = paired
    place_y = lax.axis_index("gy")
    pos = jnp.stack([lax.axis_index("gx"), lax.rem(place_y, 2), place_y]).astype(jnp.int32)
    return prepare_ops(pos, (x_ops, got_x, pair_x), (y_ops, pair_y, got_y, cross_y))


def gathered_classes(x_line_class, y_line_class):
    def rows(value, axis):
        count = lax.axis_size(axis)
        blocks = [value] + [
            lax.ppermute(value, axis, [(i, i ^ step) for i in range(count)])
            for step in range(1, count)
        ]
        order = jnp.arange(count) ^ lax.axis_index(axis)
        return jnp.take(jnp.stack(blocks), order, axis=0)

    return rows(x_line_class, "gy").reshape(-1, 1), rows(y_line_class, "gx").reshape(1, -1)


def sweep_kernel(gx, gy, count, last, xclass_ref, yclass_ref, xh_ref, xl_ref, yh_ref, yl_ref, *refs):
    ins = refs[:count]
    out_ref = refs[count]
    xclass = xclass_ref[...]
    yclass = yclass_ref[...]
    state = ins[0][0]
    for extra in ins[1:]:
        state = state + extra[0]
    high, low = split(state)
    swept = jnp.zeros(state.shape, f32)
    for cls in range(NCLASS):
        part = dot(high, xh_ref[cls, 0]) + dot(low, xh_ref[cls, 0]) + dot(high, xl_ref[cls, 0])
        swept = jnp.where(xclass == cls, part, swept)
    high, low = split(swept)
    final = jnp.zeros(state.shape, f32)
    for cls in range(NCLASS):
        part = dot(yh_ref[cls, 0], high) + dot(yh_ref[cls, 0], low) + dot(yl_ref[cls, 0], high)
        final = jnp.where(yclass == cls, part, final)
    if last:
        for a in range(gx):
            for b in range(gy):
                out_ref[a * gy + b, 0] = final[
                    b * TILE_Y : (b + 1) * TILE_Y, a * TILE_X : (a + 1) * TILE_X
                ]
    else:
        out_ref[0] = final


def sweep(classes, x_parts, y_parts, terms, gx, gy, last):
    full_y, full_x = gy * TILE_Y, gx * TILE_X
    count = len(terms)
    field = pl.BlockSpec((1, full_y, full_x), lambda k: (k, 0, 0))
    xop = pl.BlockSpec((NCLASS, 1, full_x, full_x), lambda k: (0, k, 0, 0))
    yop = pl.BlockSpec((NCLASS, 1, full_y, full_y), lambda k: (0, k, 0, 0))
    if last:
        out_specs = pl.BlockSpec((gx * gy, 1, TILE_Y, TILE_X), lambda k: (0, k, 0, 0))
        out_shape = jax.ShapeDtypeStruct((gx * gy, 3, TILE_Y, TILE_X), f32)
    else:
        out_specs = field
        out_shape = jax.ShapeDtypeStruct((3, full_y, full_x), f32)

    def body(*refs):
        sweep_kernel(gx, gy, count, last, *refs)

    return pl.pallas_call(
        body,
        grid=(3,),
        in_specs=[
            pl.BlockSpec((full_y, 1), lambda k: (0, 0)),
            pl.BlockSpec((1, full_x), lambda k: (0, 0)),
            xop,
            xop,
            yop,
            yop,
        ]
        + [field] * count,
        out_specs=out_specs,
        out_shape=out_shape,
        compiler_params=params(),
        name="sweep",
    )(*classes, *x_parts, *y_parts, *terms)


def output_kernel(flag_ref, u_ref, *refs):
    parts = refs[: 2 * CHUNKS]
    out_ref, turned = refs[2 * CHUNKS :]
    per = CZ // parts[0].shape[0]

    @pl.when(flag_ref[0] == 0)
    def _():
        for z in range(CZ):
            turned[pl.ds(z, TILE_Y // 2, stride=CZ), :] = u_ref[z, 0]

    @pl.when(flag_ref[0] > 0)
    def _():
        for z in range(CZ):
            g, i = divmod(z, per)
            turned[pl.ds(z, TILE_Y // 2, stride=CZ), :] = parts[i][g, 0]

    out_ref[0, 0] = turned[...].T


def to_output(flag, planes, parts):
    part = pl.BlockSpec(parts[0].shape[:1] + (1, TILE_Y // 2, TILE_X), lambda c, h: (0, c, h, 0))
    return pl.pallas_call(
        output_kernel,
        grid=(3, 2),
        in_specs=[
            pl.BlockSpec(memory_space=pltpu.SMEM),
            pl.BlockSpec((CZ, 1, TILE_Y // 2, TILE_X), lambda c, h: (0, c, h, 0)),
        ]
        + [part] * (2 * CHUNKS),
        out_specs=pl.BlockSpec((1, 1, TILE_X, TILE_Y // 2 * CZ), lambda c, h: (0, c, 0, h)),
        out_shape=jax.ShapeDtypeStruct((1, 3, TILE_X, TILE_Y * CZ), f32),
        scratch_shapes=[pltpu.VMEM((TILE_Y // 2 * CZ, TILE_X), f32)],
        compiler_params=params(),
        name="to_output",
    )(flag, planes, *parts)


def local(fields, x_ops, y_ops, x_line_class, y_line_class, box_offset, coupling):
    gx, gy = lax.axis_size("gx"), lax.axis_size("gy")
    groups = gx * gy
    sec = lax.axis_index("sec")
    active = (sec == 3).astype(jnp.int32)
    member = jnp.minimum(sec, 2)
    offsets = lax.dynamic_index_in_dim(box_offset, member, 0, keepdims=False)
    matrix = lax.dynamic_index_in_dim(coupling, member, 0, keepdims=False) * (0.25 * time_step)
    matrix = jnp.where(active > 0, jnp.zeros_like(matrix), matrix)
    flag = active.reshape(1)
    lower = (sec < 2).astype(jnp.int32)
    ints = jnp.stack([active, lower, offsets[0], offsets[1]])

    edges = tile_edges(fields[0])
    planes = to_planes(fields[0], [edges[0]])
    halo = [after(value, [planes]) for value in exchange(*edges)]

    (lamb,) = flow(flag, planes, halo, (), groups, ("lamb", "passed"))
    gots = [lax.all_to_all(lamb, ("gx", "gy"), 0, 0)]
    waits = (lamb, ints, matrix)
    planes, *edges = flow(flag, planes, halo, waits, groups, ("next", "edges"))
    halo = exchange(*edges)
    lamb, planes = flow(flag, planes, halo, (), groups, ("lamb", "next"))
    gots[0] = after(gots[0], [lamb])
    gots.append(lax.all_to_all(after(lamb, [gots[0]]), ("gx", "gy"), 0, 0))
    fetched, taken = fetched_ops(x_ops, y_ops, [planes])

    total = STEPS * CHUNKS
    fars, nears, firsts, seconds, thirds, ends = ([None] * total for _ in range(6))
    lines = gathered_classes(x_line_class, y_line_class)
    beside, parts = [], []
    token = list(lines)

    def placed(n):
        first = n < CHUNKS
        got = gots[n // CHUNKS]
        waits = token + taken if n == CHUNKS else token
        fars[n], nears[n] = place(ints, matrix, got, n % CHUNKS, waits, gx, gy, first)
        firsts[n] = lax.ppermute(fars[n], "sec", [(0, 1), (3, 2)] if first else [(0, 1)])
        return [fars[n]]

    def paired(n):
        fetched[:] = [after(value, token) for value in fetched]
        beside.extend(paired_ops(y_ops, *fetched))
        return token

    def prepared(n):
        brought = [after(value, token) for value in beside]
        parts.extend(prepared_ops(x_ops, y_ops, fetched, brought))
        return [*parts[0], *parts[1]]

    def first_hop(n):
        value = fars[n] + after(firsts[n], token)
        seconds[n] = lax.ppermute(value, "sec", [(1, 2), (2, 1)])
        return [value]

    def second_hop(n):
        value = nears[n] + after(seconds[n], token)
        thirds[n] = lax.ppermute(value, "sec", [(1, 0), (2, 3)])
        return [value]

    def arrived(n):
        thirds[n] = after(thirds[n], token)
        return [thirds[n]]

    def swept(n):
        terms = (nears[n], after(thirds[n], token))
        if n >= CHUNKS:
            terms += (ends[n - CHUNKS],)
        ends[n] = sweep(lines, *parts, terms, gx, gy, n >= total - CHUNKS)
        return [ends[n]]

    order = (
        (placed, 0), (placed, 1), (first_hop, 0), (placed, 2), (first_hop, 1), (second_hop, 0),
        (placed, 3), (first_hop, 2), (second_hop, 1), (arrived, 0), (paired, 0), (first_hop, 3),
        (second_hop, 2), (arrived, 1), (prepared, 0), (swept, 0), (second_hop, 3),
        (swept, 2), (swept, 1), (swept, 3),
    )
    for work, n in order:
        token = work(n)
    tiles = [lax.all_to_all(value, ("gx", "gy"), 0, 0) for value in ends[-CHUNKS:]]
    brought = [lax.ppermute(value, "sec", [(0, 3)]) for value in tiles]
    return to_output(flag, planes, brought + tiles)


highest = lax.Precision.HIGHEST


def from_root(shard, axis, root):
    mine = lax.axis_index(axis) == root
    return lax.psum(jnp.where(mine, shard, jnp.zeros_like(shard)), axis)


def padded_2(block, sides, width):
    for axis, dim in sides:
        count = lax.axis_size(axis)
        forward = [(i, i + 1) for i in range(count - 1)]
        backward = [(target, source) for source, target in forward]
        low = lax.ppermute(
            lax.slice_in_dim(block, block.shape[dim] - width, None, axis=dim), axis, forward
        )
        high = lax.ppermute(lax.slice_in_dim(block, 0, width, axis=dim), axis, backward)
        block = jnp.concatenate([low, block, high], axis=dim)
    return block


def shifted(value, axis, steps):
    count = lax.axis_size(axis)
    initial, last = (max(0, -steps), min(count, count - steps))
    return lax.ppermute(value, axis, [(source, source + steps) for source in range(initial, last)])


def flow_core(padded):
    centre = padded[:, 1:-1, 1:-1, :]
    ahead_x = padded[:, 2:, 1:-1, :]
    behind_x = padded[:, :-2, 1:-1, :]
    ahead_y = padded[:, 1:-1, 2:, :]
    behind_y = padded[:, 1:-1, :-2, :]
    ahead_z = jnp.roll(centre, -1, axis=3)
    behind_z = jnp.roll(centre, 1, axis=3)
    slope_x = 0.5 * (ahead_x - behind_x)
    slope_y = 0.5 * (ahead_y - behind_y)
    slope_z = 0.5 * (ahead_z - behind_z)
    laplace = ahead_x + behind_x + ahead_y + behind_y + ahead_z + behind_z - 6.0 * centre
    omega_x = slope_y[2] - slope_z[1]
    omega_y = slope_z[0] - slope_x[2]
    omega_z = slope_x[1] - slope_y[0]
    lamb_vector = jnp.stack(
        [
            omega_y * centre[2] - omega_z * centre[1],
            omega_z * centre[0] - omega_x * centre[2],
            omega_x * centre[1] - omega_y * centre[0],
        ]
    )
    updated = centre + time_step * (viscosity * laplace - lamb_vector)
    return (updated, lamb_vector)


def skip_flow(padded):
    centre = padded[:, 1:-1, 1:-1, :]
    return (centre, jnp.zeros_like(centre))


def unchanged(accrued):
    return accrued


def place_source(padded_lamb, offset_x, offset_y, matrix, span_x, span_y, extent_x, extent_y):
    anchor = jnp.zeros((), jnp.int32)
    corner_x = span_x - offset_x - 1
    corner_y = span_y - offset_y - 1
    window = lax.dynamic_slice(
        padded_lamb,
        (anchor, corner_x, corner_y, anchor),
        (3, extent_x + 1, extent_y + 1, padded_lamb.shape[3]),
    )
    averaged = 0.25 * (
        window[:, :-1, :-1] + window[:, 1:, :-1] + window[:, :-1, 1:] + window[:, 1:, 1:]
    )
    return jnp.einsum("kj,jxyz->kxyz", matrix, averaged, precision=highest)


def sweep_lines_x(state, x_ops, select_x, active):
    initial = jnp.zeros(state.shape[1:], jnp.float32)

    def add_piece(running, portion, anchor):

        def work(accrued):
            partial_value = jnp.einsum("ckij,kjl->ckil", x_ops, portion[0], precision=highest)
            return jnp.sum(partial_value * select_x[:, None, None, :], axis=0)

        return lax.cond(active, work, unchanged, running)

    return add_piece(initial, lax.all_gather(state, "gx", axis=2, tiled=True), jnp.int32(0))


def sweep_lines_y(state, y_ops, select_y, active):
    initial = jnp.zeros(state.shape[1:], jnp.float32)

    def add_piece(running, portion, anchor):

        def work(accrued):
            partial_value = jnp.einsum("ckij,kxjz->ckxiz", y_ops, portion[0], precision=highest)
            return jnp.sum(partial_value * select_y[:, None, :, None, None], axis=0)

        return lax.cond(active, work, unchanged, running)

    return add_piece(initial, lax.all_gather(state, "gy", axis=3, tiled=True), jnp.int32(0))


def local_general(fields, x_ops, y_ops, x_line_class, y_line_class, box_offset, coupling):
    sections = lax.axis_size("sec")
    section_index = lax.axis_index("sec")
    active = section_index == sections - 1
    member = jnp.minimum(section_index, sections - 2)
    span_x = fields.shape[2]
    merged = fields.shape[3]
    span_y = merged // CZ
    classes = jnp.arange(NCLASS, dtype=jnp.int32)
    select_y = (classes[:, None] == y_line_class[None, :]).astype(jnp.float32)
    offsets = lax.dynamic_index_in_dim(box_offset, member, 0, keepdims=False)
    matrix = lax.dynamic_index_in_dim(coupling, member, 0, keepdims=False)
    current = fields[0].reshape(3, span_x, span_y, CZ)
    share = CZ // sections
    whole_start = from_root(current, "sec", sections - 1)
    acoustic = lax.dynamic_slice_in_dim(whole_start, section_index * share, share, 3)
    for repeat in range(STEPS):
        padded = padded_2(current, (("gx", 1), ("gy", 2)), 1)
        flowed, lamb_vector = lax.cond(active, skip_flow, flow_core, padded)
        left_tile = shifted(lamb_vector, "gx", 1)
        joined = jnp.concatenate([left_tile, lamb_vector], axis=1)
        lower_tile = shifted(joined, "gy", 1)
        joined = jnp.concatenate([lower_tile, joined], axis=2)
        contribution = place_source(
            joined, offsets[0], offsets[1], matrix, span_x, span_y, span_x, span_y
        )
        source = lax.psum_scatter(contribution, "sec", scatter_dimension=3, tiled=True)
        amplitudes_grid = acoustic + time_step * source
        busy = jnp.asarray(True)
        planes = amplitudes_grid.shape[3]
        merged_now = span_y * planes
        select_x = jnp.broadcast_to(
            (classes[:, None, None] == x_line_class[None, :, None]).astype(jnp.float32),
            (NCLASS, span_y, planes),
        ).reshape(NCLASS, merged_now)
        amplitudes = amplitudes_grid.reshape(1, 3, span_x, merged_now)
        swept_x = sweep_lines_x(amplitudes, x_ops, select_x, busy)
        acoustic = sweep_lines_y(
            swept_x.reshape(1, 3, span_x, span_y, planes), y_ops, select_y, busy
        )
        current = flowed
    whole_end = lax.all_gather(acoustic, "sec", axis=3, tiled=True)
    current = jnp.where(active, whole_end, current)
    return current.reshape(1, 3, span_x, merged)


def whole_planes_fit(mesh):
    sizes = dict(mesh.shape)
    return sizes["sec"] == 4 and sizes["gx"] == 2 and sizes["gy"] == 4


def solution(mesh):
    placed = (
        P("sec", None, "gx", "gy"),
        P(None, None, "gx", None),
        P(None, None, "gy", None),
        P("gy"),
        P("gx"),
        P(),
        P(),
    )
    return jax.shard_map(
        local if whole_planes_fit(mesh) else local_general,
        mesh=mesh,
        in_specs=placed,
        out_specs=P("sec", None, "gx", "gy"),
        check_vma=False,
    )
```
